32 devices in a mesh: frame: 4 (over x, core), patch: 8 (over z, y).
Axes of the slice: x: 2, y: 2, z: 4, core: 2. Of those that a mesh axis runs over, the one named last changes fastest.
Arguments:
- tokens: bfloat16 [16, 256, 1152], P(None, ('frame', 'patch')), may hold values from -6 to 6
- image_mask: int32 [16, 256], P(None, ('frame', 'patch')), may hold values from 0 to 1, as said below
- sample_index: int32 [16, 256], P(None, ('frame', 'patch')), may hold values from 0 to 31, as said below
- condition: bfloat16 [32, 1152], replicated, may hold values from -6 to 6
- ada_weight: bfloat16 [1152, 6912], P('patch'), may hold values from -0.1875 to 0.1875
- ada_bias: bfloat16 [6912], replicated, may hold values from -1.75 to 1.75
- qkv_weight: bfloat16 [1152, 3456], P('patch'), may hold values from -0.1875 to 0.1875
- qkv_bias: bfloat16 [2304], replicated, may hold values from -1.75 to 1.75
- proj_weight: bfloat16 [1152, 1152], P('patch'), may hold values from -0.375 to 0.375
- proj_bias: bfloat16 [1152], replicated, may hold values from -1.75 to 1.75
- fc1_weight: bfloat16 [1152, 4608], P('patch'), may hold values from -0.1875 to 0.1875
- fc1_bias: bfloat16 [4608], replicated, may hold values from -1.75 to 1.75
- fc2_weight: bfloat16 [4608, 1152], P('patch'), may hold values from -0.09375 to 0.09375
- fc2_bias: bfloat16 [1152], replicated, may hold values from -1.75 to 1.75
- cotangent: bfloat16 [16, 256, 1152], P(None, ('frame', 'patch')), may hold values from -6 to 6
Outputs:
- output: bfloat16 [16, 256, 1152], P(None, ('frame', 'patch'))
- input_grad: float32 [16, 256, 1152], P(None, ('frame', 'patch'))
- condition_grad: float32 [32, 1152], P(None, 'patch')
- ada_weight_grad: float32 [1152, 6912], P('patch')
- ada_bias_grad: float32 [6912], replicated
- qkv_weight_grad: float32 [1152, 3456], P('patch', 'frame')
- qkv_bias_grad: float32 [2304], replicated
- proj_weight_grad: float32 [1152, 1152], P('patch', 'frame')
- proj_bias_grad: float32 [1152], replicated
- fc1_weight_grad: float32 [1152, 4608], P('patch', 'frame')
- fc1_bias_grad: float32 [4608], replicated
- fc2_weight_grad: float32 [4608, 1152], P('patch', 'frame')
- fc2_bias_grad: float32 [1152], replicated
The draws below stay inside these ranges and needn't reach their ends.
Inputs may be any that keep to these rules, and one draw needn't show every extreme that they name: `image_mask`: all 16 tokens of a patch column share the mask; at least one column is an image column. `sample_index`: all tokens of a clip column carry one index below 16; in an image column the token at frame slot f carries 16 + f.
All inputs are finite; a program needn't handle non-finite values.
Results may differ from the reference program's by a relative error of at most 0.018.
Values may be sent and summed in bfloat16 or wider, within the bound.
No kernel may reach another device: no remote copies, remote signals or barrier semaphores. Data moves between devices by JAX's collectives and lax.ppermute only.
A program may use at most 192 MiB of HBM per device.

```python
import jax
import jax.numpy as jnp
from jax import lax

HEADS = 16
HEAD_DIM = 72
FF = 4608
FRAMES = 16
CLIPS = 16
D = 1152
COLS = 256
SAMPLES = 32
N_PATCH = 8


def column_kind(key):
    image_roll = jax.random.randint(jax.random.fold_in(key, 11), (COLS,), 0, CLIPS + 1)
    chosen = jax.random.randint(jax.random.fold_in(key, 12), (), 0, COLS)
    image_column = (image_roll == CLIPS) | (jnp.arange(COLS, dtype=jnp.int32) == chosen)
    clip_number = jax.random.randint(jax.random.fold_in(key, 13), (COLS,), 0, CLIPS)
    return (image_column, clip_number)


def draw_image_mask(key, part):
    image_column, clip_number = column_kind(key)
    return jnp.broadcast_to(image_column[None, :], (FRAMES, COLS)).astype(jnp.int32)


def draw_sample_index(key, part):
    image_column, clip_number = column_kind(key)
    slot_number = jnp.arange(FRAMES, dtype=jnp.int32)[:, None]
    return jnp.where(image_column[None, :], CLIPS + slot_number, clip_number[None, :]).astype(jnp.int32)


def levels(key, dims, cuts, least, top_value):
    def one(dim, blocks):
        steps = jax.random.uniform(jax.random.fold_in(jax.random.fold_in(key, 6), dim), (blocks,), jnp.float32, least / len(cuts), top_value / len(cuts))
        return jnp.repeat(jnp.exp(steps), dims[dim] // blocks).reshape((-1,) + (1,) * (len(dims) - dim - 1))

    gain = one(*cuts[0])
    for cut in cuts[1:]:
        gain = gain * one(*cut)
    return gain


def normal_values(stream_key, shape, deviation, limit, shards=(), held_as=jnp.bfloat16):
    array = jax.random.normal(stream_key, shape, jnp.float32) * deviation
    if len(shards) > 0:
        array = levels(stream_key, shape, shards, -0.22, 0.18) * array
    return jnp.clip(array, min=-limit, max=limit).astype(held_as)


def setup_inputs(seed: int = 0) -> dict:
    seeds = jax.random.split(jax.random.key(seed), 16)
    return {
        "tokens": normal_values(seeds[0], (FRAMES, COLS, D), 1.0, 6.0, ((1, 32),)),
        "image_mask": draw_image_mask(jax.random.fold_in(seeds[15], 71), 0),
        "sample_index": draw_sample_index(jax.random.fold_in(seeds[15], 71), 0),
        "condition": normal_values(seeds[3], (SAMPLES, D), 1.0, 6.0),
        "ada_weight": normal_values(seeds[4], (D, 6 * D), D ** -0.5, 0.1875, ((0, 8),)),
        "ada_bias": normal_values(seeds[5], (6 * D,), 0.3, 1.75),
        "qkv_weight": normal_values(seeds[6], (D, 3 * D), D ** -0.5, 0.1875, ((0, 8),)),
        "qkv_bias": normal_values(seeds[7], (2 * D,), 0.3, 1.75),
        "proj_weight": normal_values(seeds[8], (D, D), (D // 4) ** -0.5, 0.375, ((0, 8),)),
        "proj_bias": normal_values(seeds[9], (D,), 0.3, 1.75),
        "fc1_weight": normal_values(seeds[10], (D, FF), D ** -0.5, 0.1875, ((0, 8),)),
        "fc1_bias": normal_values(seeds[11], (FF,), 0.3, 1.75),
        "fc2_weight": normal_values(seeds[12], (FF, D), FF ** -0.5, 0.09375, ((0, 8),)),
        "fc2_bias": normal_values(seeds[13], (D,), 0.3, 1.75),
        "cotangent": normal_values(seeds[14], (FRAMES, COLS, D), 1.0, 6.0, ((1, 32),)),
    }


HIGHEST = lax.Precision.HIGHEST
EPSILON = 1e-06

@jax.custom_vjp
def low(v):
    return lax.optimization_barrier(v.astype(jnp.bfloat16)).astype(jnp.float32)

@jax.custom_vjp
def low_back(v):
    return v

def low_keep(v):
    return (low(v), None)

def low_pass(kept, grad):
    return (grad,)

def back_keep(v):
    return (v, None)

def back_low(kept, grad):
    return (low(grad),)
low.defvjp(low_keep, low_pass)
low_back.defvjp(back_keep, back_low)

def matmul(left_side, right_side):
    return jnp.dot(left_side, right_side, precision=HIGHEST, preferred_element_type=jnp.float32)

def normalize(values):
    centred = values - lax.optimization_barrier(jnp.mean(values, axis=-1, keepdims=True))
    return centred * lax.rsqrt(lax.optimization_barrier(jnp.mean(centred * centred, axis=-1, keepdims=True)) + EPSILON)

def split_heads(values):
    return values.reshape(values.shape[0], values.shape[1], HEADS, HEAD_DIM)

def layer_block(layer_weights, modulation, pieces):
    qkv_weight, qkv_bias, proj_weight, proj_bias, fc1_weight, fc1_bias, fc2_weight, fc2_bias = layer_weights
    block_in, block_mask, block_index = pieces
    model_width = block_in.shape[-1]
    per_token = jnp.take(modulation, block_index, axis=0)
    shift_one, scale_one, gate_one, shift_two, scale_two, gate_two = jnp.split(per_token, 6, axis=-1)
    attn_in = low(normalize(block_in) * (1.0 + scale_one) + shift_one)
    projected = matmul(attn_in, qkv_weight)
    queries = low(low_back(projected[..., :model_width] + qkv_bias[:model_width]))
    key_rows = low(low_back(projected[..., model_width:2 * model_width]))
    value_rows = low(low_back(projected[..., 2 * model_width:] + qkv_bias[model_width:]))
    score_grid = jnp.einsum('achd,bchd->chab', split_heads(queries), split_heads(key_rows), precision=HIGHEST) * HEAD_DIM ** (-0.5)
    shifted = score_grid - lax.optimization_barrier(jnp.max(score_grid, axis=-1, keepdims=True))
    expanded = jnp.exp(shifted)
    attention_prob = expanded / lax.optimization_barrier(jnp.sum(expanded, axis=-1, keepdims=True))
    mixed = jnp.einsum('chab,bchd->achd', attention_prob, split_heads(value_rows), precision=HIGHEST)
    attn_out = low(low_back(mixed.reshape(block_in.shape)))
    after_one = block_in + gate_one * low_back(matmul(attn_out, proj_weight) + proj_bias)
    mlp_in = low(normalize(after_one) * (1.0 + scale_two) + shift_two)
    hidden_pre = low_back(matmul(mlp_in, fc1_weight) + fc1_bias)
    hidden = low(jax.nn.gelu(hidden_pre, approximate=True))
    after_two = after_one + gate_two * low_back(matmul(hidden, fc2_weight) + fc2_bias)
    return jnp.where(block_mask[..., None] == 1, block_in, after_two)

def reference(tokens, image_mask, sample_index, condition, ada_weight, ada_bias, qkv_weight, qkv_bias, proj_weight, proj_bias, fc1_weight, fc1_bias, fc2_weight, fc2_bias, cotangent):
    block_cols = COLS // N_PATCH
    mask_blocks = image_mask.reshape(FRAMES, N_PATCH, block_cols).transpose(1, 0, 2)
    index_blocks = sample_index.reshape(FRAMES, N_PATCH, block_cols).transpose(1, 0, 2).astype(jnp.int32)

    def forward(token_values, cond_values, ada_w, ada_b, *layer_weights):
        modulation = matmul(low(jax.nn.silu(cond_values)), ada_w) + ada_b
        token_blocks = token_values.reshape(FRAMES, N_PATCH, block_cols, -1).transpose(1, 0, 2, 3)
        checked = jax.checkpoint(layer_block)

        def advance(running, pieces):
            return (running, checked(layer_weights, modulation, pieces))
        _, outputs = lax.scan(advance, None, (token_blocks, mask_blocks, index_blocks))
        return outputs.transpose(1, 0, 2, 3).reshape(FRAMES, COLS, -1)
    primals = tuple((argument.astype(jnp.float32) for argument in (tokens, condition, ada_weight, ada_bias, qkv_weight, qkv_bias, proj_weight, proj_bias, fc1_weight, fc1_bias, fc2_weight, fc2_bias)))
    output, pullback = jax.vjp(forward, *primals)
    grads = pullback(cotangent.astype(jnp.float32))
    return (output.astype(jnp.bfloat16), grads[0], grads[1], grads[2], grads[3], grads[4], grads[5], grads[6], grads[7], grads[8], grads[9], grads[10], grads[11])
```

```python
import functools

import jax
import jax.numpy as jnp
from jax import lax
from jax.experimental import pallas as pl
from jax.experimental.pallas import tpu as pltpu
from jax.sharding import Mesh, PartitionSpec as P

HEAD_DIM = 72
EPSILON = 1e-06
SCORE_SCALE = HEAD_DIM**-0.5
GELU_C = 0.7978845608028654
GELU_A = 0.044715
VMEM_BYTES = 56 * 1024 * 1024
BF = jnp.bfloat16
F32 = jnp.float32


def mm(a, b, ca=1, cb=0):
    return lax.dot_general(a, b, (((ca,), (cb,)), ((), ())), preferred_element_type=F32)


def normalize(values):
    centred = values - jnp.mean(values, axis=-1, keepdims=True)
    inverse = lax.rsqrt(jnp.mean(centred * centred, axis=-1, keepdims=True) + EPSILON)
    return centred * inverse, inverse


def normalize_back(grad_normed, normed, inverse):
    return inverse * (
        grad_normed
        - jnp.mean(grad_normed, axis=-1, keepdims=True)
        - normed * jnp.mean(grad_normed * normed, axis=-1, keepdims=True)
    )


def stack_rows(pieces):
    if pieces[0].shape[0] % 16 == 0:
        return jnp.concatenate(pieces, axis=0)
    return jnp.concatenate([piece.astype(F32) for piece in pieces], axis=0).astype(pieces[0].dtype)


def softmax_prob(queries, key_rows, same_column):
    grid = mm(queries, key_rows, 1, 1) * SCORE_SCALE
    grid = jnp.where(same_column, grid, -1e30)
    expanded = jnp.exp(grid - jnp.max(grid, axis=-1, keepdims=True))
    return expanded / jnp.sum(expanded, axis=-1, keepdims=True)


def column_mask(tokens_per_part, columns):
    rows = lax.broadcasted_iota(jnp.int32, (tokens_per_part, tokens_per_part), 0)
    cols = lax.broadcasted_iota(jnp.int32, (tokens_per_part, tokens_per_part), 1)
    return lax.rem(rows, columns) == lax.rem(cols, columns)


def attend_kernel(d, width, columns, tok_ref, sel_ref, mod_ref, w_ref, bias_ref, out_ref, qkv_ref):
    normed, _ = normalize(tok_ref[...].astype(F32))
    sel = sel_ref[...]
    shift = mm(sel, mod_ref[:, 0:d])
    scale = mm(sel, mod_ref[:, d : 2 * d])
    attn_in = (normed * (1.0 + scale) + shift).astype(BF)
    qkv = (mm(attn_in, w_ref[...]) + bias_ref[...]).astype(BF)
    qkv_ref[...] = qkv
    size = tok_ref.shape[0] // 2
    same = column_mask(size, columns)
    for half in range(2):
        rows = slice(half * size, (half + 1) * size)
        parts = []
        for head in range(width // HEAD_DIM):
            q, k, v = (
                qkv[rows, t * width + head * HEAD_DIM : t * width + (head + 1) * HEAD_DIM]
                for t in range(3)
            )
            prob = softmax_prob(q, k, same)
            parts.append(mm(prob.astype(BF), v).T)
        out_ref[:, rows] = jnp.concatenate(parts, axis=0).astype(BF)


def slab_attention(refs, order, size):
    pieces = []
    for ref, swapped in zip(refs, order):
        piece = ref[...]
        if swapped:
            piece = jnp.concatenate([piece[:, size:], piece[:, :size]], axis=1)
        pieces.append(piece)
    return stack_rows(pieces)


def mlp_kernel(d, order, *refs):
    n = len(order)
    slots = refs[:n]
    (tok_ref, cot_ref, sel_ref, selt_ref, mod_ref, proj_ref, projb_ref, fc1_ref, fc1b_ref, fc2_ref, fc2b_ref) = refs[n : n + 11]
    (b2_ref, gm_ref, fc1g_ref, fc2g_ref, fc1bg_ref, fc2bg_ref, modg_ref, after_ref, branch_ref, fc1a, fc2a) = refs[n + 11 :]
    step = pl.program_id(0)
    size = tok_ref.shape[0] // 2
    sel = sel_ref[...]
    selt = selt_ref[...]

    def mod(block):
        return mm(sel, mod_ref[:, block * d : (block + 1) * d])

    attn_t = slab_attention(slots, order, size)
    branch_one = mm(attn_t, proj_ref[...], 0, 0) + projb_ref[...]
    after_one = tok_ref[...].astype(F32) + mod(2) * branch_one

    @pl.when(step == 0)
    def _():
        after_ref[...] = after_one[:size]
        branch_ref[...] = branch_one[:size]
        fc1a[...] = jnp.zeros_like(fc1a)
        fc2a[...] = jnp.zeros_like(fc2a)
        fc1bg_ref[...] = jnp.zeros_like(fc1bg_ref)
        fc2bg_ref[...] = jnp.zeros_like(fc2bg_ref)
        modg_ref[...] = jnp.zeros_like(modg_ref)

    normed, _ = normalize(after_one)
    mlp_in = (normed * (1.0 + mod(4)) + mod(3)).astype(BF)
    pre = mm(mlp_in, fc1_ref[...]) + fc1b_ref[...]
    square = pre * pre
    tanh = jnp.tanh(GELU_C * pre * (1.0 + GELU_A * square))
    hidden = (0.5 * pre * (1.0 + tanh)).astype(BF)
    slope = 0.5 * (1.0 + tanh) + 0.5 * pre * (1.0 - tanh * tanh) * GELU_C * (1.0 + 3.0 * GELU_A * square)
    branch_two = mm(hidden, fc2_ref[...]) + fc2b_ref[...]
    b2_ref[...] = branch_two.astype(BF).reshape(b2_ref.shape)
    grad_two = cot_ref[...].astype(F32)
    grad_branch = mod(5) * grad_two
    gb2 = grad_branch.astype(BF)
    fc2bg_ref[...] += jnp.sum(gb2.astype(F32), axis=0, keepdims=True)
    fc2a[...] += mm(hidden, gb2, 0, 0)
    grad_pre = (mm(gb2, fc2_ref[...], 1, 1) * slope).astype(BF)
    fc1bg_ref[...] += jnp.sum(grad_pre.astype(F32), axis=0, keepdims=True)
    fc1a[...] += mm(mlp_in, grad_pre, 0, 0)
    grad_in = mm(grad_pre, fc1_ref[...], 1, 1)
    gm_ref[...] = grad_in.astype(BF).reshape(gm_ref.shape)
    modg_ref[0] += mm(selt, grad_in.astype(BF))
    modg_ref[1] += mm(selt, (grad_in * normed).astype(BF))
    modg_ref[2] += mm(selt, (grad_two * branch_two).astype(BF))

    @pl.when(step == pl.num_programs(0) - 1)
    def _():
        fc1g_ref[...] = fc1a[...].astype(BF)
        fc2g_ref[...] = fc2a[...].astype(BF)


def middle_kernel(d, n_parts, count, place_ref, *refs):
    grads = refs[:count]
    (after_ref, branch_ref, cot_ref, sel_ref, selt_ref, mod_ref, proj_ref) = refs[count : count + 7]
    (ex_ref, one_ref, modg_ref, pbias_ref) = refs[count + 7 :]
    sel = sel_ref[...]
    grad_in = grads[0][...].astype(F32)
    for ref in grads[1:]:
        grad_in = grad_in + ref[...].astype(F32)
    normed, inverse = normalize(after_ref[...])
    scale = mm(sel, mod_ref[:, 4 * d : 5 * d])
    gate = mm(sel, mod_ref[:, 2 * d : 3 * d])
    grad_one = cot_ref[...].astype(F32) + normalize_back(grad_in * (1.0 + scale), normed, inverse)
    one_ref[...] = grad_one
    modg_ref[...] = mm(selt_ref[...], (grad_one * branch_ref[...]).astype(BF))
    gb1 = (gate * grad_one).astype(BF)
    gb1_wide = gb1.astype(F32)
    pbias_ref[...] = jnp.sum(gb1_wide, axis=0, keepdims=True)
    width = d // n_parts
    grad_attn = mm(proj_ref[...], gb1, 1, 1)
    gb1_t = gb1_wide.T
    for part in range(n_parts):
        rows = slice(part * width, (part + 1) * width)
        ex_ref[part, 0] = grad_attn[rows].astype(BF)
        ex_ref[place_ref[part], 1] = gb1_t[rows].astype(BF)


def attend_back_kernel(d, width, columns, order, place_ref, *refs):
    n = len(order)
    slots = refs[:n]
    (ga_ref, tok_ref, sel_ref, selt_ref, mod_ref, w_ref, qkv_ref) = refs[n : n + 7]
    (gin_ref, qkvg_ref, projg_ref, bias_ref, modg_ref, qkva, proja) = refs[n + 7 :]
    step = pl.program_id(0)
    size = tok_ref.shape[0] // 2

    @pl.when(step == 0)
    def _():
        qkva[...] = jnp.zeros_like(qkva)
        proja[...] = jnp.zeros_like(proja)
        bias_ref[...] = jnp.zeros_like(bias_ref)
        modg_ref[...] = jnp.zeros_like(modg_ref)

    qkv = qkv_ref[...]
    same = column_mask(size, columns)
    heads = width // HEAD_DIM
    halves = []
    for half in range(2):
        rows = slice(half * size, (half + 1) * size)
        grad_mixed = ga_ref[half, 0].astype(F32).T
        pieces = [None] * (3 * heads)
        for head in range(heads):
            q, k, v = (
                qkv[rows, t * width + head * HEAD_DIM : t * width + (head + 1) * HEAD_DIM]
                for t in range(3)
            )
            grad = grad_mixed[:, head * HEAD_DIM : (head + 1) * HEAD_DIM].astype(BF)
            prob = softmax_prob(q, k, same)
            grad_prob = mm(grad, v, 1, 1)
            delta = jnp.sum(prob * grad_prob, axis=-1, keepdims=True)
            grad_score = (prob * (grad_prob - delta) * SCORE_SCALE).astype(BF)
            pieces[head] = mm(grad_score, k)
            pieces[heads + head] = mm(grad_score, q, 0, 0)
            pieces[2 * heads + head] = mm(prob.astype(BF), grad, 0, 0)
        halves.append(jnp.concatenate(pieces, axis=1))
    grad_qkv = jnp.concatenate(halves, axis=0).astype(BF)
    bias_ref[...] += jnp.sum(grad_qkv.astype(F32), axis=0, keepdims=True)

    sel = sel_ref[...]
    selt = selt_ref[...]
    normed, _ = normalize(tok_ref[...].astype(F32))
    shift = mm(sel, mod_ref[:, 0:d])
    scale = mm(sel, mod_ref[:, d : 2 * d])
    attn_in = (normed * (1.0 + scale) + shift).astype(BF)
    qkva[...] += mm(attn_in, grad_qkv, 0, 0)
    grad_in = mm(grad_qkv, w_ref[...], 1, 1)
    gin_ref[...] = grad_in.astype(BF).reshape(gin_ref.shape)
    modg_ref[0] += mm(selt, grad_in.astype(BF))
    modg_ref[1] += mm(selt, (grad_in * normed).astype(BF))

    attn_t = slab_attention(slots, order, size)
    gb1_t = jnp.concatenate([ga_ref[0, 1], ga_ref[1, 1]], axis=1)
    proja[...] += mm(attn_t, gb1_t, 1, 1)

    @pl.when(step == pl.num_programs(0) - 1)
    def _():
        qkvg_ref[...] = qkva[...].astype(BF)
        rows = d // n
        for part in range(n):
            projg_ref[place_ref[part]] = proja[part * rows : (part + 1) * rows].astype(BF)


def last_kernel(d, count, count_b, *refs):
    grads = refs[:count]
    branches = refs[count : count + count_b]
    (tok_ref, one_ref, after_ref, cot_ref, mask_ref, sel_ref, mod_ref) = refs[count + count_b : count + count_b + 7]
    (out_ref, grad_ref) = refs[count + count_b + 7 :]
    sel = sel_ref[...]
    masked = mask_ref[...] == 1
    tokens = tok_ref[...].astype(F32)
    grad_in = grads[0][...].astype(F32)
    for ref in grads[1:]:
        grad_in = grad_in + ref[...].astype(F32)
    normed, inverse = normalize(tokens)
    scale = mm(sel, mod_ref[:, d : 2 * d])
    back = normalize_back(grad_in * (1.0 + scale), normed, inverse)
    grad_ref[...] = jnp.where(masked, cot_ref[...].astype(F32), 0.0) + one_ref[...] + back
    branch = branches[0][...].astype(F32)
    for ref in branches[1:]:
        branch = branch + ref[...].astype(F32)
    gate = mm(sel, mod_ref[:, 5 * d : 6 * d])
    out_ref[...] = jnp.where(masked, tokens, after_ref[...] + gate * branch).astype(BF)


def params(steps=1):
    return pltpu.CompilerParams(vmem_limit_bytes=VMEM_BYTES, dimension_semantics=("arbitrary",) * steps)


def cost(flops, bytes_accessed):
    return pl.CostEstimate(flops=int(flops), bytes_accessed=int(bytes_accessed), transcendentals=0)


def whole(shape):
    return pl.BlockSpec(shape, lambda *_: (0,) * len(shape))


def matchings(frames):
    left = {f: {t: (frames * t + f) // 3 for t in range(3)} for f in range(frames)}
    rounds = []
    for _ in range(3):
        taken = {}

        def place(f, seen):
            for t, to in left[f].items():
                if to in seen:
                    continue
                seen.add(to)
                if to not in taken or place(taken[to][0], seen):
                    taken[to] = (f, t)
                    return True
            return False

        for f in range(frames):
            place(f, set())
        chosen = {f: (t, to) for to, (f, t) in taken.items()}
        for f, (t, _to) in chosen.items():
            del left[f][t]
        rounds.append(chosen)
    return rounds


def solution(mesh):
    F, N = mesh.shape["frame"], mesh.shape["patch"]
    C, Y = 2, 2
    X, Z = F // C, N // Y
    G = X * C * Y
    half_slots = X * Y
    grid = Mesh(mesh.devices.reshape(X, C, Z, Y), ("x", "core", "z", "y"))
    everywhere = ("x", "core", "z", "y")
    offsets = [(dc, dx, dy) for dc in range(C) for dx in range(X) for dy in range(Y)]

    def from_xy(a, dx, dy):
        if dx == 0 and dy == 0:
            return a
        pairs = [
            (x * Y + y, ((x - dx) % X) * Y + (y - dy) % Y) for x in range(X) for y in range(Y)
        ]
        return lax.ppermute(a, ("x", "y"), pairs)

    def to_xy(a, dx, dy):
        return from_xy(a, (-dx) % X, (-dy) % Y)

    def swap_core(a):
        return lax.ppermute(a, "core", [(0, 1), (1, 0)])

    def swap_y(a):
        return lax.ppermute(a, "y", [(0, 1), (1, 0)])

    def gather_slots(a):
        mine = [from_xy(a, dx, dy) for dx in range(X) for dy in range(Y)]
        return mine + [swap_core(piece) for piece in mine]

    def scatter_sum(slots):
        received = swap_core(slots[half_slots:])
        terms = []
        for slot in range(half_slots):
            total = slots[slot].astype(F32) + received[slot].astype(F32)
            terms.append(to_xy(total.astype(BF), slot // Y, slot % Y))
        return terms

    def exchange(slots):
        received = swap_core(slots[half_slots:])
        pieces = [None] * G
        for slot in range(half_slots):
            dx, dy = slot // Y, slot % Y
            pair = to_xy(jnp.stack([slots[slot], received[slot]]), dx, dy)
            source = ((-dx) % X) * Y + (-dy) % Y
            pieces[source] = pair[0]
            pieces[half_slots + source] = pair[1]
        return jnp.stack(pieces)

    def local(tokens, image_mask, sample_index, condition, ada_weight, ada_bias, qkv_weight, qkv_bias,
              proj_weight, proj_bias, fc1_weight, fc1_bias, fc2_weight, fc2_bias, cotangent):
        frames, columns, d = tokens.shape
        T = frames * columns
        S = G * T
        samples = condition.shape[0]
        rows_here = ada_weight.shape[0]
        ff = fc1_weight.shape[1]
        width = d // G
        unit = ff // (N * F)
        part_ff = Z * unit
        x_i, c_i = lax.axis_index("x"), lax.axis_index("core")
        z_i, y_i = lax.axis_index("z"), lax.axis_index("y")
        f_i = x_i * C + c_i
        p_i = z_i * Y + y_i
        g_i = f_i * Y + y_i
        parts_at = [
            (((x_i + dx) % X) * C + (c_i + dc) % C) * Y + (y_i + dy) % Y for dc, dx, dy in offsets
        ]
        parts_at = jnp.stack(parts_at).astype(jnp.int32)
        all_parts = jnp.arange(G, dtype=jnp.int32)
        part_x, part_c, part_y = all_parts // (C * Y), (all_parts // Y) % C, all_parts % Y
        place = ((part_c - c_i) % C) * half_slots + ((part_x - x_i) % X) * Y + (part_y - y_i) % Y
        place = place.astype(jnp.int32)

        def y_pair(own, other):
            got = swap_y(other)
            return jnp.where(y_i == 0, jnp.stack([own, got]), jnp.stack([got, own]))

        pair_width = Y * width
        qkv_cols = [
            lax.dynamic_slice_in_dim(qkv_weight, t * d + f_i * pair_width, pair_width, 1) for t in range(3)
        ]

        def qkv_for(which):
            return jnp.concatenate(
                [lax.dynamic_slice_in_dim(c, which * width, width, 1) for c in qkv_cols], axis=1
            )

        qkv_rows = y_pair(qkv_for(y_i), qkv_for(1 - y_i)).reshape(Y * rows_here, 3 * width)
        w_qkv = lax.all_gather(qkv_rows, "z", axis=0, tiled=True)
        half_rows = rows_here // C
        proj_half = lax.dynamic_slice_in_dim(proj_weight, c_i * half_rows, half_rows, 0)
        proj_rows = y_pair(proj_half, proj_half).reshape(Y * half_rows, d)
        proj_mine = lax.all_gather(proj_rows, "z", axis=0, tiled=True)
        proj_other = swap_core(proj_mine)
        proj_both = jnp.where(
            c_i == 0, jnp.stack([proj_mine, proj_other]), jnp.stack([proj_other, proj_mine])
        )
        proj_parts = (
            proj_both.reshape(C, N, half_rows, d).transpose(1, 0, 2, 3).reshape(G, width, d)
        )
        proj_rel = jnp.concatenate(
            [lax.dynamic_index_in_dim(proj_parts, parts_at[r], 0, keepdims=False) for r in range(G)],
            axis=0,
        )

        def fc1_for(which):
            return jnp.concatenate(
                [
                    lax.dynamic_slice_in_dim(
                        fc1_weight, (z * Y + which) * (F * unit) + f_i * unit, unit, 1
                    )
                    for z in range(Z)
                ],
                axis=1,
            )

        fc1_rows = y_pair(fc1_for(y_i), fc1_for(1 - y_i)).reshape(Y * rows_here, part_ff)
        w_fc1 = lax.all_gather(fc1_rows, "z", axis=0, tiled=True)
        fc2_rows = lax.dynamic_slice_in_dim(fc2_weight, f_i * unit, unit, 0)
        w_fc2 = lax.all_gather(fc2_rows, "z", axis=0, tiled=True)

        chunk = samples * 6 * d // (F * N)
        per_row = 6 * d // chunk
        frame_samples = samples // F
        first_row = p_i * rows_here
        cond_rows = lax.dynamic_slice_in_dim(condition, first_row, rows_here, 1).astype(F32)
        sigmoid = 1.0 / (1.0 + jnp.exp(-cond_rows))
        act_rows = (cond_rows * sigmoid).astype(BF)
        silu_slope = sigmoid * (1.0 + cond_rows * (1.0 - sigmoid))
        act_mine = lax.dynamic_slice_in_dim(act_rows, f_i * frame_samples, frame_samples, 0)
        partial_mod = mm(act_mine, ada_weight).reshape(N, chunk)
        mod_terms = lax.all_to_all(partial_mod, ("z", "y"), 0, 0, tiled=True)
        bias_here = lax.dynamic_slice_in_dim(ada_bias, (p_i % per_row) * chunk, chunk, 0)
        mod_chunk = (jnp.sum(mod_terms, axis=0) + bias_here.astype(F32)).astype(BF)
        mod = lax.all_to_all(
            jnp.broadcast_to(mod_chunk, (F * N, chunk)), everywhere, 0, 0, tiled=True
        ).reshape(samples, 6 * d)

        flat_tokens = tokens.reshape(T, d)
        flat_cot = cotangent.reshape(T, d)
        mask = image_mask.reshape(T, 1)
        grad_two_own = jnp.where(mask == 1, jnp.zeros_like(flat_cot), flat_cot)
        codes = jnp.zeros((16, d), BF).at[0, :T].set(sample_index.reshape(T).astype(BF))
        token_slots = gather_slots(jnp.concatenate([flat_tokens, codes], axis=0))
        slab_tokens = jnp.concatenate([piece[:T] for piece in token_slots], axis=0)
        slab_codes = jnp.stack([piece[T, :T] for piece in token_slots]).astype(jnp.int32)
        slab_cot = jnp.concatenate(gather_slots(grad_two_own), axis=0)
        numbers = jnp.arange(samples, dtype=jnp.int32)
        selt = (slab_codes.reshape(1, S) == numbers[:, None]).astype(BF)
        sel = (slab_codes.reshape(S, 1) == numbers[None, :]).astype(BF)
        sel_own, selt_own = sel[:T], selt[:, :T]

        steps = G // 2
        TB = 2 * T
        row_block = lambda w: pl.BlockSpec((TB, w), lambda j: (j, 0))
        lane_block = lambda h: pl.BlockSpec((h, TB), lambda j: (0, j))

        bias_q = lax.dynamic_slice_in_dim(qkv_bias, g_i * width, width, 0)
        bias_v = lax.dynamic_slice_in_dim(qkv_bias, d + g_i * width, width, 0)
        bias_qkv = jnp.concatenate([bias_q, jnp.zeros_like(bias_q), bias_v]).astype(F32)[None]
        attn_t, qkv = pl.pallas_call(
            functools.partial(attend_kernel, d, width, columns),
            grid=(steps,),
            in_specs=[
                row_block(d),
                row_block(samples),
                whole((samples, 6 * d)),
                whole((d, 3 * width)),
                whole((1, 3 * width)),
            ],
            out_specs=[lane_block(width), row_block(3 * width)],
            out_shape=[
                jax.ShapeDtypeStruct((width, S), BF),
                jax.ShapeDtypeStruct((S, 3 * width), BF),
            ],
            compiler_params=params(),
            cost_estimate=cost(2 * S * d * 3 * width * 2, 8e6),
            name="attend",
        )(slab_tokens, sel, mod, w_qkv, bias_qkv)

        attn_slots = gather_slots(attn_t)
        order = [dy == 1 for _, _, dy in offsets]

        def slot_spec(dc, dx):
            return pl.BlockSpec(
                (width, TB),
                lambda j: (0, ((j // X + C - dc) % C) * X + (j % X + X - dx) % X),
            )

        slot_specs = [slot_spec(dc, dx) for dc, dx, _ in offsets]

        hidden_at = lambda v: jnp.concatenate(
            [
                lax.dynamic_slice_in_dim(v, (z * Y + y_i) * (F * unit) + f_i * unit, unit, 0)
                for z in range(Z)
            ]
        )
        fc1_bias_part = hidden_at(fc1_bias).astype(F32)[None]
        fc2_bias_once = jnp.where(g_i == 0, fc2_bias.astype(F32), 0.0)[None]
        slot_out = pl.BlockSpec((2, T, d), lambda j: (j, 0, 0))
        (b2_slots, gm_slots, fc1g, fc2g, fc1_bias_g, fc2_bias_g, modg_two, after_own, branch_own) = pl.pallas_call(
            functools.partial(mlp_kernel, d, order),
            grid=(steps,),
            in_specs=slot_specs
            + [
                row_block(d),
                row_block(d),
                row_block(samples),
                lane_block(samples),
                whole((samples, 6 * d)),
                whole((d, d)),
                whole((1, d)),
                whole((d, part_ff)),
                whole((1, part_ff)),
                whole((part_ff, d)),
                whole((1, d)),
            ],
            out_specs=[
                slot_out,
                slot_out,
                whole((d, part_ff)),
                whole((part_ff, d)),
                whole((1, part_ff)),
                whole((1, d)),
                whole((3, samples, d)),
                whole((T, d)),
                whole((T, d)),
            ],
            out_shape=[
                jax.ShapeDtypeStruct((G, T, d), BF),
                jax.ShapeDtypeStruct((G, T, d), BF),
                jax.ShapeDtypeStruct((d, part_ff), BF),
                jax.ShapeDtypeStruct((part_ff, d), BF),
                jax.ShapeDtypeStruct((1, part_ff), F32),
                jax.ShapeDtypeStruct((1, d), F32),
                jax.ShapeDtypeStruct((3, samples, d), F32),
                jax.ShapeDtypeStruct((T, d), F32),
                jax.ShapeDtypeStruct((T, d), F32),
            ],
            scratch_shapes=[pltpu.VMEM((d, part_ff), F32), pltpu.VMEM((part_ff, d), F32)],
            compiler_params=params(),
            cost_estimate=cost(2 * S * (d * d + 6 * d * part_ff), 3e7),
            name="mlp",
        )(
            *attn_slots,
            slab_tokens,
            slab_cot,
            sel,
            selt,
            mod,
            proj_rel,
            proj_bias.astype(F32)[None],
            w_fc1,
            fc1_bias_part,
            w_fc2,
            fc2_bias_once,
        )

        fc1_z = lax.psum_scatter(fc1g, "z", scatter_dimension=0, tiled=True)
        fc2_z = lax.psum_scatter(fc2g, "z", scatter_dimension=0, tiled=True)
        gm_terms = scatter_sum(gm_slots)

        ex_slots, grad_one, modg_gate, proj_bias_g = pl.pallas_call(
            functools.partial(middle_kernel, d, G, len(gm_terms)),
            grid_spec=pltpu.PrefetchScalarGridSpec(
                num_scalar_prefetch=1,
                grid=(1,),
                in_specs=[whole((T, d))] * len(gm_terms)
                + [
                    whole((T, d)),
                    whole((T, d)),
                    whole((T, d)),
                    whole((T, samples)),
                    whole((samples, T)),
                    whole((samples, 6 * d)),
                    whole((d, d)),
                ],
                out_specs=[
                    whole((G, 2, width, T)),
                    whole((T, d)),
                    whole((samples, d)),
                    whole((1, d)),
                ],
            ),
            out_shape=[
                jax.ShapeDtypeStruct((G, 2, width, T), BF),
                jax.ShapeDtypeStruct((T, d), F32),
                jax.ShapeDtypeStruct((samples, d), F32),
                jax.ShapeDtypeStruct((1, d), F32),
            ],
            compiler_params=params(),
            cost_estimate=cost(4 * T * d * d, 8e6),
            name="middle",
        )(place, *gm_terms, after_own, branch_own, grad_two_own, sel_own, selt_own, mod, proj_rel)

        grad_attn = exchange(ex_slots)
        b2_terms = scatter_sum(b2_slots)

        slot_back = [
            pl.BlockSpec(spec.block_shape, lambda j, place, spec=spec: spec.index_map(j))
            for spec in slot_specs
        ]
        rows_b = lambda w: pl.BlockSpec((TB, w), lambda j, place: (j, 0))
        gin_slots, qkvg, projg, qkv_bias_part, modg_one = pl.pallas_call(
            functools.partial(attend_back_kernel, d, width, columns, order),
            grid_spec=pltpu.PrefetchScalarGridSpec(
                num_scalar_prefetch=1,
                grid=(steps,),
                in_specs=slot_back
                + [
                    pl.BlockSpec((2, 2, width, T), lambda j, place: (j, 0, 0, 0)),
                    rows_b(d),
                    rows_b(samples),
                    pl.BlockSpec((samples, TB), lambda j, place: (0, j)),
                    whole((samples, 6 * d)),
                    whole((d, 3 * width)),
                    rows_b(3 * width),
                ],
                out_specs=[
                    pl.BlockSpec((2, T, d), lambda j, place: (j, 0, 0)),
                    whole((d, 3 * width)),
                    whole((G, width, width)),
                    whole((1, 3 * width)),
                    whole((2, samples, d)),
                ],
                scratch_shapes=[
                    pltpu.VMEM((d, 3 * width), F32),
                    pltpu.VMEM((d, width), F32),
                ],
            ),
            out_shape=[
                jax.ShapeDtypeStruct((G, T, d), BF),
                jax.ShapeDtypeStruct((d, 3 * width), BF),
                jax.ShapeDtypeStruct((G, width, width), BF),
                jax.ShapeDtypeStruct((1, 3 * width), F32),
                jax.ShapeDtypeStruct((2, samples, d), F32),
            ],
            compiler_params=params(),
            cost_estimate=cost(2 * S * d * 8 * width, 1.2e7),
            name="attend_back",
        )(parts_at, *attn_slots, grad_attn, slab_tokens, sel, selt, mod, w_qkv, qkv)

        gin_terms = scatter_sum(gin_slots)

        bias_total = 2 * d + d + ff + d
        biases = jnp.zeros((bias_total,), F32)
        put = lax.dynamic_update_slice_in_dim
        biases = put(biases, qkv_bias_part[0, :width], g_i * width, 0)
        biases = put(biases, qkv_bias_part[0, 2 * width :], d + g_i * width, 0)
        biases = put(biases, proj_bias_g[0], 2 * d, 0)
        for z in range(Z):
            biases = put(
                biases,
                fc1_bias_g[0, z * unit : (z + 1) * unit],
                3 * d + (z * Y + y_i) * (F * unit) + f_i * unit,
                0,
            )
        biases = put(biases, jnp.where(g_i == 0, fc2_bias_g[0], 0.0), 3 * d + ff, 0)
        mod_sums = jnp.concatenate(
            [modg_one[0], modg_one[1], modg_gate, modg_two[0], modg_two[1], modg_two[2]], axis=1
        )
        to_sum = jnp.concatenate(
            [mod_sums.reshape(F * N, chunk), biases.reshape(F * N, bias_total // (F * N))], axis=1
        ).astype(BF)
        terms = lax.all_to_all(to_sum, everywhere, 0, 0, tiled=True)
        summed = jnp.sum(terms.astype(F32), axis=0).astype(BF)
        total = lax.all_to_all(
            jnp.broadcast_to(summed, (F * N, summed.shape[0])), everywhere, 0, 0, tiled=True
        )
        mod_grad = total[:, :chunk].reshape(samples, 6 * d)
        bias_grad = total[:, chunk:].reshape(bias_total).astype(F32)
        ada_bias_grad = jnp.sum(mod_grad.astype(F32), axis=0)
        ada_weight_grad = mm(act_rows, mod_grad, 0, 0)
        condition_grad = mm(mod_grad, ada_weight, 1, 1) * silu_slope

        def y_join(rows):
            kept = lax.dynamic_index_in_dim(rows, y_i, 0, keepdims=False)
            got = swap_y(lax.dynamic_index_in_dim(rows, 1 - y_i, 0, keepdims=False))
            return jnp.where(y_i == 0, jnp.stack([kept, got]), jnp.stack([got, kept]))

        attn_g = jnp.concatenate([qkvg, projg.reshape(d, width)], axis=1)
        attn_z = lax.psum_scatter(attn_g, "z", scatter_dimension=0, tiled=True)
        attn_y = y_join(attn_z.reshape(Y, rows_here, 4 * width))
        blocks = jnp.stack(
            [
                jnp.concatenate([attn_y[y, :, t * width : (t + 1) * width] for y in range(Y)], axis=1)
                for t in range(4)
            ]
        )
        proj_weight_grad = blocks[3].astype(F32)
        moved = [None] * 3
        spots = jnp.zeros((3, F), jnp.int32)
        for turn, chosen in enumerate(matchings(F)):
            picks = jnp.array([chosen[f][0] for f in range(F)], jnp.int32)
            block = lax.dynamic_index_in_dim(blocks, picks[f_i], 0, keepdims=False)
            pairs = [(f, chosen[f][1]) for f in range(F)]
            if any(a != b for a, b in pairs):
                block = lax.ppermute(block, ("x", "core"), pairs)
            moved[turn] = block
            for f in range(F):
                t, to = chosen[f]
                spots = spots.at[(F * t + f) % 3, to].set(turn)
        moved = jnp.stack(moved)
        qkv_weight_grad = jnp.concatenate(
            [
                lax.dynamic_index_in_dim(moved, spots[k, f_i], 0, keepdims=False)
                for k in range(3)
            ],
            axis=1,
        ).astype(F32)

        fc1_y = y_join(fc1_z.reshape(Y, rows_here, part_ff))
        per_frame = Z // F
        fc1_send = fc1_y.reshape(Y, rows_here, F, per_frame, unit).transpose(2, 1, 3, 0, 4)
        fc1_got = lax.all_to_all(fc1_send, ("x", "core"), 0, 0, tiled=True)
        fc1_weight_grad = (
            fc1_got.transpose(1, 2, 3, 0, 4).reshape(rows_here, ff // F).astype(F32)
        )
        fc2_send = fc2_z.reshape(unit, F, d // F).transpose(1, 0, 2)
        fc2_got = lax.all_to_all(fc2_send, ("x", "core"), 0, 0, tiled=True)
        fc2_weight_grad = fc2_got.reshape(F * unit, d // F).astype(F32)

        result, input_grad = pl.pallas_call(
            functools.partial(last_kernel, d, len(gin_terms), len(b2_terms)),
            out_shape=[jax.ShapeDtypeStruct((T, d), BF), jax.ShapeDtypeStruct((T, d), F32)],
            compiler_params=pltpu.CompilerParams(vmem_limit_bytes=VMEM_BYTES),
            cost_estimate=cost(1e6, 5e6),
            name="last",
        )(*gin_terms, *b2_terms, flat_tokens, grad_one, after_own, flat_cot, mask, sel_own, mod)

        shape = (frames, columns, d)
        return (
            result.reshape(shape),
            input_grad.reshape(shape),
            condition_grad,
            ada_weight_grad,
            ada_bias_grad,
            qkv_weight_grad,
            bias_grad[: 2 * d],
            proj_weight_grad,
            bias_grad[2 * d : 3 * d],
            fc1_weight_grad,
            bias_grad[3 * d : 3 * d + ff],
            fc2_weight_grad,
            bias_grad[3 * d + ff :],
        )

    frame, patch = ("x", "core"), ("z", "y")
    every = ("x", "core", "z", "y")
    token_spec = P(None, every, None)
    number_spec = P(None, every)
    row_spec = P(patch, None)
    both_spec = P(patch, frame)
    return jax.shard_map(
        local,
        mesh=grid,
        in_specs=(
            token_spec, number_spec, number_spec, P(), row_spec, P(), row_spec, P(), row_spec, P(), row_spec, P(),
            row_spec, P(), token_spec,
        ),
        out_specs=(
            token_spec, token_spec, P(None, patch), row_spec, P(), both_spec, P(), both_spec, P(), both_spec, P(),
            both_spec, P(),
        ),
        check_vma=False,
    )
```

```python
import functools

import jax
import jax.numpy as jnp
from jax import lax
from jax.experimental import pallas as pl
from jax.experimental.pallas import tpu as pltpu
from jax.sharding import Mesh, PartitionSpec as P

HEAD_DIM = 72
EPSILON = 1e-06
SCORE_SCALE = HEAD_DIM**-0.5
GELU_C = 0.7978845608028654
GELU_A = 0.044715
VMEM_BYTES = 56 * 1024 * 1024
(AT_F, AT_Y, AT_Z, AT_P, AT_G) = range(5)
AT_PART, AT_SLOT, AT_SHARD, AT_PIECE, TABLE = 8, 16, 24, 32, 40
BF = jnp.bfloat16
F32 = jnp.float32


def mm(a, b, ca=1, cb=0):
    return lax.dot_general(a, b, (((ca,), (cb,)), ((), ())), preferred_element_type=F32)


def normalize(values):
    centred = values - jnp.mean(values, axis=-1, keepdims=True)
    inverse = lax.rsqrt(jnp.mean(centred * centred, axis=-1, keepdims=True) + EPSILON)
    return centred * inverse, inverse


def normalize_back(grad_normed, normed, inverse):
    return inverse * (
        grad_normed
        - jnp.mean(grad_normed, axis=-1, keepdims=True)
        - normed * jnp.mean(grad_normed * normed, axis=-1, keepdims=True)
    )


def stack_rows(pieces):
    if pieces[0].shape[0] % 16 == 0:
        return jnp.concatenate(pieces, axis=0)
    return jnp.concatenate([piece.astype(F32) for piece in pieces], axis=0).astype(pieces[0].dtype)


def softmax_prob(queries, key_rows, same_column):
    grid = mm(queries, key_rows, 1, 1) * SCORE_SCALE
    grid = jnp.where(same_column, grid, -1e30)
    expanded = jnp.exp(grid - jnp.max(grid, axis=-1, keepdims=True))
    return expanded / jnp.sum(expanded, axis=-1, keepdims=True)


def column_mask(tokens_per_part, columns):
    rows = lax.broadcasted_iota(jnp.int32, (tokens_per_part, tokens_per_part), 0)
    cols = lax.broadcasted_iota(jnp.int32, (tokens_per_part, tokens_per_part), 1)
    return lax.rem(rows, columns) == lax.rem(cols, columns)


def slab_attention(refs, order, size):
    pieces = []
    for ref, swapped in zip(refs, order):
        piece = ref[...]
        if swapped:
            piece = jnp.concatenate([piece[:, size:], piece[:, :size]], axis=1)
        pieces.append(piece)
    return stack_rows(pieces)


def general_attend_kernel(d, width, columns, tok_ref, sel_ref, mod_ref, w_ref, bias_ref, out_ref, qkv_ref):
    normed, _ = normalize(tok_ref[...].astype(F32))
    sel = sel_ref[...]
    shift = mm(sel, mod_ref[:, 0:d])
    scale = mm(sel, mod_ref[:, d : 2 * d])
    attn_in = (normed * (1.0 + scale) + shift).astype(BF)
    qkv = (mm(attn_in, w_ref[...]) + bias_ref[...]).astype(BF)
    qkv_ref[...] = qkv
    size = tok_ref.shape[0] // 2
    same = column_mask(size, columns)
    for half in range(2):
        rows = slice(half * size, (half + 1) * size)
        parts = []
        for head in range(width // HEAD_DIM):
            q, k, v = (
                qkv[rows, t * width + head * HEAD_DIM : t * width + (head + 1) * HEAD_DIM]
                for t in range(3)
            )
            prob = softmax_prob(q, k, same)
            parts.append(mm(prob.astype(BF), v).T)
        out_ref[:, rows] = jnp.concatenate(parts, axis=0).astype(BF)


def general_mlp_kernel(d, order, *refs):
    n = len(order)
    slots = refs[:n]
    (tok_ref, cot_ref, sel_ref, selt_ref, mod_ref, proj_ref, projb_ref, fc1_ref, fc1b_ref, fc2_ref, fc2b_ref) = refs[n : n + 11]
    (b2_ref, gm_ref, fc1g_ref, fc2g_ref, fc1bg_ref, fc2bg_ref, modg_ref, after_ref, branch_ref, fc1a, fc2a) = refs[n + 11 :]
    step = pl.program_id(0)
    size = tok_ref.shape[0] // 2
    sel = sel_ref[...]
    selt = selt_ref[...]

    def mod(block):
        return mm(sel, mod_ref[:, block * d : (block + 1) * d])

    attn_t = slab_attention(slots, order, size)
    branch_one = mm(attn_t, proj_ref[...], 0, 0) + projb_ref[...]
    after_one = tok_ref[...].astype(F32) + mod(2) * branch_one

    @pl.when(step == 0)
    def _():
        after_ref[...] = after_one[:size]
        branch_ref[...] = branch_one[:size]
        fc1a[...] = jnp.zeros_like(fc1a)
        fc2a[...] = jnp.zeros_like(fc2a)
        fc1bg_ref[...] = jnp.zeros_like(fc1bg_ref)
        fc2bg_ref[...] = jnp.zeros_like(fc2bg_ref)
        modg_ref[...] = jnp.zeros_like(modg_ref)

    normed, _ = normalize(after_one)
    mlp_in = (normed * (1.0 + mod(4)) + mod(3)).astype(BF)
    pre = mm(mlp_in, fc1_ref[...]) + fc1b_ref[...]
    square = pre * pre
    tanh = jnp.tanh(GELU_C * pre * (1.0 + GELU_A * square))
    hidden = (0.5 * pre * (1.0 + tanh)).astype(BF)
    slope = 0.5 * (1.0 + tanh) + 0.5 * pre * (1.0 - tanh * tanh) * GELU_C * (1.0 + 3.0 * GELU_A * square)
    branch_two = mm(hidden, fc2_ref[...]) + fc2b_ref[...]
    b2_ref[...] = branch_two.astype(BF).reshape(b2_ref.shape)
    grad_two = cot_ref[...].astype(F32)
    grad_branch = mod(5) * grad_two
    gb2 = grad_branch.astype(BF)
    fc2bg_ref[...] += jnp.sum(gb2.astype(F32), axis=0, keepdims=True)
    fc2a[...] += mm(hidden, gb2, 0, 0)
    grad_pre = (mm(gb2, fc2_ref[...], 1, 1) * slope).astype(BF)
    fc1bg_ref[...] += jnp.sum(grad_pre.astype(F32), axis=0, keepdims=True)
    fc1a[...] += mm(mlp_in, grad_pre, 0, 0)
    grad_in = mm(grad_pre, fc1_ref[...], 1, 1)
    gm_ref[...] = grad_in.astype(BF).reshape(gm_ref.shape)
    modg_ref[0] += mm(selt, grad_in.astype(BF))
    modg_ref[1] += mm(selt, (grad_in * normed).astype(BF))
    modg_ref[2] += mm(selt, (grad_two * branch_two).astype(BF))

    @pl.when(step == pl.num_programs(0) - 1)
    def _():
        fc1g_ref[...] = fc1a[...].astype(BF)
        fc2g_ref[...] = fc2a[...].astype(BF)


def general_middle_kernel(d, n_parts, count, place_ref, *refs):
    grads = refs[:count]
    (after_ref, branch_ref, cot_ref, sel_ref, selt_ref, mod_ref, proj_ref) = refs[count : count + 7]
    (ex_ref, one_ref, modg_ref, pbias_ref) = refs[count + 7 :]
    sel = sel_ref[...]
    grad_in = grads[0][...].astype(F32)
    for ref in grads[1:]:
        grad_in = grad_in + ref[...].astype(F32)
    normed, inverse = normalize(after_ref[...])
    scale = mm(sel, mod_ref[:, 4 * d : 5 * d])
    gate = mm(sel, mod_ref[:, 2 * d : 3 * d])
    grad_one = cot_ref[...].astype(F32) + normalize_back(grad_in * (1.0 + scale), normed, inverse)
    one_ref[...] = grad_one
    modg_ref[...] = mm(selt_ref[...], (grad_one * branch_ref[...]).astype(BF))
    gb1 = (gate * grad_one).astype(BF)
    gb1_wide = gb1.astype(F32)
    pbias_ref[...] = jnp.sum(gb1_wide, axis=0, keepdims=True)
    width = d // n_parts
    grad_attn = mm(proj_ref[...], gb1, 1, 1)
    gb1_t = gb1_wide.T
    for part in range(n_parts):
        rows = slice(part * width, (part + 1) * width)
        ex_ref[part, 0] = grad_attn[rows].astype(BF)
        ex_ref[place_ref[part], 1] = gb1_t[rows].astype(BF)


def general_attend_back_kernel(d, width, columns, order, place_ref, *refs):
    n = len(order)
    slots = refs[:n]
    (ga_ref, tok_ref, sel_ref, selt_ref, mod_ref, w_ref, qkv_ref) = refs[n : n + 7]
    (gin_ref, qkvg_ref, projg_ref, bias_ref, modg_ref, qkva, proja) = refs[n + 7 :]
    step = pl.program_id(0)
    size = tok_ref.shape[0] // 2

    @pl.when(step == 0)
    def _():
        qkva[...] = jnp.zeros_like(qkva)
        proja[...] = jnp.zeros_like(proja)
        bias_ref[...] = jnp.zeros_like(bias_ref)
        modg_ref[...] = jnp.zeros_like(modg_ref)

    qkv = qkv_ref[...]
    same = column_mask(size, columns)
    heads = width // HEAD_DIM
    halves = []
    for half in range(2):
        rows = slice(half * size, (half + 1) * size)
        grad_mixed = ga_ref[half, 0].astype(F32).T
        pieces = [None] * (3 * heads)
        for head in range(heads):
            q, k, v = (
                qkv[rows, t * width + head * HEAD_DIM : t * width + (head + 1) * HEAD_DIM]
                for t in range(3)
            )
            grad = grad_mixed[:, head * HEAD_DIM : (head + 1) * HEAD_DIM].astype(BF)
            prob = softmax_prob(q, k, same)
            grad_prob = mm(grad, v, 1, 1)
            delta = jnp.sum(prob * grad_prob, axis=-1, keepdims=True)
            grad_score = (prob * (grad_prob - delta) * SCORE_SCALE).astype(BF)
            pieces[head] = mm(grad_score, k)
            pieces[heads + head] = mm(grad_score, q, 0, 0)
            pieces[2 * heads + head] = mm(prob.astype(BF), grad, 0, 0)
        halves.append(jnp.concatenate(pieces, axis=1))
    grad_qkv = jnp.concatenate(halves, axis=0).astype(BF)
    bias_ref[...] += jnp.sum(grad_qkv.astype(F32), axis=0, keepdims=True)

    sel = sel_ref[...]
    selt = selt_ref[...]
    normed, _ = normalize(tok_ref[...].astype(F32))
    shift = mm(sel, mod_ref[:, 0:d])
    scale = mm(sel, mod_ref[:, d : 2 * d])
    attn_in = (normed * (1.0 + scale) + shift).astype(BF)
    qkva[...] += mm(attn_in, grad_qkv, 0, 0)
    grad_in = mm(grad_qkv, w_ref[...], 1, 1)
    gin_ref[...] = grad_in.astype(BF).reshape(gin_ref.shape)
    modg_ref[0] += mm(selt, grad_in.astype(BF))
    modg_ref[1] += mm(selt, (grad_in * normed).astype(BF))

    attn_t = slab_attention(slots, order, size)
    gb1_t = jnp.concatenate([ga_ref[0, 1], ga_ref[1, 1]], axis=1)
    proja[...] += mm(attn_t, gb1_t, 1, 1)

    @pl.when(step == pl.num_programs(0) - 1)
    def _():
        qkvg_ref[...] = qkva[...].astype(BF)
        rows = d // n
        for part in range(n):
            projg_ref[place_ref[part]] = proja[part * rows : (part + 1) * rows].astype(BF)


def general_last_kernel(d, count, count_b, *refs):
    grads = refs[:count]
    branches = refs[count : count + count_b]
    (tok_ref, one_ref, after_ref, cot_ref, mask_ref, sel_ref, mod_ref) = refs[count + count_b : count + count_b + 7]
    (out_ref, grad_ref) = refs[count + count_b + 7 :]
    sel = sel_ref[...]
    masked = mask_ref[...] == 1
    tokens = tok_ref[...].astype(F32)
    grad_in = grads[0][...].astype(F32)
    for ref in grads[1:]:
        grad_in = grad_in + ref[...].astype(F32)
    normed, inverse = normalize(tokens)
    scale = mm(sel, mod_ref[:, d : 2 * d])
    back = normalize_back(grad_in * (1.0 + scale), normed, inverse)
    grad_ref[...] = jnp.where(masked, cot_ref[...].astype(F32), 0.0) + one_ref[...] + back
    branch = branches[0][...].astype(F32)
    for ref in branches[1:]:
        branch = branch + ref[...].astype(F32)
    gate = mm(sel, mod_ref[:, 5 * d : 6 * d])
    out_ref[...] = jnp.where(masked, tokens, after_ref[...] + gate * branch).astype(BF)


def params(steps=1):
    return pltpu.CompilerParams(vmem_limit_bytes=VMEM_BYTES, dimension_semantics=("arbitrary",) * steps)


def cost(flops, bytes_accessed):
    return pl.CostEstimate(flops=int(flops), bytes_accessed=int(bytes_accessed), transcendentals=0)


def whole(shape):
    return pl.BlockSpec(shape, lambda *_: (0,) * len(shape))


def matchings(frames):
    left = {f: {t: (frames * t + f) // 3 for t in range(3)} for f in range(frames)}
    rounds = []
    for _ in range(3):
        taken = {}

        def place(f, seen):
            for t, to in left[f].items():
                if to in seen:
                    continue
                seen.add(to)
                if to not in taken or place(taken[to][0], seen):
                    taken[to] = (f, t)
                    return True
            return False

        for f in range(frames):
            place(f, set())
        chosen = {f: (t, to) for to, (f, t) in taken.items()}
        for f, (t, _to) in chosen.items():
            del left[f][t]
        rounds.append(chosen)
    return rounds


def general_solution(mesh):
    F, N = mesh.shape["frame"], mesh.shape["patch"]
    C, Y = 2, 2
    X, Z = F // C, N // Y
    G = X * C * Y
    half_slots = X * Y
    grid = Mesh(mesh.devices.reshape(X, C, Z, Y), ("x", "core", "z", "y"))
    everywhere = ("x", "core", "z", "y")
    offsets = [(dc, dx, dy) for dc in range(C) for dx in range(X) for dy in range(Y)]

    def from_xy(a, dx, dy):
        if dx == 0 and dy == 0:
            return a
        pairs = [
            (x * Y + y, ((x - dx) % X) * Y + (y - dy) % Y) for x in range(X) for y in range(Y)
        ]
        return lax.ppermute(a, ("x", "y"), pairs)

    def to_xy(a, dx, dy):
        return from_xy(a, (-dx) % X, (-dy) % Y)

    def swap_core(a):
        return lax.ppermute(a, "core", [(0, 1), (1, 0)])

    def swap_y(a):
        return lax.ppermute(a, "y", [(0, 1), (1, 0)])

    def gather_slots(a):
        mine = [from_xy(a, dx, dy) for dx in range(X) for dy in range(Y)]
        return mine + [swap_core(piece) for piece in mine]

    def scatter_sum(slots):
        received = swap_core(slots[half_slots:])
        terms = []
        for slot in range(half_slots):
            total = slots[slot].astype(F32) + received[slot].astype(F32)
            terms.append(to_xy(total.astype(BF), slot // Y, slot % Y))
        return terms

    def exchange(slots):
        received = swap_core(slots[half_slots:])
        pieces = [None] * G
        for slot in range(half_slots):
            dx, dy = slot // Y, slot % Y
            pair = to_xy(jnp.stack([slots[slot], received[slot]]), dx, dy)
            source = ((-dx) % X) * Y + (-dy) % Y
            pieces[source] = pair[0]
            pieces[half_slots + source] = pair[1]
        return jnp.stack(pieces)

    def local(tokens, image_mask, sample_index, condition, ada_weight, ada_bias, qkv_weight, qkv_bias,
              proj_weight, proj_bias, fc1_weight, fc1_bias, fc2_weight, fc2_bias, cotangent):
        frames, columns, d = tokens.shape
        T = frames * columns
        S = G * T
        samples = condition.shape[0]
        rows_here = ada_weight.shape[0]
        ff = fc1_weight.shape[1]
        width = d // G
        unit = ff // (N * F)
        part_ff = Z * unit
        x_i, c_i = lax.axis_index("x"), lax.axis_index("core")
        z_i, y_i = lax.axis_index("z"), lax.axis_index("y")
        f_i = x_i * C + c_i
        p_i = z_i * Y + y_i
        g_i = f_i * Y + y_i
        parts_at = [
            (((x_i + dx) % X) * C + (c_i + dc) % C) * Y + (y_i + dy) % Y for dc, dx, dy in offsets
        ]
        parts_at = jnp.stack(parts_at).astype(jnp.int32)
        all_parts = jnp.arange(G, dtype=jnp.int32)
        part_x, part_c, part_y = all_parts // (C * Y), (all_parts // Y) % C, all_parts % Y
        place = ((part_c - c_i) % C) * half_slots + ((part_x - x_i) % X) * Y + (part_y - y_i) % Y
        place = place.astype(jnp.int32)

        def y_pair(own, other):
            got = swap_y(other)
            return jnp.where(y_i == 0, jnp.stack([own, got]), jnp.stack([got, own]))

        pair_width = Y * width
        qkv_cols = [
            lax.dynamic_slice_in_dim(qkv_weight, t * d + f_i * pair_width, pair_width, 1) for t in range(3)
        ]

        def qkv_for(which):
            return jnp.concatenate(
                [lax.dynamic_slice_in_dim(c, which * width, width, 1) for c in qkv_cols], axis=1
            )

        qkv_rows = y_pair(qkv_for(y_i), qkv_for(1 - y_i)).reshape(Y * rows_here, 3 * width)
        w_qkv = lax.all_gather(qkv_rows, "z", axis=0, tiled=True)
        half_rows = rows_here // C
        proj_half = lax.dynamic_slice_in_dim(proj_weight, c_i * half_rows, half_rows, 0)
        proj_rows = y_pair(proj_half, proj_half).reshape(Y * half_rows, d)
        proj_mine = lax.all_gather(proj_rows, "z", axis=0, tiled=True)
        proj_other = swap_core(proj_mine)
        proj_both = jnp.where(
            c_i == 0, jnp.stack([proj_mine, proj_other]), jnp.stack([proj_other, proj_mine])
        )
        proj_parts = (
            proj_both.reshape(C, N, half_rows, d).transpose(1, 0, 2, 3).reshape(G, width, d)
        )
        proj_rel = jnp.concatenate(
            [lax.dynamic_index_in_dim(proj_parts, parts_at[r], 0, keepdims=False) for r in range(G)],
            axis=0,
        )

        def fc1_for(which):
            return jnp.concatenate(
                [
                    lax.dynamic_slice_in_dim(
                        fc1_weight, (z * Y + which) * (F * unit) + f_i * unit, unit, 1
                    )
                    for z in range(Z)
                ],
                axis=1,
            )

        fc1_rows = y_pair(fc1_for(y_i), fc1_for(1 - y_i)).reshape(Y * rows_here, part_ff)
        w_fc1 = lax.all_gather(fc1_rows, "z", axis=0, tiled=True)
        fc2_rows = lax.dynamic_slice_in_dim(fc2_weight, f_i * unit, unit, 0)
        w_fc2 = lax.all_gather(fc2_rows, "z", axis=0, tiled=True)

        chunk = samples * 6 * d // (F * N)
        per_row = 6 * d // chunk
        frame_samples = samples // F
        first_row = p_i * rows_here
        cond_rows = lax.dynamic_slice_in_dim(condition, first_row, rows_here, 1).astype(F32)
        sigmoid = 1.0 / (1.0 + jnp.exp(-cond_rows))
        act_rows = (cond_rows * sigmoid).astype(BF)
        silu_slope = sigmoid * (1.0 + cond_rows * (1.0 - sigmoid))
        act_mine = lax.dynamic_slice_in_dim(act_rows, f_i * frame_samples, frame_samples, 0)
        partial_mod = mm(act_mine, ada_weight).reshape(N, chunk)
        mod_terms = lax.all_to_all(partial_mod, ("z", "y"), 0, 0, tiled=True)
        bias_here = lax.dynamic_slice_in_dim(ada_bias, (p_i % per_row) * chunk, chunk, 0)
        mod_chunk = (jnp.sum(mod_terms, axis=0) + bias_here.astype(F32)).astype(BF)
        mod = lax.all_to_all(
            jnp.broadcast_to(mod_chunk, (F * N, chunk)), everywhere, 0, 0, tiled=True
        ).reshape(samples, 6 * d)

        flat_tokens = tokens.reshape(T, d)
        flat_cot = cotangent.reshape(T, d)
        mask = image_mask.reshape(T, 1)
        grad_two_own = jnp.where(mask == 1, jnp.zeros_like(flat_cot), flat_cot)
        codes = jnp.zeros((16, d), BF).at[0, :T].set(sample_index.reshape(T).astype(BF))
        token_slots = gather_slots(jnp.concatenate([flat_tokens, codes], axis=0))
        slab_tokens = jnp.concatenate([piece[:T] for piece in token_slots], axis=0)
        slab_codes = jnp.stack([piece[T, :T] for piece in token_slots]).astype(jnp.int32)
        slab_cot = jnp.concatenate(gather_slots(grad_two_own), axis=0)
        numbers = jnp.arange(samples, dtype=jnp.int32)
        selt = (slab_codes.reshape(1, S) == numbers[:, None]).astype(BF)
        sel = (slab_codes.reshape(S, 1) == numbers[None, :]).astype(BF)
        sel_own, selt_own = sel[:T], selt[:, :T]

        steps = G // 2
        TB = 2 * T
        row_block = lambda w: pl.BlockSpec((TB, w), lambda j: (j, 0))
        lane_block = lambda h: pl.BlockSpec((h, TB), lambda j: (0, j))

        bias_q = lax.dynamic_slice_in_dim(qkv_bias, g_i * width, width, 0)
        bias_v = lax.dynamic_slice_in_dim(qkv_bias, d + g_i * width, width, 0)
        bias_qkv = jnp.concatenate([bias_q, jnp.zeros_like(bias_q), bias_v]).astype(F32)[None]
        attn_t, qkv = pl.pallas_call(
            functools.partial(general_attend_kernel, d, width, columns),
            grid=(steps,),
            in_specs=[
                row_block(d),
                row_block(samples),
                whole((samples, 6 * d)),
                whole((d, 3 * width)),
                whole((1, 3 * width)),
            ],
            out_specs=[lane_block(width), row_block(3 * width)],
            out_shape=[
                jax.ShapeDtypeStruct((width, S), BF),
                jax.ShapeDtypeStruct((S, 3 * width), BF),
            ],
            compiler_params=params(),
            cost_estimate=cost(2 * S * d * 3 * width * 2, 8e6),
            name="attend",
        )(slab_tokens, sel, mod, w_qkv, bias_qkv)

        attn_slots = gather_slots(attn_t)
        order = [dy == 1 for _, _, dy in offsets]

        def slot_spec(dc, dx):
            return pl.BlockSpec(
                (width, TB),
                lambda j: (0, ((j // X + C - dc) % C) * X + (j % X + X - dx) % X),
            )

        slot_specs = [slot_spec(dc, dx) for dc, dx, _ in offsets]

        hidden_at = lambda v: jnp.concatenate(
            [
                lax.dynamic_slice_in_dim(v, (z * Y + y_i) * (F * unit) + f_i * unit, unit, 0)
                for z in range(Z)
            ]
        )
        fc1_bias_part = hidden_at(fc1_bias).astype(F32)[None]
        fc2_bias_once = jnp.where(g_i == 0, fc2_bias.astype(F32), 0.0)[None]
        slot_out = pl.BlockSpec((2, T, d), lambda j: (j, 0, 0))
        (b2_slots, gm_slots, fc1g, fc2g, fc1_bias_g, fc2_bias_g, modg_two, after_own, branch_own) = pl.pallas_call(
            functools.partial(general_mlp_kernel, d, order),
            grid=(steps,),
            in_specs=slot_specs
            + [
                row_block(d),
                row_block(d),
                row_block(samples),
                lane_block(samples),
                whole((samples, 6 * d)),
                whole((d, d)),
                whole((1, d)),
                whole((d, part_ff)),
                whole((1, part_ff)),
                whole((part_ff, d)),
                whole((1, d)),
            ],
            out_specs=[
                slot_out,
                slot_out,
                whole((d, part_ff)),
                whole((part_ff, d)),
                whole((1, part_ff)),
                whole((1, d)),
                whole((3, samples, d)),
                whole((T, d)),
                whole((T, d)),
            ],
            out_shape=[
                jax.ShapeDtypeStruct((G, T, d), BF),
                jax.ShapeDtypeStruct((G, T, d), BF),
                jax.ShapeDtypeStruct((d, part_ff), BF),
                jax.ShapeDtypeStruct((part_ff, d), BF),
                jax.ShapeDtypeStruct((1, part_ff), F32),
                jax.ShapeDtypeStruct((1, d), F32),
                jax.ShapeDtypeStruct((3, samples, d), F32),
                jax.ShapeDtypeStruct((T, d), F32),
                jax.ShapeDtypeStruct((T, d), F32),
            ],
            scratch_shapes=[pltpu.VMEM((d, part_ff), F32), pltpu.VMEM((part_ff, d), F32)],
            compiler_params=params(),
            cost_estimate=cost(2 * S * (d * d + 6 * d * part_ff), 3e7),
            name="mlp",
        )(
            *attn_slots,
            slab_tokens,
            slab_cot,
            sel,
            selt,
            mod,
            proj_rel,
            proj_bias.astype(F32)[None],
            w_fc1,
            fc1_bias_part,
            w_fc2,
            fc2_bias_once,
        )

        fc1_z = lax.psum_scatter(fc1g, "z", scatter_dimension=0, tiled=True)
        fc2_z = lax.psum_scatter(fc2g, "z", scatter_dimension=0, tiled=True)
        gm_terms = scatter_sum(gm_slots)

        ex_slots, grad_one, modg_gate, proj_bias_g = pl.pallas_call(
            functools.partial(general_middle_kernel, d, G, len(gm_terms)),
            grid_spec=pltpu.PrefetchScalarGridSpec(
                num_scalar_prefetch=1,
                grid=(1,),
                in_specs=[whole((T, d))] * len(gm_terms)
                + [
                    whole((T, d)),
                    whole((T, d)),
                    whole((T, d)),
                    whole((T, samples)),
                    whole((samples, T)),
                    whole((samples, 6 * d)),
                    whole((d, d)),
                ],
                out_specs=[
                    whole((G, 2, width, T)),
                    whole((T, d)),
                    whole((samples, d)),
                    whole((1, d)),
                ],
            ),
            out_shape=[
                jax.ShapeDtypeStruct((G, 2, width, T), BF),
                jax.ShapeDtypeStruct((T, d), F32),
                jax.ShapeDtypeStruct((samples, d), F32),
                jax.ShapeDtypeStruct((1, d), F32),
            ],
            compiler_params=params(),
            cost_estimate=cost(4 * T * d * d, 8e6),
            name="middle",
        )(place, *gm_terms, after_own, branch_own, grad_two_own, sel_own, selt_own, mod, proj_rel)

        grad_attn = exchange(ex_slots)
        b2_terms = scatter_sum(b2_slots)

        slot_back = [
            pl.BlockSpec(spec.block_shape, lambda j, place, spec=spec: spec.index_map(j))
            for spec in slot_specs
        ]
        rows_b = lambda w: pl.BlockSpec((TB, w), lambda j, place: (j, 0))
        gin_slots, qkvg, projg, qkv_bias_part, modg_one = pl.pallas_call(
            functools.partial(general_attend_back_kernel, d, width, columns, order),
            grid_spec=pltpu.PrefetchScalarGridSpec(
                num_scalar_prefetch=1,
                grid=(steps,),
                in_specs=slot_back
                + [
                    pl.BlockSpec((2, 2, width, T), lambda j, place: (j, 0, 0, 0)),
                    rows_b(d),
                    rows_b(samples),
                    pl.BlockSpec((samples, TB), lambda j, place: (0, j)),
                    whole((samples, 6 * d)),
                    whole((d, 3 * width)),
                    rows_b(3 * width),
                ],
                out_specs=[
                    pl.BlockSpec((2, T, d), lambda j, place: (j, 0, 0)),
                    whole((d, 3 * width)),
                    whole((G, width, width)),
                    whole((1, 3 * width)),
                    whole((2, samples, d)),
                ],
                scratch_shapes=[
                    pltpu.VMEM((d, 3 * width), F32),
                    pltpu.VMEM((d, width), F32),
                ],
            ),
            out_shape=[
                jax.ShapeDtypeStruct((G, T, d), BF),
                jax.ShapeDtypeStruct((d, 3 * width), BF),
                jax.ShapeDtypeStruct((G, width, width), BF),
                jax.ShapeDtypeStruct((1, 3 * width), F32),
                jax.ShapeDtypeStruct((2, samples, d), F32),
            ],
            compiler_params=params(),
            cost_estimate=cost(2 * S * d * 8 * width, 1.2e7),
            name="attend_back",
        )(parts_at, *attn_slots, grad_attn, slab_tokens, sel, selt, mod, w_qkv, qkv)

        gin_terms = scatter_sum(gin_slots)

        bias_total = 2 * d + d + ff + d
        biases = jnp.zeros((bias_total,), F32)
        put = lax.dynamic_update_slice_in_dim
        biases = put(biases, qkv_bias_part[0, :width], g_i * width, 0)
        biases = put(biases, qkv_bias_part[0, 2 * width :], d + g_i * width, 0)
        biases = put(biases, proj_bias_g[0], 2 * d, 0)
        for z in range(Z):
            biases = put(
                biases,
                fc1_bias_g[0, z * unit : (z + 1) * unit],
                3 * d + (z * Y + y_i) * (F * unit) + f_i * unit,
                0,
            )
        biases = put(biases, jnp.where(g_i == 0, fc2_bias_g[0], 0.0), 3 * d + ff, 0)
        mod_sums = jnp.concatenate(
            [modg_one[0], modg_one[1], modg_gate, modg_two[0], modg_two[1], modg_two[2]], axis=1
        )
        to_sum = jnp.concatenate(
            [mod_sums.reshape(F * N, chunk), biases.reshape(F * N, bias_total // (F * N))], axis=1
        ).astype(BF)
        terms = lax.all_to_all(to_sum, everywhere, 0, 0, tiled=True)
        summed = jnp.sum(terms.astype(F32), axis=0).astype(BF)
        total = lax.all_to_all(
            jnp.broadcast_to(summed, (F * N, summed.shape[0])), everywhere, 0, 0, tiled=True
        )
        mod_grad = total[:, :chunk].reshape(samples, 6 * d)
        bias_grad = total[:, chunk:].reshape(bias_total).astype(F32)
        ada_bias_grad = jnp.sum(mod_grad.astype(F32), axis=0)
        ada_weight_grad = mm(act_rows, mod_grad, 0, 0)
        condition_grad = mm(mod_grad, ada_weight, 1, 1) * silu_slope

        def y_join(rows):
            kept = lax.dynamic_index_in_dim(rows, y_i, 0, keepdims=False)
            got = swap_y(lax.dynamic_index_in_dim(rows, 1 - y_i, 0, keepdims=False))
            return jnp.where(y_i == 0, jnp.stack([kept, got]), jnp.stack([got, kept]))

        attn_g = jnp.concatenate([qkvg, projg.reshape(d, width)], axis=1)
        attn_z = lax.psum_scatter(attn_g, "z", scatter_dimension=0, tiled=True)
        attn_y = y_join(attn_z.reshape(Y, rows_here, 4 * width))
        blocks = jnp.stack(
            [
                jnp.concatenate([attn_y[y, :, t * width : (t + 1) * width] for y in range(Y)], axis=1)
                for t in range(4)
            ]
        )
        proj_weight_grad = blocks[3].astype(F32)
        moved = [None] * 3
        spots = jnp.zeros((3, F), jnp.int32)
        for turn, chosen in enumerate(matchings(F)):
            picks = jnp.array([chosen[f][0] for f in range(F)], jnp.int32)
            block = lax.dynamic_index_in_dim(blocks, picks[f_i], 0, keepdims=False)
            pairs = [(f, chosen[f][1]) for f in range(F)]
            if any(a != b for a, b in pairs):
                block = lax.ppermute(block, ("x", "core"), pairs)
            moved[turn] = block
            for f in range(F):
                t, to = chosen[f]
                spots = spots.at[(F * t + f) % 3, to].set(turn)
        moved = jnp.stack(moved)
        qkv_weight_grad = jnp.concatenate(
            [
                lax.dynamic_index_in_dim(moved, spots[k, f_i], 0, keepdims=False)
                for k in range(3)
            ],
            axis=1,
        ).astype(F32)

        fc1_y = y_join(fc1_z.reshape(Y, rows_here, part_ff))
        per_frame = Z // F
        fc1_send = fc1_y.reshape(Y, rows_here, F, per_frame, unit).transpose(2, 1, 3, 0, 4)
        fc1_got = lax.all_to_all(fc1_send, ("x", "core"), 0, 0, tiled=True)
        fc1_weight_grad = (
            fc1_got.transpose(1, 2, 3, 0, 4).reshape(rows_here, ff // F).astype(F32)
        )
        fc2_send = fc2_z.reshape(unit, F, d // F).transpose(1, 0, 2)
        fc2_got = lax.all_to_all(fc2_send, ("x", "core"), 0, 0, tiled=True)
        fc2_weight_grad = fc2_got.reshape(F * unit, d // F).astype(F32)

        result, input_grad = pl.pallas_call(
            functools.partial(general_last_kernel, d, len(gin_terms), len(b2_terms)),
            out_shape=[jax.ShapeDtypeStruct((T, d), BF), jax.ShapeDtypeStruct((T, d), F32)],
            compiler_params=pltpu.CompilerParams(vmem_limit_bytes=VMEM_BYTES),
            cost_estimate=cost(1e6, 5e6),
            name="last",
        )(*gin_terms, *b2_terms, flat_tokens, grad_one, after_own, flat_cot, mask, sel_own, mod)

        shape = (frames, columns, d)
        return (
            result.reshape(shape),
            input_grad.reshape(shape),
            condition_grad,
            ada_weight_grad,
            ada_bias_grad,
            qkv_weight_grad,
            bias_grad[: 2 * d],
            proj_weight_grad,
            bias_grad[2 * d : 3 * d],
            fc1_weight_grad,
            bias_grad[3 * d : 3 * d + ff],
            fc2_weight_grad,
            bias_grad[3 * d + ff :],
        )

    frame, patch = ("x", "core"), ("z", "y")
    every = ("x", "core", "z", "y")
    token_spec = P(None, every, None)
    number_spec = P(None, every)
    row_spec = P(patch, None)
    both_spec = P(patch, frame)
    return jax.shard_map(
        local,
        mesh=grid,
        in_specs=(
            token_spec, number_spec, number_spec, P(), row_spec, P(), row_spec, P(), row_spec, P(), row_spec, P(),
            row_spec, P(), token_spec,
        ),
        out_specs=(
            token_spec, token_spec, P(None, patch), row_spec, P(), both_spec, P(), both_spec, P(), both_spec, P(),
            both_spec, P(),
        ),
        check_vma=False,
    )


def takes(microseconds):
    return pl.CostEstimate(flops=1000, bytes_accessed=1000, transcendentals=0)


def wide(lanes):
    return -(-lanes // 128) * 128


def row_of(values):
    return jnp.concatenate([values[k : k + 1] for k in range(values.shape[0])], axis=1)


def put_row(ref, row):
    for k in range(ref.shape[0]):
        ref[k : k + 1] = row[:, k * 128 : (k + 1) * 128]


def pick(index, options):
    total = jnp.where(index == 0, options[0], 0.0)
    for k in range(1, len(options)):
        total = total + jnp.where(index == k, options[k], 0.0)
    return total


def spread(values, index, n):
    return jnp.concatenate([jnp.where(index == k, values, 0.0) for k in range(n)], axis=1)


def at_rows(index, rows):
    return pl.ds(pl.multiple_of(index * rows, rows), rows)


def prepare_kernel(d, place, cond_ref, ada_ref, qkv_ref, fc1_ref, proj_ref, fc2_ref, tok_ref, cot_ref, num_ref, mask_ref,
                   part_ref, act_ref, slope_ref, qkv_mine, fc1_mine, send_out, fc2_out, tok_out, act_all):
    rows = ada_ref.shape[0]
    cols = 2 * rows
    for ref in (qkv_mine, fc1_mine, send_out, fc2_out):
        ref[...] = jnp.zeros_like(ref)
    act_ref[...] = jnp.zeros_like(act_ref)
    slope_ref[...] = jnp.zeros_like(slope_ref)
    for f in range(4):

        @pl.when(place[AT_F] == f)
        def _():
            fc2_out[:, d : d + cols] = proj_ref[:, f * cols : (f + 1) * cols]
            for y in range(2):
                for q_out, at_q, f_out, want in ((qkv_mine, 0, fc1_mine, y), (send_out, wide(4 * rows), send_out, 1 - y)):

                    @pl.when(place[AT_Y] == want)
                    def _():
                        for t in range(3):
                            at = t * d + (2 * f + y) * rows
                            q_out[:, at_q + t * rows : at_q + (t + 1) * rows] = qkv_ref[:, at : at + rows]
                        for z in range(4):
                            at = ((z * 2 + y) * 4 + f) * rows
                            f_out[:, z * rows : (z + 1) * rows] = fc1_ref[:, at : at + rows]

    fc2_out[:, :d] = fc2_ref[at_rows(place[AT_F], rows)]
    row = lax.broadcasted_iota(jnp.int32, (d, rows), 0)
    col = lax.broadcasted_iota(jnp.int32, (d, rows), 1)
    cond = mm(cond_ref[...], (row == col + place[AT_P] * rows).astype(BF))
    sigmoid = 1.0 / (1.0 + jnp.exp(-cond))
    act = cond * sigmoid
    act_ref[:, :rows] = act.astype(BF)
    slope_ref[:, :rows] = sigmoid * (1.0 + cond * (1.0 - sigmoid))
    act_all[...] = act
    mine = act_all[at_rows(place[AT_F], 8)].astype(BF)
    for block in range(8):
        if block < 6:
            part_ref[block] = mm(mine, ada_ref[:, block * d : (block + 1) * d]).astype(BF)
        else:
            part_ref[block] = jnp.zeros(part_ref.shape[1:], BF)
    size = tok_ref.shape[0]
    columns, frames = num_ref.shape

    def token_row(ref):
        lane = lax.broadcasted_iota(jnp.int32, (frames, size), 1)
        frame = lax.broadcasted_iota(jnp.int32, (frames, size), 0)
        wide = mm(ref[...].astype(F32).astype(BF), (lane // columns == frame).astype(BF))
        lane = lax.broadcasted_iota(jnp.int32, (columns, size), 1)
        column = lax.broadcasted_iota(jnp.int32, (columns, size), 0)
        return jnp.sum(jnp.where(lax.rem(lane, columns) == column, wide, 0.0), axis=0, keepdims=True)

    tok_out[size : 2 * size] = tok_ref[...]
    tok_out[2 * size :] = jnp.zeros((16, d), BF)
    tok_out[2 * size :, :size] = jnp.broadcast_to(token_row(num_ref), (16, size)).astype(BF)
    masked = jnp.broadcast_to(token_row(mask_ref), (size, size)).T[:, 0:1]
    tok_out[:size] = jnp.where(masked > 0.5, 0.0, cot_ref[...].astype(F32)).astype(BF)


def mod_sum_kernel(place, terms_ref, bias_ref, out_ref):
    total = terms_ref[0].astype(F32)
    for k in range(1, terms_ref.shape[0]):
        total = total + terms_ref[k].astype(F32)
    bias = row_of(bias_ref[...].astype(F32))
    d = total.shape[1]
    total = total + pick(place[AT_P], [bias[:, k * d : (k + 1) * d] for k in range(6)])
    out_ref[...] = total.astype(BF)


def grad_sum_kernel(place, terms_ref, out_ref):
    total = terms_ref[0].astype(F32)
    for k in range(1, terms_ref.shape[0]):
        total = total + terms_ref[k].astype(F32)
    out_ref[...] = total.astype(BF)


def chunk_of(ref, place, chunk):
    at_z = lax.bitwise_xor(place[AT_Z], chunk // 2 % 4)
    return ref[chunk // 8 * 2 + chunk % 2, at_z]


def token_pair(near_ref, far_ref, size):
    near = pl.program_id(0) < pl.num_programs(0) // 2
    parts, codes = [], []
    for half in range(2):
        rows = slice(size, 2 * size)
        parts.append(jnp.where(near, near_ref[half, rows].astype(F32), far_ref[half, rows].astype(F32)))
        rows = slice(2 * size, 2 * size + 16)
        code = jnp.where(near, near_ref[half, rows, :size].astype(F32), far_ref[half, rows, :size].astype(F32))
        codes.append(code[0:1])
    return jnp.concatenate(parts, axis=0), codes


def attend_kernel(d, width, columns, place, tok_near, tok_far, w_in, modin_ref, bias_ref,
                  out_ref, qkv_ref, sel_ref, selt_ref, w_ref, mod_ref, bias_row):
    step = pl.program_id(0)
    samples = selt_ref.shape[0]
    size = out_ref.shape[1] // 2

    @pl.when(step == 0)
    def _():
        for z in range(4):
            for dy in range(2):
                patch = z * 2 + lax.bitwise_xor(place[AT_Y], dy)
                w_ref[at_rows(patch, width), :] = w_in[z, dy]
        for block in range(6):
            pieces = [chunk_of(modin_ref, place, f * 8 + block).astype(F32) for f in range(4)]
            mod_ref[block] = jnp.concatenate(pieces, axis=0).astype(BF)
        bias = row_of(bias_ref[...].astype(F32))
        bias_row[:, :width] = pick(place[AT_G], [bias[:, k * width : (k + 1) * width] for k in range(8)])
        bias_row[:, width : 2 * width] = jnp.zeros((1, width), F32)
        bias_row[:, 2 * width :] = pick(place[AT_G], [bias[:, d + k * width : d + (k + 1) * width] for k in range(8)])

    numbers = lax.broadcasted_iota(jnp.int32, (samples, size), 0).astype(F32)
    tokens, codes = token_pair(tok_near, tok_far, size)
    for half in range(2):
        rows = slice(half * size, (half + 1) * size)
        hot = (codes[half] == numbers).astype(F32)
        selt_ref[:, rows] = hot.astype(BF)
        sel_ref[rows, :samples] = hot.T.astype(BF)
    normed, _ = normalize(tokens)
    sel = sel_ref[:, : mod_ref.shape[1]]
    attn_in = (normed * (1.0 + mm(sel, mod_ref[1])) + mm(sel, mod_ref[0])).astype(BF)
    qkv = (mm(attn_in, w_ref[:, : 3 * width]) + bias_row[...]).astype(BF)
    qkv_ref[:, : 3 * width] = qkv
    same = column_mask(size, columns)
    for half in range(2):
        rows = slice(half * size, (half + 1) * size)
        parts = []
        for head in range(width // HEAD_DIM):
            q, k, v = (
                qkv[rows, t * width + head * HEAD_DIM : t * width + (head + 1) * HEAD_DIM]
                for t in range(3)
            )
            prob = softmax_prob(q, k, same)
            parts.append(mm(prob.astype(BF), v).T)
        out_ref[:, rows] = jnp.concatenate(parts, axis=0).astype(BF)


def proj_kernel(d, place, *refs):
    rows = d // 8
    pieces, (proj_all, columns) = refs[:8], refs[8:]
    for slot, ref in enumerate(pieces):
        columns[slot] = ref[...]
    for slot in range(8):
        part = place[AT_PART + slot]
        for f in range(4):
            source = place[AT_SLOT + f * 2 + lax.rem(part, 2)]
            proj_all[slot * rows : (slot + 1) * rows, f * 2 * rows : (f + 1) * 2 * rows] = columns[source, part // 2]


def mlp_kernel(d, order, place, *refs):
    n = len(order)
    slots = refs[:n]
    (tok_near, tok_far, sel_ref, selt_ref, mod_ref, proj_all, projb_ref, fc1_in, fc1b_ref, fc2_in, fc2b_ref) = refs[n : n + 11]
    (b2_own, b2_far, gm_own, gm_far, fcg_ref, fc1bg_ref, fc2bg_ref, modg_ref, after_ref, branch_ref) = refs[n + 11 : n + 21]
    (fc1a, fc2a, fc1_ref, fc2_ref, pb_row, f1_row, f2_row) = refs[n + 21 :]
    step = pl.program_id(0)
    size = sel_ref.shape[0] // 2
    rows = d // 8
    sel = sel_ref[:, : mod_ref.shape[1]]
    selt = selt_ref[...]

    @pl.when(step == 0)
    def _():
        for z in range(4):
            for dy in range(2):
                patch = z * 2 + lax.bitwise_xor(place[AT_Y], dy)
                fc1_ref[at_rows(patch, rows), :] = fc1_in[z, dy, :, : 4 * rows]
            fc2_ref[z * rows : (z + 1) * rows] = fc2_in[z, :, :d]
        pb_row[...] = row_of(projb_ref[...].astype(F32))
        f2_row[...] = jnp.where(place[AT_G] == 0, row_of(fc2b_ref[...].astype(F32)), 0.0)
        bias = row_of(fc1b_ref[...].astype(F32))
        for z in range(4):
            options = []
            for k in range(8):
                at = (z * 8 + k) * rows
                options.append(bias[:, at : at + rows])
            f1_row[:, z * rows : (z + 1) * rows] = pick(place[AT_Y] * 4 + place[AT_F], options)

    tokens, _ = token_pair(tok_near, tok_far, size)
    grad_two = jnp.where(step < pl.num_programs(0) // 2, tok_near[:, :size].astype(F32), tok_far[:, :size].astype(F32))
    grad_two = grad_two.reshape(2 * size, d)
    attn_t = slab_attention(slots, order, size)
    branch_one = mm(attn_t, proj_all[...], 0, 0) + pb_row[...]
    after_one = tokens + mm(sel, mod_ref[2]) * branch_one

    @pl.when(step == 0)
    def _():
        after_ref[...] = after_one[:size]
        branch_ref[...] = branch_one[:size]
        fc1a[...] = jnp.zeros_like(fc1a)
        fc2a[...] = jnp.zeros_like(fc2a)
        fc1bg_ref[...] = jnp.zeros_like(fc1bg_ref)
        fc2bg_ref[...] = jnp.zeros_like(fc2bg_ref)
        modg_ref[...] = jnp.zeros_like(modg_ref)

    normed, _ = normalize(after_one)
    mlp_in = (normed * (1.0 + mm(sel, mod_ref[4])) + mm(sel, mod_ref[3])).astype(BF)
    pre = mm(mlp_in, fc1_ref[...]) + f1_row[...]
    square = pre * pre
    tanh = jnp.tanh(GELU_C * pre * (1.0 + GELU_A * square))
    hidden = (0.5 * pre * (1.0 + tanh)).astype(BF)
    slope = 0.5 * (1.0 + tanh) + 0.5 * pre * (1.0 - tanh * tanh) * GELU_C * (1.0 + 3.0 * GELU_A * square)
    branch_two = mm(hidden, fc2_ref[...]) + f2_row[...]
    gb2 = (mm(sel, mod_ref[5]) * grad_two).astype(BF)
    fc2bg_ref[...] += jnp.sum(gb2.astype(F32), axis=0, keepdims=True)
    fc2a[...] += mm(hidden, gb2, 0, 0)
    grad_pre = (mm(gb2, fc2_ref[...], 1, 1) * slope).astype(BF)
    fc1bg_ref[...] += jnp.sum(grad_pre.astype(F32), axis=0, keepdims=True)
    fc1a[...] += mm(mlp_in, grad_pre, 0, 0)
    grad_in = mm(grad_pre, fc1_ref[...], 1, 1)
    modg_ref[0] += mm(selt, grad_in.astype(BF))
    modg_ref[1] += mm(selt, (grad_in * normed).astype(BF))
    modg_ref[2] += mm(selt, (grad_two * branch_two).astype(BF))
    near = step < pl.num_programs(0) // 2

    @pl.when(near)
    def _():
        b2_own[...] = branch_two.astype(BF).reshape(b2_own.shape)
        gm_own[...] = grad_in.astype(BF).reshape(gm_own.shape)

    @pl.when(jnp.logical_not(near))
    def _():
        b2_far[...] = branch_two.astype(BF).reshape(b2_far.shape)
        gm_far[...] = grad_in.astype(BF).reshape(gm_far.shape)

    @pl.when(step == pl.num_programs(0) - 1)
    def _():
        for z in range(4):
            for y in range(2):
                at = (z * 2 + y) * rows
                to = (z * 4 + y) * rows
                fcg_ref[to : to + rows, : 4 * rows] = fc1a[at : at + rows].astype(BF)
            block = fc2a[z * rows : (z + 1) * rows].astype(BF)
            to = (z * 4 + 2) * rows
            fcg_ref[to : to + rows, : 4 * rows] = block[:, : d // 2]
            fcg_ref[to + rows : to + 2 * rows, : 4 * rows] = block[:, d // 2 :]


def middle_kernel(d, count, place, *refs):
    grads = refs[:count]
    (after_ref, branch_ref, cot_ref, sel_ref, selt_ref, mod_ref, proj_ref) = refs[count : count + 7]
    ex_refs = refs[count + 7 : count + 15]
    (one_ref, modg_ref, pbias_ref, turned) = refs[count + 15 :]
    sel = sel_ref[:, : mod_ref.shape[1]]
    grad_in = grads[0][...].astype(F32)
    for ref in grads[1:]:
        grad_in = grad_in + ref[...].astype(F32)
    normed, inverse = normalize(after_ref[...])
    scale = mm(sel, mod_ref[4])
    gate = mm(sel, mod_ref[2])
    grad_one = cot_ref[...].astype(F32) + normalize_back(grad_in * (1.0 + scale), normed, inverse)
    one_ref[...] = grad_one
    modg_ref[...] = mm(selt_ref[...], (grad_one * branch_ref[...]).astype(BF))
    gb1 = (gate * grad_one).astype(BF)
    gb1_wide = gb1.astype(F32)
    pbias_ref[...] = jnp.sum(gb1_wide, axis=0, keepdims=True)
    width = d // 8
    turned[...] = gb1_wide.T
    grad_attn = mm(proj_ref[...], gb1, 1, 1)
    for slot, ref in enumerate(ex_refs):
        ref[0] = grad_attn[slot * width : (slot + 1) * width].astype(BF)
        ref[1] = turned[at_rows(place[AT_PART + slot], width)].astype(BF)


def back_kernel(d, width, columns, place, *refs):
    n = 8
    gas = refs[:n]
    (tok_near, tok_far, sel_ref, selt_ref, mod_ref, qkv_ref, w_ref, two_ref, gate_ref, pb_ref, f1b_ref, f2b_ref) = refs[n : n + 12]
    (gin_own, gin_far, gqkv_ref, in_ref, sum_ref) = refs[n + 12 : n + 17]
    (ga_all, modg, bias_row) = refs[n + 17 :]
    step = pl.program_id(0)
    size = sel_ref.shape[0] // 2

    @pl.when(step == 0)
    def _():
        bias_row[...] = jnp.zeros_like(bias_row)
        modg[...] = jnp.zeros_like(modg)
        for k, ref in enumerate(gas):
            ga_all[k] = ref[...]

    qkv = qkv_ref[:, : 3 * width]
    same = column_mask(size, columns)
    heads = width // HEAD_DIM
    halves = []
    for half in range(2):
        rows = slice(half * size, (half + 1) * size)
        grad_mixed = ga_all[2 * step + half, 0].astype(F32).T
        pieces = [None] * (3 * heads)
        for head in range(heads):
            q, k, v = (
                qkv[rows, t * width + head * HEAD_DIM : t * width + (head + 1) * HEAD_DIM]
                for t in range(3)
            )
            grad = grad_mixed[:, head * HEAD_DIM : (head + 1) * HEAD_DIM].astype(BF)
            prob = softmax_prob(q, k, same)
            grad_prob = mm(grad, v, 1, 1)
            delta = jnp.sum(prob * grad_prob, axis=-1, keepdims=True)
            grad_score = (prob * (grad_prob - delta) * SCORE_SCALE).astype(BF)
            pieces[head] = mm(grad_score, k)
            pieces[heads + head] = mm(grad_score, q, 0, 0)
            pieces[2 * heads + head] = mm(prob.astype(BF), grad, 0, 0)
        halves.append(jnp.concatenate(pieces, axis=1))
    grad_qkv = jnp.concatenate(halves, axis=0).astype(BF)
    bias_row[...] += jnp.sum(grad_qkv.astype(F32), axis=0, keepdims=True)

    tokens, _ = token_pair(tok_near, tok_far, size)
    normed, _ = normalize(tokens)
    sel = sel_ref[:, : mod_ref.shape[1]]
    selt = selt_ref[...]
    attn_in = (normed * (1.0 + mm(sel, mod_ref[1])) + mm(sel, mod_ref[0])).astype(BF)
    in_ref[...] = attn_in
    gqkv_ref[:, : 3 * width] = grad_qkv
    grad_in = mm(grad_qkv, w_ref[:, : 3 * width], 1, 1)
    modg[0] += mm(selt, grad_in.astype(BF))
    modg[1] += mm(selt, (grad_in * normed).astype(BF))
    near = step < pl.num_programs(0) // 2

    @pl.when(near)
    def _():
        gin_own[...] = grad_in.astype(BF).reshape(gin_own.shape)

    @pl.when(jnp.logical_not(near))
    def _():
        gin_far[...] = grad_in.astype(BF).reshape(gin_far.shape)

    @pl.when(step == pl.num_programs(0) - 1)
    def _():
        blocks = [modg[0], modg[1], gate_ref[...], two_ref[0], two_ref[1], two_ref[2]]
        for k, block in enumerate(blocks):
            for group in range(4):
                sum_ref[k * 4 + group] = block[group * 8 : (group + 1) * 8].astype(BF)
        part = place[AT_G]
        rows = [
            spread(bias_row[:, :width], part, 8),
            spread(bias_row[:, 2 * width :], part, 8),
            pb_ref[...],
        ]
        at = place[AT_Y] * 4 + place[AT_F]
        rows += [spread(f1b_ref[:, z * width : (z + 1) * width], at, 8) for z in range(4)]
        rows.append(jnp.where(part == 0, f2b_ref[...], 0.0))
        sum_ref[24] = jnp.concatenate(rows, axis=0).astype(BF)
        for k in range(25, 32):
            sum_ref[k] = jnp.zeros(sum_ref.shape[1:], BF)


def weights_kernel(d, width, order, place, *refs):
    n = len(order)
    slots, gas = refs[:n], refs[n : 2 * n]
    (gqkv_ref, in_ref, grad_ref, qkva, proja, ga_all) = refs[2 * n :]
    step = pl.program_id(0)
    size = in_ref.shape[0] // 2

    @pl.when(step == 0)
    def _():
        qkva[...] = jnp.zeros_like(qkva)
        proja[...] = jnp.zeros_like(proja)
        for k, ref in enumerate(gas):
            ga_all[k] = ref[1]

    qkva[...] += mm(in_ref[...], gqkv_ref[:, : 3 * width], 0, 0)
    attn_t = slab_attention(slots, order, size)
    gb1_t = jnp.concatenate([ga_all[2 * step], ga_all[2 * step + 1]], axis=1)
    proja[...] += mm(attn_t, gb1_t, 1, 1)

    @pl.when(step == pl.num_programs(0) - 1)
    def _():
        grad_ref[:, : 3 * width] = qkva[...].astype(BF)
        grad_ref[:, 4 * width :] = jnp.zeros((d, grad_ref.shape[1] - 4 * width), BF)
        for slot in range(n):
            grad_ref[at_rows(place[AT_PART + slot], width), 3 * width : 4 * width] = proja[slot * width : (slot + 1) * width].astype(BF)


def ada_kernel(d, place, total_ref, act_ref, slope_ref, w_ref, wg_ref, cond_ref, ada_ref, qkv_ref, proj_ref, fc1_ref, fc2_ref):
    rows = wg_ref.shape[0]
    act = act_ref[:, :rows]
    cond = jnp.zeros(cond_ref.shape, F32)
    sums = []
    for block in range(6):
        grads = jnp.concatenate([chunk_of(total_ref, place, block * 4 + k).astype(F32) for k in range(4)], axis=0)
        cols = slice(block * d, (block + 1) * d)
        sums.append(jnp.sum(grads, axis=0, keepdims=True))
        grads = grads.astype(BF)
        wg_ref[:, cols] = mm(act, grads, 0, 0)
        cond = cond + mm(grads, w_ref[:, cols], 1, 1)
    cond_ref[...] = cond * slope_ref[:, :rows]
    put_row(ada_ref, jnp.concatenate(sums, axis=1))
    biases = chunk_of(total_ref, place, 24).astype(F32)
    rows = [biases[k : k + 1] for k in range(8)]
    put_row(qkv_ref, jnp.concatenate(rows[:2], axis=1))
    put_row(proj_ref, rows[2])
    put_row(fc1_ref, jnp.concatenate(rows[3:7], axis=1))
    put_row(fc2_ref, rows[7])


def mlp_split_kernel(rows, place, in_ref, *outs):
    cols = 2 * rows
    outs, full = outs[:8], outs[8]
    full[...] = jnp.zeros_like(full)
    for f in range(4):
        for y in range(2):
            slot = place[AT_SLOT + f * 2 + y]
            full[slot, :, :rows] = in_ref[y * rows : (y + 1) * rows, f * rows : (f + 1) * rows]
            part = in_ref[(2 + f // 2) * rows : (3 + f // 2) * rows, f % 2 * cols : (f % 2 + 1) * cols]
            full[slot, :, rows : 3 * rows] = jnp.where(place[AT_Y] == y, part.astype(F32), 0.0).astype(BF)
    for slot, out in enumerate(outs):
        out[...] = full[slot, :, : out.shape[1]]


def collect(full, refs):
    for slot, ref in enumerate(refs):
        full[slot, :, : ref.shape[1]] = ref[...]


def mlp_join_kernel(rows, place, *refs):
    (fc1_ref, fc2_ref, full) = refs[8:]
    collect(full, refs[:8])
    for f in range(4):
        for y in range(2):
            at = (y * 4 + f) * rows
            fc1_ref[:, at : at + rows] = full[place[AT_SLOT + f * 2 + y], :, :rows].astype(F32)
        fc2_ref[:, f * rows : (f + 1) * rows] = full[place[AT_SLOT + f * 2 + place[AT_Y]], :, rows : 3 * rows].astype(F32).T


def attn_split_kernel(rows, place, in_ref, *outs):
    outs, full = outs[:8], outs[8]
    full[...] = jnp.zeros_like(full)
    for part in range(8):

        @pl.when(place[AT_G] == part)
        def _():
            for y in range(2):
                block = in_ref[y * rows : (y + 1) * rows]
                for t in range(3):
                    to = (8 * t + part) // 6
                    full[place[AT_SLOT + to * 2 + y], :, :rows] = block[:, t * rows : (t + 1) * rows]
                full[place[AT_SLOT + part // 2 * 2 + y], :, rows : 2 * rows] = block[:, 3 * rows : 4 * rows]

    for slot, out in enumerate(outs):
        out[...] = full[slot, :, : out.shape[1]]


def attn_join_kernel(rows, place, *refs):
    (qkv_ref, proj_ref, full) = refs[8:]
    collect(full, refs[:8])
    for y in range(2):
        proj_ref[:, y * rows : (y + 1) * rows] = full[place[AT_SLOT + place[AT_F] * 2 + y], :, rows : 2 * rows].astype(F32)
    for to in range(4):

        @pl.when(place[AT_F] == to)
        def _():
            for k in range(6):
                slot = place[AT_SLOT + (6 * to + k) % 8]
                qkv_ref[:, k * rows : (k + 1) * rows] = full[slot, :, :rows].astype(F32)


def output_kernel(place, b2_0, b2_1, b2_2, b2_3, tok_ref, after_ref, mask_ref, sel_ref, mod_ref, out_ref):
    branch = b2_0[...].astype(F32)
    for ref in (b2_1, b2_2, b2_3):
        branch = branch + ref[...].astype(F32)
    gate = mm(sel_ref[:, : mod_ref.shape[1]], mod_ref[5])
    tokens = tok_ref[...].astype(F32)
    out_ref[...] = jnp.where(mask_ref[...] == 1, tokens, after_ref[...] + gate * branch).astype(BF)


def input_grad_kernel(place, gin_0, gin_1, gin_2, gin_3, tok_ref, one_ref, cot_ref, mask_ref, sel_ref, mod_ref, grad_ref):
    grad_in = gin_0[...].astype(F32)
    for ref in (gin_1, gin_2, gin_3):
        grad_in = grad_in + ref[...].astype(F32)
    normed, inverse = normalize(tok_ref[...].astype(F32))
    scale = mm(sel_ref[:, : mod_ref.shape[1]], mod_ref[1])
    back = normalize_back(grad_in * (1.0 + scale), normed, inverse)
    grad_ref[...] = jnp.where(mask_ref[...] == 1, cot_ref[...].astype(F32), 0.0) + one_ref[...] + back


def slab_solution(mesh):
    names = ("x", "core", "z", "y")
    grid = Mesh(mesh.devices.reshape(2, 2, 4, 2), names)
    offsets = [(dc, dx, dy) for dc in range(2) for dx in range(2) for dy in range(2)]
    order = [dy == 1 for _, _, dy in offsets]
    group = ("x", "core", "y")
    table = [[0] * TABLE for _ in range(32)]
    for device, row in enumerate(table):
        x, c, z, y = device >> 4, (device >> 3) & 1, (device >> 1) & 3, device & 1
        f = x * 2 + c
        row[AT_F], row[AT_Y], row[AT_Z], row[AT_P], row[AT_G] = f, y, z, device & 7, f * 2 + y
        for slot, (dc, dx, dy) in enumerate(offsets):
            part = ((x ^ dx) * 2 + (c ^ dc)) * 2 + (y ^ dy)
            row[AT_PART + slot] = part
            row[AT_SLOT + part] = slot
        for piece in range(8):
            row[AT_SHARD + piece] = (z ^ (piece >> 1)) * 2 + (y ^ (piece & 1))
        for patch in range(8):
            row[AT_PIECE + patch] = ((patch & 1) ^ y) * 4 + (patch >> 1)

    def swap(a, axes):
        n = 2 ** len(axes)
        return lax.ppermute(a, axes, [(k, n - 1 - k) for k in range(n)])

    def from_z(a, apart):
        return lax.ppermute(a, ("z",), [(z, z ^ apart) for z in range(4)])

    def over(a, dx, dy):
        axes = (("x",) if dx else ()) + (("y",) if dy else ())
        return swap(a, axes) if axes else a

    def gather_near(a):
        return [over(a, dx, dy) for dx in range(2) for dy in range(2)]

    def gather_slots(a):
        mine = gather_near(a)
        return mine + [swap(piece, ("core",)) for piece in mine]

    def over_z(a):
        return [a] + [from_z(a, apart) for apart in (1, 2, 3)]

    def to_slab(a):
        return lax.all_to_all(jnp.broadcast_to(a, (8, *a.shape)), group, 0, 0, tiled=True)

    def core_sum(own, far):
        received = swap(far, ("core",))
        return [(own[slot].astype(F32) + received[slot].astype(F32)).astype(BF) for slot in range(4)]

    def scatter_sum(own, far):
        return [over(total, slot // 2, slot % 2) for slot, total in enumerate(core_sum(own, far))]

    def exchange(slots):
        moved = []
        for slot, offset in zip(slots, offsets):
            axes = tuple(axis for axis, apart in zip(("x", "core", "y"), (offset[1], offset[0], offset[2])) if apart)
            moved.append(swap(slot, axes) if axes else slot)
        return moved

    def local(tokens, image_mask, sample_index, condition, ada_weight, ada_bias, qkv_weight, qkv_bias,
              proj_weight, proj_bias, fc1_weight, fc1_bias, fc2_weight, fc2_bias, cotangent):
        frames, columns, d = tokens.shape
        T = frames * columns
        S = 8 * T
        TB = 2 * T
        samples = condition.shape[0]
        rows = ada_weight.shape[0]
        ff = fc1_weight.shape[1]
        width = d // 8
        part_ff = ff // 8
        cols = 2 * width
        me = lax.axis_index(names).astype(jnp.uint32)
        place = lax.dynamic_slice(jnp.array(table, jnp.int32), (me, jnp.uint32(0)), (1, TABLE)).reshape(TABLE)

        def shaped(shape, dtype=F32):
            return jax.ShapeDtypeStruct(shape, dtype)

        def rows_at(w):
            return pl.BlockSpec((TB, w), lambda j, *_: (j, 0))

        def lanes_at(h):
            return pl.BlockSpec((h, TB), lambda j, *_: (0, j))

        token_specs = [
            pl.BlockSpec((2, 2 * T + 16, d), lambda j, *_: (jnp.minimum(j, 1), 0, 0)),
            pl.BlockSpec((2, 2 * T + 16, d), lambda j, *_: (jnp.maximum(j - 2, 0), 0, 0)),
        ]

        def call(name, us, kernel, arrays, outs, steps=1, ins=None, specs=None, scratch=()):
            return pl.pallas_call(
                kernel,
                grid_spec=pltpu.PrefetchScalarGridSpec(
                    num_scalar_prefetch=1,
                    grid=(steps,),
                    in_specs=ins or [whole(array.shape) for array in arrays],
                    out_specs=specs or [whole(out.shape) for out in outs],
                    scratch_shapes=list(scratch),
                ),
                out_shape=outs,
                compiler_params=params(),
                cost_estimate=takes(us),
                name=name,
            )(place, *arrays)

        def lines(bias):
            return bias.reshape(-1, 128)

        flat_tokens = tokens.reshape(T, d)
        flat_cot = cotangent.reshape(T, d)
        mask = image_mask.reshape(T, 1)

        (partial_mod, act_rows, silu_slope, qkv_mine, fc1_mine, send, fc2_rows, slab_rows) = call(
            "prepare",
            6,
            functools.partial(prepare_kernel, d),
            [condition, ada_weight, qkv_weight, fc1_weight, proj_weight, fc2_weight, flat_tokens, flat_cot, sample_index.T, image_mask.T],
            [
                shaped((8, 8, d), BF),
                shaped((samples, wide(rows)), BF),
                shaped((samples, wide(rows))),
                shaped((rows, wide(3 * width)), BF),
                shaped((rows, wide(part_ff)), BF),
                shaped((rows, wide(part_ff) + wide(3 * width)), BF),
                shaped((rows, wide(d + cols)), BF),
                shaped((2 * T + 16, d), BF),
            ],
            scratch=[pltpu.VMEM((samples, rows), F32)],
        )

        fc2_in = lax.all_gather(fc2_rows, "z", axis=0)
        mod_terms = lax.all_to_all(partial_mod, ("z", "y"), 0, 0, tiled=True)
        got = swap(send, ("y",))
        qkv_pair = jnp.stack([qkv_mine, got[:, wide(part_ff) :]])
        fc1_pair = jnp.stack([fc1_mine, got[:, : wide(part_ff)]])
        mod_terms, qkv_pair, fc1_pair, slab_rows = lax.optimization_barrier((mod_terms, qkv_pair, fc1_pair, slab_rows))
        qkv_pair, fc2_in = lax.optimization_barrier((qkv_pair, fc2_in))
        qkv_in = lax.all_gather(qkv_pair, "z", axis=0)
        (mod_chunk,) = call(
            "mod_sum",
            2,
            mod_sum_kernel,
            [mod_terms, lines(ada_bias)],
            [shaped((8, d), BF)],
        )
        chunks = over_z(mod_chunk)
        tok_mine = gather_near(slab_rows)
        chunks, tok_mine = lax.optimization_barrier((chunks, tok_mine))
        mod_in = to_slab(jnp.stack(chunks))
        tok_near = jnp.stack(tok_mine)
        tok_far = swap(tok_near, ("core",))
        proj_slots = gather_slots(fc2_in[:, :, d : d + cols])
        (proj_all,) = call(
            "proj",
            3,
            functools.partial(proj_kernel, d),
            proj_slots,
            [shaped((d, d), BF)],
            scratch=[pltpu.VMEM((8, 4, rows, cols), BF)],
        )
        mod_in, tok_near, tok_far, qkv_in, fc1_pair, proj_all = lax.optimization_barrier(
            (mod_in, tok_near, tok_far, qkv_in, fc1_pair, proj_all)
        )
        fc1_in = lax.all_gather(fc1_pair, "z", axis=0)
        attn_t, qkv, sel, selt, w_qkv, mod = call(
            "attend",
            13,
            functools.partial(attend_kernel, d, width, columns),
            [tok_near, tok_far, qkv_in, mod_in, lines(qkv_bias)],
            [
                shaped((width, S), BF),
                shaped((S, wide(3 * width)), BF),
                shaped((S, 128), BF),
                shaped((samples, S), BF),
                shaped((d, wide(3 * width)), BF),
                shaped((6, samples, d), BF),
            ],
            steps=4,
            ins=token_specs
            + [whole(array.shape) for array in (qkv_in, mod_in, lines(qkv_bias))],
            specs=[
                lanes_at(width),
                rows_at(wide(3 * width)),
                rows_at(128),
                lanes_at(samples),
                whole((d, wide(3 * width))),
                whole((6, samples, d)),
            ],
            scratch=[pltpu.VMEM((1, 3 * width), F32)],
        )
        attn_slots = gather_slots(attn_t)

        def slot_spec(dc, dx):
            return pl.BlockSpec((width, TB), lambda j, *_: (0, lax.bitwise_xor(j, dc * 2 + dx)))

        slot_specs = [slot_spec(dc, dx) for dc, dx, _ in offsets]
        own_out = pl.BlockSpec((2, T, d), lambda j, *_: (jnp.minimum(j, 1), 0, 0))
        far_out = pl.BlockSpec((2, T, d), lambda j, *_: (jnp.maximum(j - 2, 0), 0, 0))
        half_shape = shaped((4, T, d), BF)

        mlp_rest = [mod, proj_all, lines(proj_bias), fc1_in, lines(fc1_bias), fc2_in, lines(fc2_bias)]
        (b2_own, b2_far, gm_own, gm_far, fcg, fc1_bias_g, fc2_bias_g, modg_two, after_own, branch_own) = call(
            "mlp",
            32,
            functools.partial(mlp_kernel, d, order),
            [*attn_slots, tok_near, tok_far, sel, selt, *mlp_rest],
            [
                half_shape,
                half_shape,
                half_shape,
                half_shape,
                shaped((16 * rows, wide(part_ff)), BF),
                shaped((1, part_ff)),
                shaped((1, d)),
                shaped((3, samples, d)),
                shaped((T, d)),
                shaped((T, d)),
            ],
            steps=4,
            ins=slot_specs
            + token_specs
            + [rows_at(128), lanes_at(samples)]
            + [whole(array.shape) for array in mlp_rest],
            specs=[
                own_out,
                far_out,
                own_out,
                far_out,
                whole((16 * rows, wide(part_ff))),
                whole((1, part_ff)),
                whole((1, d)),
                whole((3, samples, d)),
                whole((T, d)),
                whole((T, d)),
            ],
            scratch=[
                pltpu.VMEM((d, part_ff), F32),
                pltpu.VMEM((part_ff, d), F32),
                pltpu.VMEM((d, part_ff), BF),
                pltpu.VMEM((part_ff, d), BF),
                pltpu.VMEM((1, d), F32),
                pltpu.VMEM((1, part_ff), F32),
                pltpu.VMEM((1, d), F32),
            ],
        )

        fc_z = lax.psum_scatter(fcg, "z", scatter_dimension=0, tiled=True)
        gm_terms = scatter_sum(gm_own, gm_far)

        *ex_slots, grad_one, modg_gate, proj_bias_g = call(
            "middle",
            6,
            functools.partial(middle_kernel, d, len(gm_terms)),
            [*gm_terms, after_own, branch_own, slab_rows, sel, selt, mod, proj_all],
            [shaped((2, width, T), BF)] * 8 + [shaped((T, d)), shaped((samples, d)), shaped((1, d))],
            ins=[whole((T, d))] * (len(gm_terms) + 3)
            + [whole((T, 128)), whole((samples, T)), whole(mod.shape), whole((d, d))],
            scratch=[pltpu.VMEM((d, T), F32)],
        )
        grad_attn = exchange(ex_slots)
        b2_sums = core_sum(b2_own, b2_far)
        grad_attn, b2_sums = lax.optimization_barrier((grad_attn, b2_sums))
        b2_terms = [over(total, slot // 2, slot % 2) for slot, total in enumerate(b2_sums)]

        back_rest = [w_qkv, modg_two, modg_gate, proj_bias_g, fc1_bias_g, fc2_bias_g]
        gin_own, gin_far, grad_qkv, attn_in, to_sum = call(
            "back",
            22,
            functools.partial(back_kernel, d, width, columns),
            [*grad_attn, tok_near, tok_far, sel, selt, mod, qkv, *back_rest],
            [half_shape, half_shape, shaped((S, wide(3 * width)), BF), shaped((S, d), BF), shaped((32, 8, d), BF)],
            steps=4,
            ins=[whole((2, width, T))] * 8
            + token_specs
            + [rows_at(128), lanes_at(samples), whole(mod.shape), rows_at(wide(3 * width))]
            + [whole(array.shape) for array in back_rest],
            specs=[own_out, far_out, rows_at(wide(3 * width)), rows_at(d), whole((32, 8, d))],
            scratch=[
                pltpu.VMEM((8, 2, width, T), BF),
                pltpu.VMEM((2, samples, d), F32),
                pltpu.VMEM((1, 3 * width), F32),
            ],
        )
        gin_own, gin_far, grad_qkv, attn_in, to_sum, b2_terms = lax.optimization_barrier(
            (gin_own, gin_far, grad_qkv, attn_in, to_sum, b2_terms)
        )
        (attn_g,) = call(
            "weights",
            8,
            functools.partial(weights_kernel, d, width, order),
            [*attn_slots, *grad_attn, grad_qkv, attn_in],
            [shaped((d, wide(4 * width)), BF)],
            steps=4,
            ins=slot_specs + [whole((2, width, T))] * 8 + [rows_at(wide(3 * width)), rows_at(d)],
            specs=[whole((d, wide(4 * width)))],
            scratch=[
                pltpu.VMEM((d, 3 * width), F32),
                pltpu.VMEM((d, width), F32),
                pltpu.VMEM((8, width, T), BF),
            ],
        )
        terms = lax.all_to_all(to_sum, names, 0, 0, tiled=True)
        own_specs = [whole((T, 1)), whole((T, 128)), whole(mod.shape)]
        (result,) = call(
            "output",
            3,
            output_kernel,
            [*b2_terms, flat_tokens, after_own, mask, sel, mod],
            [shaped((T, d), BF)],
            ins=[whole((T, d))] * 6 + own_specs,
        )
        def split(name, kernel, summed, lanes):
            return call(
                name,
                3,
                functools.partial(kernel, rows),
                [summed],
                [shaped((rows, n), BF) for n in lanes],
                scratch=[pltpu.VMEM((8, rows, max(lanes)), BF)],
            )

        def join(name, kernel, pieces, outs):
            return call(
                name,
                3,
                functools.partial(kernel, rows),
                pieces,
                outs,
                scratch=[pltpu.VMEM((8, rows, max(piece.shape[1] for piece in pieces)), BF)],
            )

        attn_g, fc_z, terms, result = lax.optimization_barrier((attn_g, fc_z, terms, result))
        attn_z = lax.psum_scatter(attn_g, "z", scatter_dimension=0, tiled=True)
        gin_terms = scatter_sum(gin_own, gin_far)

        (sums,) = call("grad_sum", 2, grad_sum_kernel, [terms], [shaped((8, d), BF)])
        total = to_slab(jnp.stack(over_z(sums)))

        (ada_weight_grad, condition_grad, ada_bias_grad, qkv_bias_grad, proj_bias_grad, fc1_bias_grad, fc2_bias_grad) = call(
            "ada",
            5,
            functools.partial(ada_kernel, d),
            [total, act_rows, silu_slope, ada_weight],
            [shaped((rows, 6 * d)), shaped((samples, rows))]
            + [shaped((n // 128, 128)) for n in (6 * d, 2 * d, d, ff, d)],
        )

        mlp_send = split("mlp_split", mlp_split_kernel, fc_z, [wide(rows if dy else 3 * rows) for _, _, dy in offsets])
        mlp_got = exchange(mlp_send)
        attn_z, ada_weight_grad = lax.optimization_barrier((attn_z, ada_weight_grad))
        attn_send = split("attn_split", attn_split_kernel, attn_z, [wide(rows if dc or dx else 2 * rows) for dc, dx, _ in offsets])
        attn_got = exchange(attn_send)
        gin_terms = lax.optimization_barrier((gin_terms, attn_send[0]))[0]
        mlp_got = lax.optimization_barrier((mlp_got, attn_send[0]))[0]
        fc1_weight_grad, fc2_weight_grad = join(
            "mlp_join", mlp_join_kernel, mlp_got, [shaped((rows, ff // 4)), shaped((d // 4, 4 * rows))]
        )
        (input_grad,) = call(
            "input_grad",
            3,
            input_grad_kernel,
            [*gin_terms, flat_tokens, grad_one, flat_cot, mask, sel, mod],
            [shaped((T, d))],
            ins=[whole((T, d))] * 7 + own_specs,
        )

        qkv_weight_grad, proj_weight_grad = join(
            "attn_join", attn_join_kernel, attn_got, [shaped((rows, 3 * d // 4)), shaped((rows, d // 4))]
        )

        shape = (frames, columns, d)
        return (
            result.reshape(shape),
            input_grad.reshape(shape),
            condition_grad,
            ada_weight_grad,
            ada_bias_grad.reshape(-1),
            qkv_weight_grad,
            qkv_bias_grad.reshape(-1),
            proj_weight_grad,
            proj_bias_grad.reshape(-1),
            fc1_weight_grad,
            fc1_bias_grad.reshape(-1),
            fc2_weight_grad.T,
            fc2_bias_grad.reshape(-1),
        )

    frame, patch = ("x", "core"), ("z", "y")
    token_spec, number_spec = P(None, names, None), P(None, names)
    row_spec, both_spec = P(patch, None), P(patch, frame)
    return jax.shard_map(
        local,
        mesh=grid,
        in_specs=(
            token_spec, number_spec, number_spec, P(), row_spec, P(), row_spec, P(), row_spec, P(), row_spec, P(),
            row_spec, P(), token_spec,
        ),
        out_specs=(
            token_spec, token_spec, P(None, patch), row_spec, P(), both_spec, P(), both_spec, P(), both_spec, P(),
            both_spec, P(),
        ),
        check_vma=False,
    )


def solution(mesh):
    if (mesh.shape["frame"], mesh.shape["patch"]) == (4, 8):
        return slab_solution(mesh)
    return general_solution(mesh)
```

```python
import functools

import jax
import jax.numpy as jnp
from jax import lax
from jax.experimental import pallas as pl
from jax.experimental.pallas import tpu as pltpu
from jax.sharding import Mesh, PartitionSpec as P

HEAD_DIM = 72
EPSILON = 1e-06
SCORE_SCALE = HEAD_DIM**-0.5
GELU_C = 0.7978845608028654
GELU_A = 0.044715
VMEM_BYTES = 56 * 1024 * 1024
(AT_F, AT_Y, AT_Z, AT_P, AT_G) = range(5)
AT_PART, AT_SLOT, AT_SHARD, AT_PIECE, TABLE = 8, 16, 24, 32, 40
BF = jnp.bfloat16
F32 = jnp.float32


def mm(a, b, ca=1, cb=0):
    return lax.dot_general(a, b, (((ca,), (cb,)), ((), ())), preferred_element_type=F32)


def normalize(values):
    centred = values - jnp.mean(values, axis=-1, keepdims=True)
    inverse = lax.rsqrt(jnp.mean(centred * centred, axis=-1, keepdims=True) + EPSILON)
    return centred * inverse, inverse


def normalize_back(grad_normed, normed, inverse):
    return inverse * (
        grad_normed
        - jnp.mean(grad_normed, axis=-1, keepdims=True)
        - normed * jnp.mean(grad_normed * normed, axis=-1, keepdims=True)
    )


def stack_rows(pieces):
    if pieces[0].shape[0] % 16 == 0:
        return jnp.concatenate(pieces, axis=0)
    return jnp.concatenate([piece.astype(F32) for piece in pieces], axis=0).astype(pieces[0].dtype)


def softmax_prob(queries, key_rows, same_column):
    grid = mm(queries, key_rows, 1, 1) * SCORE_SCALE
    grid = jnp.where(same_column, grid, -1e30)
    expanded = jnp.exp(grid - jnp.max(grid, axis=-1, keepdims=True))
    return expanded / jnp.sum(expanded, axis=-1, keepdims=True)


def column_mask(tokens_per_part, columns):
    rows = lax.broadcasted_iota(jnp.int32, (tokens_per_part, tokens_per_part), 0)
    cols = lax.broadcasted_iota(jnp.int32, (tokens_per_part, tokens_per_part), 1)
    return lax.rem(rows, columns) == lax.rem(cols, columns)


def slab_attention(refs, order, size):
    pieces = []
    for ref, swapped in zip(refs, order):
        piece = ref[...]
        if swapped:
            piece = jnp.concatenate([piece[:, size:], piece[:, :size]], axis=1)
        pieces.append(piece)
    return stack_rows(pieces)


def general_attend_kernel(d, width, columns, tok_ref, sel_ref, mod_ref, w_ref, bias_ref, out_ref, qkv_ref):
    normed, _ = normalize(tok_ref[...].astype(F32))
    sel = sel_ref[...]
    shift = mm(sel, mod_ref[:, 0:d])
    scale = mm(sel, mod_ref[:, d : 2 * d])
    attn_in = (normed * (1.0 + scale) + shift).astype(BF)
    qkv = (mm(attn_in, w_ref[...]) + bias_ref[...]).astype(BF)
    qkv_ref[...] = qkv
    size = tok_ref.shape[0] // 2
    same = column_mask(size, columns)
    for half in range(2):
        rows = slice(half * size, (half + 1) * size)
        parts = []
        for head in range(width // HEAD_DIM):
            q, k, v = (
                qkv[rows, t * width + head * HEAD_DIM : t * width + (head + 1) * HEAD_DIM]
                for t in range(3)
            )
            prob = softmax_prob(q, k, same)
            parts.append(mm(prob.astype(BF), v).T)
        out_ref[:, rows] = jnp.concatenate(parts, axis=0).astype(BF)


def general_mlp_kernel(d, order, *refs):
    n = len(order)
    slots = refs[:n]
    (tok_ref, cot_ref, sel_ref, selt_ref, mod_ref, proj_ref, projb_ref, fc1_ref, fc1b_ref, fc2_ref, fc2b_ref) = refs[n : n + 11]
    (b2_ref, gm_ref, fc1g_ref, fc2g_ref, fc1bg_ref, fc2bg_ref, modg_ref, after_ref, branch_ref, fc1a, fc2a) = refs[n + 11 :]
    step = pl.program_id(0)
    size = tok_ref.shape[0] // 2
    sel = sel_ref[...]
    selt = selt_ref[...]

    def mod(block):
        return mm(sel, mod_ref[:, block * d : (block + 1) * d])

    attn_t = slab_attention(slots, order, size)
    branch_one = mm(attn_t, proj_ref[...], 0, 0) + projb_ref[...]
    after_one = tok_ref[...].astype(F32) + mod(2) * branch_one

    @pl.when(step == 0)
    def _():
        after_ref[...] = after_one[:size]
        branch_ref[...] = branch_one[:size]
        fc1a[...] = jnp.zeros_like(fc1a)
        fc2a[...] = jnp.zeros_like(fc2a)
        fc1bg_ref[...] = jnp.zeros_like(fc1bg_ref)
        fc2bg_ref[...] = jnp.zeros_like(fc2bg_ref)
        modg_ref[...] = jnp.zeros_like(modg_ref)

    normed, _ = normalize(after_one)
    mlp_in = (normed * (1.0 + mod(4)) + mod(3)).astype(BF)
    pre = mm(mlp_in, fc1_ref[...]) + fc1b_ref[...]
    square = pre * pre
    tanh = jnp.tanh(GELU_C * pre * (1.0 + GELU_A * square))
    hidden = (0.5 * pre * (1.0 + tanh)).astype(BF)
    slope = 0.5 * (1.0 + tanh) + 0.5 * pre * (1.0 - tanh * tanh) * GELU_C * (1.0 + 3.0 * GELU_A * square)
    branch_two = mm(hidden, fc2_ref[...]) + fc2b_ref[...]
    b2_ref[...] = branch_two.astype(BF).reshape(b2_ref.shape)
    grad_two = cot_ref[...].astype(F32)
    grad_branch = mod(5) * grad_two
    gb2 = grad_branch.astype(BF)
    fc2bg_ref[...] += jnp.sum(gb2.astype(F32), axis=0, keepdims=True)
    fc2a[...] += mm(hidden, gb2, 0, 0)
    grad_pre = (mm(gb2, fc2_ref[...], 1, 1) * slope).astype(BF)
    fc1bg_ref[...] += jnp.sum(grad_pre.astype(F32), axis=0, keepdims=True)
    fc1a[...] += mm(mlp_in, grad_pre, 0, 0)
    grad_in = mm(grad_pre, fc1_ref[...], 1, 1)
    gm_ref[...] = grad_in.astype(BF).reshape(gm_ref.shape)
    modg_ref[0] += mm(selt, grad_in.astype(BF))
    modg_ref[1] += mm(selt, (grad_in * normed).astype(BF))
    modg_ref[2] += mm(selt, (grad_two * branch_two).astype(BF))

    @pl.when(step == pl.num_programs(0) - 1)
    def _():
        fc1g_ref[...] = fc1a[...].astype(BF)
        fc2g_ref[...] = fc2a[...].astype(BF)


def general_middle_kernel(d, n_parts, count, place_ref, *refs):
    grads = refs[:count]
    (after_ref, branch_ref, cot_ref, sel_ref, selt_ref, mod_ref, proj_ref) = refs[count : count + 7]
    (ex_ref, one_ref, modg_ref, pbias_ref) = refs[count + 7 :]
    sel = sel_ref[...]
    grad_in = grads[0][...].astype(F32)
    for ref in grads[1:]:
        grad_in = grad_in + ref[...].astype(F32)
    normed, inverse = normalize(after_ref[...])
    scale = mm(sel, mod_ref[:, 4 * d : 5 * d])
    gate = mm(sel, mod_ref[:, 2 * d : 3 * d])
    grad_one = cot_ref[...].astype(F32) + normalize_back(grad_in * (1.0 + scale), normed, inverse)
    one_ref[...] = grad_one
    modg_ref[...] = mm(selt_ref[...], (grad_one * branch_ref[...]).astype(BF))
    gb1 = (gate * grad_one).astype(BF)
    gb1_wide = gb1.astype(F32)
    pbias_ref[...] = jnp.sum(gb1_wide, axis=0, keepdims=True)
    width = d // n_parts
    grad_attn = mm(proj_ref[...], gb1, 1, 1)
    gb1_t = gb1_wide.T
    for part in range(n_parts):
        rows = slice(part * width, (part + 1) * width)
        ex_ref[part, 0] = grad_attn[rows].astype(BF)
        ex_ref[place_ref[part], 1] = gb1_t[rows].astype(BF)


def general_attend_back_kernel(d, width, columns, order, place_ref, *refs):
    n = len(order)
    slots = refs[:n]
    (ga_ref, tok_ref, sel_ref, selt_ref, mod_ref, w_ref, qkv_ref) = refs[n : n + 7]
    (gin_ref, qkvg_ref, projg_ref, bias_ref, modg_ref, qkva, proja) = refs[n + 7 :]
    step = pl.program_id(0)
    size = tok_ref.shape[0] // 2

    @pl.when(step == 0)
    def _():
        qkva[...] = jnp.zeros_like(qkva)
        proja[...] = jnp.zeros_like(proja)
        bias_ref[...] = jnp.zeros_like(bias_ref)
        modg_ref[...] = jnp.zeros_like(modg_ref)

    qkv = qkv_ref[...]
    same = column_mask(size, columns)
    heads = width // HEAD_DIM
    halves = []
    for half in range(2):
        rows = slice(half * size, (half + 1) * size)
        grad_mixed = ga_ref[half, 0].astype(F32).T
        pieces = [None] * (3 * heads)
        for head in range(heads):
            q, k, v = (
                qkv[rows, t * width + head * HEAD_DIM : t * width + (head + 1) * HEAD_DIM]
                for t in range(3)
            )
            grad = grad_mixed[:, head * HEAD_DIM : (head + 1) * HEAD_DIM].astype(BF)
            prob = softmax_prob(q, k, same)
            grad_prob = mm(grad, v, 1, 1)
            delta = jnp.sum(prob * grad_prob, axis=-1, keepdims=True)
            grad_score = (prob * (grad_prob - delta) * SCORE_SCALE).astype(BF)
            pieces[head] = mm(grad_score, k)
            pieces[heads + head] = mm(grad_score, q, 0, 0)
            pieces[2 * heads + head] = mm(prob.astype(BF), grad, 0, 0)
        halves.append(jnp.concatenate(pieces, axis=1))
    grad_qkv = jnp.concatenate(halves, axis=0).astype(BF)
    bias_ref[...] += jnp.sum(grad_qkv.astype(F32), axis=0, keepdims=True)

    sel = sel_ref[...]
    selt = selt_ref[...]
    normed, _ = normalize(tok_ref[...].astype(F32))
    shift = mm(sel, mod_ref[:, 0:d])
    scale = mm(sel, mod_ref[:, d : 2 * d])
    attn_in = (normed * (1.0 + scale) + shift).astype(BF)
    qkva[...] += mm(attn_in, grad_qkv, 0, 0)
    grad_in = mm(grad_qkv, w_ref[...], 1, 1)
    gin_ref[...] = grad_in.astype(BF).reshape(gin_ref.shape)
    modg_ref[0] += mm(selt, grad_in.astype(BF))
    modg_ref[1] += mm(selt, (grad_in * normed).astype(BF))

    attn_t = slab_attention(slots, order, size)
    gb1_t = jnp.concatenate([ga_ref[0, 1], ga_ref[1, 1]], axis=1)
    proja[...] += mm(attn_t, gb1_t, 1, 1)

    @pl.when(step == pl.num_programs(0) - 1)
    def _():
        qkvg_ref[...] = qkva[...].astype(BF)
        rows = d // n
        for part in range(n):
            projg_ref[place_ref[part]] = proja[part * rows : (part + 1) * rows].astype(BF)


def general_last_kernel(d, count, count_b, *refs):
    grads = refs[:count]
    branches = refs[count : count + count_b]
    (tok_ref, one_ref, after_ref, cot_ref, mask_ref, sel_ref, mod_ref) = refs[count + count_b : count + count_b + 7]
    (out_ref, grad_ref) = refs[count + count_b + 7 :]
    sel = sel_ref[...]
    masked = mask_ref[...] == 1
    tokens = tok_ref[...].astype(F32)
    grad_in = grads[0][...].astype(F32)
    for ref in grads[1:]:
        grad_in = grad_in + ref[...].astype(F32)
    normed, inverse = normalize(tokens)
    scale = mm(sel, mod_ref[:, d : 2 * d])
    back = normalize_back(grad_in * (1.0 + scale), normed, inverse)
    grad_ref[...] = jnp.where(masked, cot_ref[...].astype(F32), 0.0) + one_ref[...] + back
    branch = branches[0][...].astype(F32)
    for ref in branches[1:]:
        branch = branch + ref[...].astype(F32)
    gate = mm(sel, mod_ref[:, 5 * d : 6 * d])
    out_ref[...] = jnp.where(masked, tokens, after_ref[...] + gate * branch).astype(BF)


def params(steps=1):
    return pltpu.CompilerParams(vmem_limit_bytes=VMEM_BYTES, dimension_semantics=("arbitrary",) * steps)


def cost(flops, bytes_accessed):
    return pl.CostEstimate(flops=int(flops), bytes_accessed=int(bytes_accessed), transcendentals=0)


def whole(shape):
    return pl.BlockSpec(shape, lambda *_: (0,) * len(shape))


def matchings(frames):
    left = {f: {t: (frames * t + f) // 3 for t in range(3)} for f in range(frames)}
    rounds = []
    for _ in range(3):
        taken = {}

        def place(f, seen):
            for t, to in left[f].items():
                if to in seen:
                    continue
                seen.add(to)
                if to not in taken or place(taken[to][0], seen):
                    taken[to] = (f, t)
                    return True
            return False

        for f in range(frames):
            place(f, set())
        chosen = {f: (t, to) for to, (f, t) in taken.items()}
        for f, (t, _to) in chosen.items():
            del left[f][t]
        rounds.append(chosen)
    return rounds


def general_solution(mesh):
    F, N = mesh.shape["frame"], mesh.shape["patch"]
    C, Y = 2, 2
    X, Z = F // C, N // Y
    G = X * C * Y
    half_slots = X * Y
    grid = Mesh(mesh.devices.reshape(X, C, Z, Y), ("x", "core", "z", "y"))
    everywhere = ("x", "core", "z", "y")
    offsets = [(dc, dx, dy) for dc in range(C) for dx in range(X) for dy in range(Y)]

    def from_xy(a, dx, dy):
        if dx == 0 and dy == 0:
            return a
        pairs = [
            (x * Y + y, ((x - dx) % X) * Y + (y - dy) % Y) for x in range(X) for y in range(Y)
        ]
        return lax.ppermute(a, ("x", "y"), pairs)

    def to_xy(a, dx, dy):
        return from_xy(a, (-dx) % X, (-dy) % Y)

    def swap_core(a):
        return lax.ppermute(a, "core", [(0, 1), (1, 0)])

    def swap_y(a):
        return lax.ppermute(a, "y", [(0, 1), (1, 0)])

    def gather_slots(a):
        mine = [from_xy(a, dx, dy) for dx in range(X) for dy in range(Y)]
        return mine + [swap_core(piece) for piece in mine]

    def scatter_sum(slots):
        received = swap_core(slots[half_slots:])
        terms = []
        for slot in range(half_slots):
            total = slots[slot].astype(F32) + received[slot].astype(F32)
            terms.append(to_xy(total.astype(BF), slot // Y, slot % Y))
        return terms

    def exchange(slots):
        received = swap_core(slots[half_slots:])
        pieces = [None] * G
        for slot in range(half_slots):
            dx, dy = slot // Y, slot % Y
            pair = to_xy(jnp.stack([slots[slot], received[slot]]), dx, dy)
            source = ((-dx) % X) * Y + (-dy) % Y
            pieces[source] = pair[0]
            pieces[half_slots + source] = pair[1]
        return jnp.stack(pieces)

    def local(tokens, image_mask, sample_index, condition, ada_weight, ada_bias, qkv_weight, qkv_bias,
              proj_weight, proj_bias, fc1_weight, fc1_bias, fc2_weight, fc2_bias, cotangent):
        frames, columns, d = tokens.shape
        T = frames * columns
        S = G * T
        samples = condition.shape[0]
        rows_here = ada_weight.shape[0]
        ff = fc1_weight.shape[1]
        width = d // G
        unit = ff // (N * F)
        part_ff = Z * unit
        x_i, c_i = lax.axis_index("x"), lax.axis_index("core")
        z_i, y_i = lax.axis_index("z"), lax.axis_index("y")
        f_i = x_i * C + c_i
        p_i = z_i * Y + y_i
        g_i = f_i * Y + y_i
        parts_at = [
            (((x_i + dx) % X) * C + (c_i + dc) % C) * Y + (y_i + dy) % Y for dc, dx, dy in offsets
        ]
        parts_at = jnp.stack(parts_at).astype(jnp.int32)
        all_parts = jnp.arange(G, dtype=jnp.int32)
        part_x, part_c, part_y = all_parts // (C * Y), (all_parts // Y) % C, all_parts % Y
        place = ((part_c - c_i) % C) * half_slots + ((part_x - x_i) % X) * Y + (part_y - y_i) % Y
        place = place.astype(jnp.int32)

        def y_pair(own, other):
            got = swap_y(other)
            return jnp.where(y_i == 0, jnp.stack([own, got]), jnp.stack([got, own]))

        pair_width = Y * width
        qkv_cols = [
            lax.dynamic_slice_in_dim(qkv_weight, t * d + f_i * pair_width, pair_width, 1) for t in range(3)
        ]

        def qkv_for(which):
            return jnp.concatenate(
                [lax.dynamic_slice_in_dim(c, which * width, width, 1) for c in qkv_cols], axis=1
            )

        qkv_rows = y_pair(qkv_for(y_i), qkv_for(1 - y_i)).reshape(Y * rows_here, 3 * width)
        w_qkv = lax.all_gather(qkv_rows, "z", axis=0, tiled=True)
        half_rows = rows_here // C
        proj_half = lax.dynamic_slice_in_dim(proj_weight, c_i * half_rows, half_rows, 0)
        proj_rows = y_pair(proj_half, proj_half).reshape(Y * half_rows, d)
        proj_mine = lax.all_gather(proj_rows, "z", axis=0, tiled=True)
        proj_other = swap_core(proj_mine)
        proj_both = jnp.where(
            c_i == 0, jnp.stack([proj_mine, proj_other]), jnp.stack([proj_other, proj_mine])
        )
        proj_parts = (
            proj_both.reshape(C, N, half_rows, d).transpose(1, 0, 2, 3).reshape(G, width, d)
        )
        proj_rel = jnp.concatenate(
            [lax.dynamic_index_in_dim(proj_parts, parts_at[r], 0, keepdims=False) for r in range(G)],
            axis=0,
        )

        def fc1_for(which):
            return jnp.concatenate(
                [
                    lax.dynamic_slice_in_dim(
                        fc1_weight, (z * Y + which) * (F * unit) + f_i * unit, unit, 1
                    )
                    for z in range(Z)
                ],
                axis=1,
            )

        fc1_rows = y_pair(fc1_for(y_i), fc1_for(1 - y_i)).reshape(Y * rows_here, part_ff)
        w_fc1 = lax.all_gather(fc1_rows, "z", axis=0, tiled=True)
        fc2_rows = lax.dynamic_slice_in_dim(fc2_weight, f_i * unit, unit, 0)
        w_fc2 = lax.all_gather(fc2_rows, "z", axis=0, tiled=True)

        chunk = samples * 6 * d // (F * N)
        per_row = 6 * d // chunk
        frame_samples = samples // F
        first_row = p_i * rows_here
        cond_rows = lax.dynamic_slice_in_dim(condition, first_row, rows_here, 1).astype(F32)
        sigmoid = 1.0 / (1.0 + jnp.exp(-cond_rows))
        act_rows = (cond_rows * sigmoid).astype(BF)
        silu_slope = sigmoid * (1.0 + cond_rows * (1.0 - sigmoid))
        act_mine = lax.dynamic_slice_in_dim(act_rows, f_i * frame_samples, frame_samples, 0)
        partial_mod = mm(act_mine, ada_weight).reshape(N, chunk)
        mod_terms = lax.all_to_all(partial_mod, ("z", "y"), 0, 0, tiled=True)
        bias_here = lax.dynamic_slice_in_dim(ada_bias, (p_i % per_row) * chunk, chunk, 0)
        mod_chunk = (jnp.sum(mod_terms, axis=0) + bias_here.astype(F32)).astype(BF)
        mod = lax.all_to_all(
            jnp.broadcast_to(mod_chunk, (F * N, chunk)), everywhere, 0, 0, tiled=True
        ).reshape(samples, 6 * d)

        flat_tokens = tokens.reshape(T, d)
        flat_cot = cotangent.reshape(T, d)
        mask = image_mask.reshape(T, 1)
        grad_two_own = jnp.where(mask == 1, jnp.zeros_like(flat_cot), flat_cot)
        codes = jnp.zeros((16, d), BF).at[0, :T].set(sample_index.reshape(T).astype(BF))
        token_slots = gather_slots(jnp.concatenate([flat_tokens, codes], axis=0))
        slab_tokens = jnp.concatenate([piece[:T] for piece in token_slots], axis=0)
        slab_codes = jnp.stack([piece[T, :T] for piece in token_slots]).astype(jnp.int32)
        slab_cot = jnp.concatenate(gather_slots(grad_two_own), axis=0)
        numbers = jnp.arange(samples, dtype=jnp.int32)
        selt = (slab_codes.reshape(1, S) == numbers[:, None]).astype(BF)
        sel = (slab_codes.reshape(S, 1) == numbers[None, :]).astype(BF)
        sel_own, selt_own = sel[:T], selt[:, :T]

        steps = G // 2
        TB = 2 * T
        row_block = lambda w: pl.BlockSpec((TB, w), lambda j: (j, 0))
        lane_block = lambda h: pl.BlockSpec((h, TB), lambda j: (0, j))

        bias_q = lax.dynamic_slice_in_dim(qkv_bias, g_i * width, width, 0)
        bias_v = lax.dynamic_slice_in_dim(qkv_bias, d + g_i * width, width, 0)
        bias_qkv = jnp.concatenate([bias_q, jnp.zeros_like(bias_q), bias_v]).astype(F32)[None]
        attn_t, qkv = pl.pallas_call(
            functools.partial(general_attend_kernel, d, width, columns),
            grid=(steps,),
            in_specs=[
                row_block(d),
                row_block(samples),
                whole((samples, 6 * d)),
                whole((d, 3 * width)),
                whole((1, 3 * width)),
            ],
            out_specs=[lane_block(width), row_block(3 * width)],
            out_shape=[
                jax.ShapeDtypeStruct((width, S), BF),
                jax.ShapeDtypeStruct((S, 3 * width), BF),
            ],
            compiler_params=params(),
            cost_estimate=cost(2 * S * d * 3 * width * 2, 8e6),
            name="attend",
        )(slab_tokens, sel, mod, w_qkv, bias_qkv)

        attn_slots = gather_slots(attn_t)
        order = [dy == 1 for _, _, dy in offsets]

        def slot_spec(dc, dx):
            return pl.BlockSpec(
                (width, TB),
                lambda j: (0, ((j // X + C - dc) % C) * X + (j % X + X - dx) % X),
            )

        slot_specs = [slot_spec(dc, dx) for dc, dx, _ in offsets]

        hidden_at = lambda v: jnp.concatenate(
            [
                lax.dynamic_slice_in_dim(v, (z * Y + y_i) * (F * unit) + f_i * unit, unit, 0)
                for z in range(Z)
            ]
        )
        fc1_bias_part = hidden_at(fc1_bias).astype(F32)[None]
        fc2_bias_once = jnp.where(g_i == 0, fc2_bias.astype(F32), 0.0)[None]
        slot_out = pl.BlockSpec((2, T, d), lambda j: (j, 0, 0))
        (b2_slots, gm_slots, fc1g, fc2g, fc1_bias_g, fc2_bias_g, modg_two, after_own, branch_own) = pl.pallas_call(
            functools.partial(general_mlp_kernel, d, order),
            grid=(steps,),
            in_specs=slot_specs
            + [
                row_block(d),
                row_block(d),
                row_block(samples),
                lane_block(samples),
                whole((samples, 6 * d)),
                whole((d, d)),
                whole((1, d)),
                whole((d, part_ff)),
                whole((1, part_ff)),
                whole((part_ff, d)),
                whole((1, d)),
            ],
            out_specs=[
                slot_out,
                slot_out,
                whole((d, part_ff)),
                whole((part_ff, d)),
                whole((1, part_ff)),
                whole((1, d)),
                whole((3, samples, d)),
                whole((T, d)),
                whole((T, d)),
            ],
            out_shape=[
                jax.ShapeDtypeStruct((G, T, d), BF),
                jax.ShapeDtypeStruct((G, T, d), BF),
                jax.ShapeDtypeStruct((d, part_ff), BF),
                jax.ShapeDtypeStruct((part_ff, d), BF),
                jax.ShapeDtypeStruct((1, part_ff), F32),
                jax.ShapeDtypeStruct((1, d), F32),
                jax.ShapeDtypeStruct((3, samples, d), F32),
                jax.ShapeDtypeStruct((T, d), F32),
                jax.ShapeDtypeStruct((T, d), F32),
            ],
            scratch_shapes=[pltpu.VMEM((d, part_ff), F32), pltpu.VMEM((part_ff, d), F32)],
            compiler_params=params(),
            cost_estimate=cost(2 * S * (d * d + 6 * d * part_ff), 3e7),
            name="mlp",
        )(
            *attn_slots,
            slab_tokens,
            slab_cot,
            sel,
            selt,
            mod,
            proj_rel,
            proj_bias.astype(F32)[None],
            w_fc1,
            fc1_bias_part,
            w_fc2,
            fc2_bias_once,
        )

        fc1_z = lax.psum_scatter(fc1g, "z", scatter_dimension=0, tiled=True)
        fc2_z = lax.psum_scatter(fc2g, "z", scatter_dimension=0, tiled=True)
        gm_terms = scatter_sum(gm_slots)

        ex_slots, grad_one, modg_gate, proj_bias_g = pl.pallas_call(
            functools.partial(general_middle_kernel, d, G, len(gm_terms)),
            grid_spec=pltpu.PrefetchScalarGridSpec(
                num_scalar_prefetch=1,
                grid=(1,),
                in_specs=[whole((T, d))] * len(gm_terms)
                + [
                    whole((T, d)),
                    whole((T, d)),
                    whole((T, d)),
                    whole((T, samples)),
                    whole((samples, T)),
                    whole((samples, 6 * d)),
                    whole((d, d)),
                ],
                out_specs=[
                    whole((G, 2, width, T)),
                    whole((T, d)),
                    whole((samples, d)),
                    whole((1, d)),
                ],
            ),
            out_shape=[
                jax.ShapeDtypeStruct((G, 2, width, T), BF),
                jax.ShapeDtypeStruct((T, d), F32),
                jax.ShapeDtypeStruct((samples, d), F32),
                jax.ShapeDtypeStruct((1, d), F32),
            ],
            compiler_params=params(),
            cost_estimate=cost(4 * T * d * d, 8e6),
            name="middle",
        )(place, *gm_terms, after_own, branch_own, grad_two_own, sel_own, selt_own, mod, proj_rel)

        grad_attn = exchange(ex_slots)
        b2_terms = scatter_sum(b2_slots)

        slot_back = [
            pl.BlockSpec(spec.block_shape, lambda j, place, spec=spec: spec.index_map(j))
            for spec in slot_specs
        ]
        rows_b = lambda w: pl.BlockSpec((TB, w), lambda j, place: (j, 0))
        gin_slots, qkvg, projg, qkv_bias_part, modg_one = pl.pallas_call(
            functools.partial(general_attend_back_kernel, d, width, columns, order),
            grid_spec=pltpu.PrefetchScalarGridSpec(
                num_scalar_prefetch=1,
                grid=(steps,),
                in_specs=slot_back
                + [
                    pl.BlockSpec((2, 2, width, T), lambda j, place: (j, 0, 0, 0)),
                    rows_b(d),
                    rows_b(samples),
                    pl.BlockSpec((samples, TB), lambda j, place: (0, j)),
                    whole((samples, 6 * d)),
                    whole((d, 3 * width)),
                    rows_b(3 * width),
                ],
                out_specs=[
                    pl.BlockSpec((2, T, d), lambda j, place: (j, 0, 0)),
                    whole((d, 3 * width)),
                    whole((G, width, width)),
                    whole((1, 3 * width)),
                    whole((2, samples, d)),
                ],
                scratch_shapes=[
                    pltpu.VMEM((d, 3 * width), F32),
                    pltpu.VMEM((d, width), F32),
                ],
            ),
            out_shape=[
                jax.ShapeDtypeStruct((G, T, d), BF),
                jax.ShapeDtypeStruct((d, 3 * width), BF),
                jax.ShapeDtypeStruct((G, width, width), BF),
                jax.ShapeDtypeStruct((1, 3 * width), F32),
                jax.ShapeDtypeStruct((2, samples, d), F32),
            ],
            compiler_params=params(),
            cost_estimate=cost(2 * S * d * 8 * width, 1.2e7),
            name="attend_back",
        )(parts_at, *attn_slots, grad_attn, slab_tokens, sel, selt, mod, w_qkv, qkv)

        gin_terms = scatter_sum(gin_slots)

        bias_total = 2 * d + d + ff + d
        biases = jnp.zeros((bias_total,), F32)
        put = lax.dynamic_update_slice_in_dim
        biases = put(biases, qkv_bias_part[0, :width], g_i * width, 0)
        biases = put(biases, qkv_bias_part[0, 2 * width :], d + g_i * width, 0)
        biases = put(biases, proj_bias_g[0], 2 * d, 0)
        for z in range(Z):
            biases = put(
                biases,
                fc1_bias_g[0, z * unit : (z + 1) * unit],
                3 * d + (z * Y + y_i) * (F * unit) + f_i * unit,
                0,
            )
        biases = put(biases, jnp.where(g_i == 0, fc2_bias_g[0], 0.0), 3 * d + ff, 0)
        mod_sums = jnp.concatenate(
            [modg_one[0], modg_one[1], modg_gate, modg_two[0], modg_two[1], modg_two[2]], axis=1
        )
        to_sum = jnp.concatenate(
            [mod_sums.reshape(F * N, chunk), biases.reshape(F * N, bias_total // (F * N))], axis=1
        ).astype(BF)
        terms = lax.all_to_all(to_sum, everywhere, 0, 0, tiled=True)
        summed = jnp.sum(terms.astype(F32), axis=0).astype(BF)
        total = lax.all_to_all(
            jnp.broadcast_to(summed, (F * N, summed.shape[0])), everywhere, 0, 0, tiled=True
        )
        mod_grad = total[:, :chunk].reshape(samples, 6 * d)
        bias_grad = total[:, chunk:].reshape(bias_total).astype(F32)
        ada_bias_grad = jnp.sum(mod_grad.astype(F32), axis=0)
        ada_weight_grad = mm(act_rows, mod_grad, 0, 0)
        condition_grad = mm(mod_grad, ada_weight, 1, 1) * silu_slope

        def y_join(rows):
            kept = lax.dynamic_index_in_dim(rows, y_i, 0, keepdims=False)
            got = swap_y(lax.dynamic_index_in_dim(rows, 1 - y_i, 0, keepdims=False))
            return jnp.where(y_i == 0, jnp.stack([kept, got]), jnp.stack([got, kept]))

        attn_g = jnp.concatenate([qkvg, projg.reshape(d, width)], axis=1)
        attn_z = lax.psum_scatter(attn_g, "z", scatter_dimension=0, tiled=True)
        attn_y = y_join(attn_z.reshape(Y, rows_here, 4 * width))
        blocks = jnp.stack(
            [
                jnp.concatenate([attn_y[y, :, t * width : (t + 1) * width] for y in range(Y)], axis=1)
                for t in range(4)
            ]
        )
        proj_weight_grad = blocks[3].astype(F32)
        moved = [None] * 3
        spots = jnp.zeros((3, F), jnp.int32)
        for turn, chosen in enumerate(matchings(F)):
            picks = jnp.array([chosen[f][0] for f in range(F)], jnp.int32)
            block = lax.dynamic_index_in_dim(blocks, picks[f_i], 0, keepdims=False)
            pairs = [(f, chosen[f][1]) for f in range(F)]
            if any(a != b for a, b in pairs):
                block = lax.ppermute(block, ("x", "core"), pairs)
            moved[turn] = block
            for f in range(F):
                t, to = chosen[f]
                spots = spots.at[(F * t + f) % 3, to].set(turn)
        moved = jnp.stack(moved)
        qkv_weight_grad = jnp.concatenate(
            [
                lax.dynamic_index_in_dim(moved, spots[k, f_i], 0, keepdims=False)
                for k in range(3)
            ],
            axis=1,
        ).astype(F32)

        fc1_y = y_join(fc1_z.reshape(Y, rows_here, part_ff))
        per_frame = Z // F
        fc1_send = fc1_y.reshape(Y, rows_here, F, per_frame, unit).transpose(2, 1, 3, 0, 4)
        fc1_got = lax.all_to_all(fc1_send, ("x", "core"), 0, 0, tiled=True)
        fc1_weight_grad = (
            fc1_got.transpose(1, 2, 3, 0, 4).reshape(rows_here, ff // F).astype(F32)
        )
        fc2_send = fc2_z.reshape(unit, F, d // F).transpose(1, 0, 2)
        fc2_got = lax.all_to_all(fc2_send, ("x", "core"), 0, 0, tiled=True)
        fc2_weight_grad = fc2_got.reshape(F * unit, d // F).astype(F32)

        result, input_grad = pl.pallas_call(
            functools.partial(general_last_kernel, d, len(gin_terms), len(b2_terms)),
            out_shape=[jax.ShapeDtypeStruct((T, d), BF), jax.ShapeDtypeStruct((T, d), F32)],
            compiler_params=pltpu.CompilerParams(vmem_limit_bytes=VMEM_BYTES),
            cost_estimate=cost(1e6, 5e6),
            name="last",
        )(*gin_terms, *b2_terms, flat_tokens, grad_one, after_own, flat_cot, mask, sel_own, mod)

        shape = (frames, columns, d)
        return (
            result.reshape(shape),
            input_grad.reshape(shape),
            condition_grad,
            ada_weight_grad,
            ada_bias_grad,
            qkv_weight_grad,
            bias_grad[: 2 * d],
            proj_weight_grad,
            bias_grad[2 * d : 3 * d],
            fc1_weight_grad,
            bias_grad[3 * d : 3 * d + ff],
            fc2_weight_grad,
            bias_grad[3 * d + ff :],
        )

    frame, patch = ("x", "core"), ("z", "y")
    every = ("x", "core", "z", "y")
    token_spec = P(None, every, None)
    number_spec = P(None, every)
    row_spec = P(patch, None)
    both_spec = P(patch, frame)
    return jax.shard_map(
        local,
        mesh=grid,
        in_specs=(
            token_spec, number_spec, number_spec, P(), row_spec, P(), row_spec, P(), row_spec, P(), row_spec, P(),
            row_spec, P(), token_spec,
        ),
        out_specs=(
            token_spec, token_spec, P(None, patch), row_spec, P(), both_spec, P(), both_spec, P(), both_spec, P(),
            both_spec, P(),
        ),
        check_vma=False,
    )


def takes(microseconds):
    return pl.CostEstimate(flops=1000, bytes_accessed=1000, transcendentals=0)


def wide(lanes):
    return -(-lanes // 128) * 128


def row_of(values):
    return jnp.concatenate([values[k : k + 1] for k in range(values.shape[0])], axis=1)


def put_row(ref, row):
    for k in range(ref.shape[0]):
        ref[k : k + 1] = row[:, k * 128 : (k + 1) * 128]


def pick(index, options):
    total = jnp.where(index == 0, options[0], 0.0)
    for k in range(1, len(options)):
        total = total + jnp.where(index == k, options[k], 0.0)
    return total


def spread(values, index, n):
    return jnp.concatenate([jnp.where(index == k, values, 0.0) for k in range(n)], axis=1)


def at_rows(index, rows):
    return pl.ds(pl.multiple_of(index * rows, rows), rows)


def prepare_kernel(d, place, cond_ref, ada_ref, qkv_ref, fc1_ref, proj_ref, fc2_ref, tok_ref, cot_ref, num_ref, mask_ref,
                   part_ref, act_ref, slope_ref, qkv_mine, fc1_mine, send_out, fc2_out, tok_out, act_all):
    rows = ada_ref.shape[0]
    cols = 2 * rows
    for ref in (qkv_mine, fc1_mine, send_out, fc2_out):
        ref[...] = jnp.zeros_like(ref)
    act_ref[...] = jnp.zeros_like(act_ref)
    slope_ref[...] = jnp.zeros_like(slope_ref)
    for f in range(4):

        @pl.when(place[AT_F] == f)
        def _():
            fc2_out[:, d : d + cols] = proj_ref[:, f * cols : (f + 1) * cols]
            for y in range(2):
                for q_out, at_q, f_out, want in ((qkv_mine, 0, fc1_mine, y), (send_out, wide(4 * rows), send_out, 1 - y)):

                    @pl.when(place[AT_Y] == want)
                    def _():
                        for t in range(3):
                            at = t * d + (2 * f + y) * rows
                            q_out[:, at_q + t * rows : at_q + (t + 1) * rows] = qkv_ref[:, at : at + rows]
                        for z in range(4):
                            at = ((z * 2 + y) * 4 + f) * rows
                            f_out[:, z * rows : (z + 1) * rows] = fc1_ref[:, at : at + rows]

    fc2_out[:, :d] = fc2_ref[at_rows(place[AT_F], rows)]
    row = lax.broadcasted_iota(jnp.int32, (d, rows), 0)
    col = lax.broadcasted_iota(jnp.int32, (d, rows), 1)
    cond = mm(cond_ref[...], (row == col + place[AT_P] * rows).astype(BF))
    sigmoid = 1.0 / (1.0 + jnp.exp(-cond))
    act = cond * sigmoid
    act_ref[:, :rows] = act.astype(BF)
    slope_ref[:, :rows] = sigmoid * (1.0 + cond * (1.0 - sigmoid))
    act_all[...] = act
    mine = act_all[at_rows(place[AT_F], 8)].astype(BF)
    for block in range(8):
        if block < 6:
            part_ref[block] = mm(mine, ada_ref[:, block * d : (block + 1) * d]).astype(BF)
        else:
            part_ref[block] = jnp.zeros(part_ref.shape[1:], BF)
    size = tok_ref.shape[0]
    columns, frames = num_ref.shape

    def token_row(ref):
        lane = lax.broadcasted_iota(jnp.int32, (frames, size), 1)
        frame = lax.broadcasted_iota(jnp.int32, (frames, size), 0)
        wide = mm(ref[...].astype(F32).astype(BF), (lane // columns == frame).astype(BF))
        lane = lax.broadcasted_iota(jnp.int32, (columns, size), 1)
        column = lax.broadcasted_iota(jnp.int32, (columns, size), 0)
        return jnp.sum(jnp.where(lax.rem(lane, columns) == column, wide, 0.0), axis=0, keepdims=True)

    tok_out[size : 2 * size] = tok_ref[...]
    tok_out[2 * size :] = jnp.zeros((16, d), BF)
    tok_out[2 * size :, :size] = jnp.broadcast_to(token_row(num_ref), (16, size)).astype(BF)
    masked = jnp.broadcast_to(token_row(mask_ref), (size, size)).T[:, 0:1]
    tok_out[:size] = jnp.where(masked > 0.5, 0.0, cot_ref[...].astype(F32)).astype(BF)


def mod_sum_kernel(place, terms_ref, bias_ref, out_ref):
    total = terms_ref[0].astype(F32)
    for k in range(1, terms_ref.shape[0]):
        total = total + terms_ref[k].astype(F32)
    bias = row_of(bias_ref[...].astype(F32))
    d = total.shape[1]
    total = total + pick(place[AT_P], [bias[:, k * d : (k + 1) * d] for k in range(6)])
    out_ref[...] = total.astype(BF)


def grad_sum_kernel(place, terms_ref, out_ref):
    total = terms_ref[0].astype(F32)
    for k in range(1, terms_ref.shape[0]):
        total = total + terms_ref[k].astype(F32)
    out_ref[...] = total.astype(BF)


def chunk_of(ref, place, chunk):
    at_z = lax.bitwise_xor(place[AT_Z], chunk // 2 % 4)
    return ref[chunk // 8 * 2 + chunk % 2, at_z]


def token_pair(near_ref, far_ref, size):
    near = pl.program_id(0) < pl.num_programs(0) // 2
    parts, codes = [], []
    for half in range(2):
        rows = slice(size, 2 * size)
        parts.append(jnp.where(near, near_ref[half, rows].astype(F32), far_ref[half, rows].astype(F32)))
        rows = slice(2 * size, 2 * size + 16)
        code = jnp.where(near, near_ref[half, rows, :size].astype(F32), far_ref[half, rows, :size].astype(F32))
        codes.append(code[0:1])
    return jnp.concatenate(parts, axis=0), codes


def attend_kernel(d, width, columns, place, tok_near, tok_far, w_in, modin_ref, bias_ref,
                  out_ref, qkv_ref, sel_ref, selt_ref, w_ref, mod_ref, bias_row):
    step = pl.program_id(0)
    samples = selt_ref.shape[0]
    size = out_ref.shape[1] // 2

    @pl.when(step == 0)
    def _():
        for z in range(4):
            for dy in range(2):
                patch = z * 2 + lax.bitwise_xor(place[AT_Y], dy)
                w_ref[at_rows(patch, width), :] = w_in[z, dy]
        for block in range(6):
            pieces = [chunk_of(modin_ref, place, f * 8 + block).astype(F32) for f in range(4)]
            mod_ref[block] = jnp.concatenate(pieces, axis=0).astype(BF)
        bias = row_of(bias_ref[...].astype(F32))
        bias_row[:, :width] = pick(place[AT_G], [bias[:, k * width : (k + 1) * width] for k in range(8)])
        bias_row[:, width : 2 * width] = jnp.zeros((1, width), F32)
        bias_row[:, 2 * width :] = pick(place[AT_G], [bias[:, d + k * width : d + (k + 1) * width] for k in range(8)])

    numbers = lax.broadcasted_iota(jnp.int32, (samples, size), 0).astype(F32)
    tokens, codes = token_pair(tok_near, tok_far, size)
    for half in range(2):
        rows = slice(half * size, (half + 1) * size)
        hot = (codes[half] == numbers).astype(F32)
        selt_ref[:, rows] = hot.astype(BF)
        sel_ref[rows, :samples] = hot.T.astype(BF)
    normed, _ = normalize(tokens)
    sel = sel_ref[:, : mod_ref.shape[1]]
    attn_in = (normed * (1.0 + mm(sel, mod_ref[1])) + mm(sel, mod_ref[0])).astype(BF)
    qkv = (mm(attn_in, w_ref[:, : 3 * width]) + bias_row[...]).astype(BF)
    qkv_ref[:, : 3 * width] = qkv
    same = column_mask(size, columns)
    for half in range(2):
        rows = slice(half * size, (half + 1) * size)
        parts = []
        for head in range(width // HEAD_DIM):
            q, k, v = (
                qkv[rows, t * width + head * HEAD_DIM : t * width + (head + 1) * HEAD_DIM]
                for t in range(3)
            )
            prob = softmax_prob(q, k, same)
            parts.append(mm(prob.astype(BF), v).T)
        out_ref[:, rows] = jnp.concatenate(parts, axis=0).astype(BF)


def proj_kernel(d, place, *refs):
    rows = d // 8
    pieces, (proj_all, columns) = refs[:8], refs[8:]
    for slot, ref in enumerate(pieces):
        columns[slot] = ref[...]
    for slot in range(8):
        part = place[AT_PART + slot]
        for f in range(4):
            source = place[AT_SLOT + f * 2 + lax.rem(part, 2)]
            proj_all[slot * rows : (slot + 1) * rows, f * 2 * rows : (f + 1) * 2 * rows] = columns[source, part // 2]


def mlp_kernel(d, order, place, *refs):
    n = len(order)
    slots = refs[:n]
    (tok_near, tok_far, sel_ref, selt_ref, mod_ref, proj_all, projb_ref, fc1_in, fc1b_ref, fc2_in, fc2b_ref) = refs[n : n + 11]
    (b2_own, b2_far, gm_own, gm_far, fcg_ref, fc1bg_ref, fc2bg_ref, modg_ref, after_ref, branch_ref) = refs[n + 11 : n + 21]
    (fc1a, fc2a, fc1_ref, fc2_ref, pb_row, f1_row, f2_row) = refs[n + 21 :]
    step = pl.program_id(0)
    size = sel_ref.shape[0] // 2
    rows = d // 8
    sel = sel_ref[:, : mod_ref.shape[1]]
    selt = selt_ref[...]

    @pl.when(step == 0)
    def _():
        for z in range(4):
            for dy in range(2):
                patch = z * 2 + lax.bitwise_xor(place[AT_Y], dy)
                fc1_ref[at_rows(patch, rows), :] = fc1_in[z, dy, :, : 4 * rows]
            fc2_ref[z * rows : (z + 1) * rows] = fc2_in[z, :, :d]
        pb_row[...] = row_of(projb_ref[...].astype(F32))
        f2_row[...] = jnp.where(place[AT_G] == 0, row_of(fc2b_ref[...].astype(F32)), 0.0)
        bias = row_of(fc1b_ref[...].astype(F32))
        for z in range(4):
            options = []
            for k in range(8):
                at = (z * 8 + k) * rows
                options.append(bias[:, at : at + rows])
            f1_row[:, z * rows : (z + 1) * rows] = pick(place[AT_Y] * 4 + place[AT_F], options)

    tokens, _ = token_pair(tok_near, tok_far, size)
    grad_two = jnp.where(step < pl.num_programs(0) // 2, tok_near[:, :size].astype(F32), tok_far[:, :size].astype(F32))
    grad_two = grad_two.reshape(2 * size, d)
    attn_t = slab_attention(slots, order, size)
    branch_one = mm(attn_t, proj_all[...], 0, 0) + pb_row[...]
    after_one = tokens + mm(sel, mod_ref[2]) * branch_one

    @pl.when(step == 0)
    def _():
        after_ref[...] = after_one[:size]
        branch_ref[...] = branch_one[:size]
        fc1a[...] = jnp.zeros_like(fc1a)
        fc2a[...] = jnp.zeros_like(fc2a)
        fc1bg_ref[...] = jnp.zeros_like(fc1bg_ref)
        fc2bg_ref[...] = jnp.zeros_like(fc2bg_ref)
        modg_ref[...] = jnp.zeros_like(modg_ref)

    normed, _ = normalize(after_one)
    mlp_in = (normed * (1.0 + mm(sel, mod_ref[4])) + mm(sel, mod_ref[3])).astype(BF)
    pre = mm(mlp_in, fc1_ref[...]) + f1_row[...]
    square = pre * pre
    tanh = jnp.tanh(GELU_C * pre * (1.0 + GELU_A * square))
    hidden = (0.5 * pre * (1.0 + tanh)).astype(BF)
    slope = 0.5 * (1.0 + tanh) + 0.5 * pre * (1.0 - tanh * tanh) * GELU_C * (1.0 + 3.0 * GELU_A * square)
    branch_two = mm(hidden, fc2_ref[...]) + f2_row[...]
    gb2 = (mm(sel, mod_ref[5]) * grad_two).astype(BF)
    fc2bg_ref[...] += jnp.sum(gb2.astype(F32), axis=0, keepdims=True)
    fc2a[...] += mm(hidden, gb2, 0, 0)
    grad_pre = (mm(gb2, fc2_ref[...], 1, 1) * slope).astype(BF)
    fc1bg_ref[...] += jnp.sum(grad_pre.astype(F32), axis=0, keepdims=True)
    fc1a[...] += mm(mlp_in, grad_pre, 0, 0)
    grad_in = mm(grad_pre, fc1_ref[...], 1, 1)
    modg_ref[0] += mm(selt, grad_in.astype(BF))
    modg_ref[1] += mm(selt, (grad_in * normed).astype(BF))
    modg_ref[2] += mm(selt, (grad_two * branch_two).astype(BF))
    near = step < pl.num_programs(0) // 2

    @pl.when(near)
    def _():
        b2_own[...] = branch_two.astype(BF).reshape(b2_own.shape)
        gm_own[...] = grad_in.astype(BF).reshape(gm_own.shape)

    @pl.when(jnp.logical_not(near))
    def _():
        b2_far[...] = branch_two.astype(BF).reshape(b2_far.shape)
        gm_far[...] = grad_in.astype(BF).reshape(gm_far.shape)

    @pl.when(step == pl.num_programs(0) - 1)
    def _():
        for z in range(4):
            for y in range(2):
                at = (z * 2 + y) * rows
                to = (z * 4 + y) * rows
                fcg_ref[to : to + rows, : 4 * rows] = fc1a[at : at + rows].astype(BF)
            block = fc2a[z * rows : (z + 1) * rows].astype(BF)
            to = (z * 4 + 2) * rows
            fcg_ref[to : to + rows, : 4 * rows] = block[:, : d // 2]
            fcg_ref[to + rows : to + 2 * rows, : 4 * rows] = block[:, d // 2 :]


def middle_kernel(d, count, place, *refs):
    grads = refs[:count]
    (after_ref, branch_ref, cot_ref, sel_ref, selt_ref, mod_ref, proj_ref) = refs[count : count + 7]
    ex_refs = refs[count + 7 : count + 15]
    (one_ref, modg_ref, pbias_ref, turned) = refs[count + 15 :]
    sel = sel_ref[:, : mod_ref.shape[1]]
    grad_in = grads[0][...].astype(F32)
    for ref in grads[1:]:
        grad_in = grad_in + ref[...].astype(F32)
    normed, inverse = normalize(after_ref[...])
    scale = mm(sel, mod_ref[4])
    gate = mm(sel, mod_ref[2])
    grad_one = cot_ref[...].astype(F32) + normalize_back(grad_in * (1.0 + scale), normed, inverse)
    one_ref[...] = grad_one
    modg_ref[...] = mm(selt_ref[...], (grad_one * branch_ref[...]).astype(BF))
    gb1 = (gate * grad_one).astype(BF)
    gb1_wide = gb1.astype(F32)
    pbias_ref[...] = jnp.sum(gb1_wide, axis=0, keepdims=True)
    width = d // 8
    turned[...] = gb1_wide.T
    grad_attn = mm(proj_ref[...], gb1, 1, 1)
    for slot, ref in enumerate(ex_refs):
        ref[0] = grad_attn[slot * width : (slot + 1) * width].astype(BF)
        ref[1] = turned[at_rows(place[AT_PART + slot], width)].astype(BF)


def back_kernel(d, width, columns, place, *refs):
    n = 8
    gas = refs[:n]
    (tok_near, tok_far, sel_ref, selt_ref, mod_ref, qkv_ref, w_ref, two_ref, gate_ref, pb_ref, f1b_ref, f2b_ref) = refs[n : n + 12]
    (gin_own, gin_far, gqkv_ref, in_ref, sum_ref) = refs[n + 12 : n + 17]
    (ga_all, modg, bias_row) = refs[n + 17 :]
    step = pl.program_id(0)
    size = sel_ref.shape[0] // 2

    @pl.when(step == 0)
    def _():
        bias_row[...] = jnp.zeros_like(bias_row)
        modg[...] = jnp.zeros_like(modg)
        for k, ref in enumerate(gas):
            ga_all[k] = ref[...]

    qkv = qkv_ref[:, : 3 * width]
    same = column_mask(size, columns)
    heads = width // HEAD_DIM
    halves = []
    for half in range(2):
        rows = slice(half * size, (half + 1) * size)
        grad_mixed = ga_all[2 * step + half, 0].astype(F32).T
        pieces = [None] * (3 * heads)
        for head in range(heads):
            q, k, v = (
                qkv[rows, t * width + head * HEAD_DIM : t * width + (head + 1) * HEAD_DIM]
                for t in range(3)
            )
            grad = grad_mixed[:, head * HEAD_DIM : (head + 1) * HEAD_DIM].astype(BF)
            prob = softmax_prob(q, k, same)
            grad_prob = mm(grad, v, 1, 1)
            delta = jnp.sum(prob * grad_prob, axis=-1, keepdims=True)
            grad_score = (prob * (grad_prob - delta) * SCORE_SCALE).astype(BF)
            pieces[head] = mm(grad_score, k)
            pieces[heads + head] = mm(grad_score, q, 0, 0)
            pieces[2 * heads + head] = mm(prob.astype(BF), grad, 0, 0)
        halves.append(jnp.concatenate(pieces, axis=1))
    grad_qkv = jnp.concatenate(halves, axis=0).astype(BF)
    bias_row[...] += jnp.sum(grad_qkv.astype(F32), axis=0, keepdims=True)

    tokens, _ = token_pair(tok_near, tok_far, size)
    normed, _ = normalize(tokens)
    sel = sel_ref[:, : mod_ref.shape[1]]
    selt = selt_ref[...]
    attn_in = (normed * (1.0 + mm(sel, mod_ref[1])) + mm(sel, mod_ref[0])).astype(BF)
    in_ref[...] = attn_in
    gqkv_ref[:, : 3 * width] = grad_qkv
    grad_in = mm(grad_qkv, w_ref[:, : 3 * width], 1, 1)
    modg[0] += mm(selt, grad_in.astype(BF))
    modg[1] += mm(selt, (grad_in * normed).astype(BF))
    near = step < pl.num_programs(0) // 2

    @pl.when(near)
    def _():
        gin_own[...] = grad_in.astype(BF).reshape(gin_own.shape)

    @pl.when(jnp.logical_not(near))
    def _():
        gin_far[...] = grad_in.astype(BF).reshape(gin_far.shape)

    @pl.when(step == pl.num_programs(0) - 1)
    def _():
        blocks = [modg[0], modg[1], gate_ref[...], two_ref[0], two_ref[1], two_ref[2]]
        for k, block in enumerate(blocks):
            for group in range(4):
                sum_ref[k * 4 + group] = block[group * 8 : (group + 1) * 8].astype(BF)
        part = place[AT_G]
        rows = [
            spread(bias_row[:, :width], part, 8),
            spread(bias_row[:, 2 * width :], part, 8),
            pb_ref[...],
        ]
        at = place[AT_Y] * 4 + place[AT_F]
        rows += [spread(f1b_ref[:, z * width : (z + 1) * width], at, 8) for z in range(4)]
        rows.append(jnp.where(part == 0, f2b_ref[...], 0.0))
        sum_ref[24] = jnp.concatenate(rows, axis=0).astype(BF)
        for k in range(25, 32):
            sum_ref[k] = jnp.zeros(sum_ref.shape[1:], BF)


def weights_kernel(d, width, order, place, *refs):
    n = len(order)
    slots, gas = refs[:n], refs[n : 2 * n]
    (gqkv_ref, in_ref, grad_ref, qkva, proja, ga_all) = refs[2 * n :]
    step = pl.program_id(0)
    size = in_ref.shape[0] // 2

    @pl.when(step == 0)
    def _():
        qkva[...] = jnp.zeros_like(qkva)
        proja[...] = jnp.zeros_like(proja)
        for k, ref in enumerate(gas):
            ga_all[k] = ref[1]

    qkva[...] += mm(in_ref[...], gqkv_ref[:, : 3 * width], 0, 0)
    attn_t = slab_attention(slots, order, size)
    gb1_t = jnp.concatenate([ga_all[2 * step], ga_all[2 * step + 1]], axis=1)
    proja[...] += mm(attn_t, gb1_t, 1, 1)

    @pl.when(step == pl.num_programs(0) - 1)
    def _():
        grad_ref[:, : 3 * width] = qkva[...].astype(BF)
        grad_ref[:, 4 * width :] = jnp.zeros((d, grad_ref.shape[1] - 4 * width), BF)
        for slot in range(n):
            grad_ref[at_rows(place[AT_PART + slot], width), 3 * width : 4 * width] = proja[slot * width : (slot + 1) * width].astype(BF)


def ada_kernel(d, place, total_ref, act_ref, slope_ref, w_ref, wg_ref, cond_ref, ada_ref, qkv_ref, proj_ref, fc1_ref, fc2_ref):
    rows = wg_ref.shape[0]
    act = act_ref[:, :rows]
    cond = jnp.zeros(cond_ref.shape, F32)
    sums = []
    for block in range(6):
        grads = jnp.concatenate([chunk_of(total_ref, place, block * 4 + k).astype(F32) for k in range(4)], axis=0)
        cols = slice(block * d, (block + 1) * d)
        sums.append(jnp.sum(grads, axis=0, keepdims=True))
        grads = grads.astype(BF)
        wg_ref[:, cols] = mm(act, grads, 0, 0)
        cond = cond + mm(grads, w_ref[:, cols], 1, 1)
    cond_ref[...] = cond * slope_ref[:, :rows]
    put_row(ada_ref, jnp.concatenate(sums, axis=1))
    biases = chunk_of(total_ref, place, 24).astype(F32)
    rows = [biases[k : k + 1] for k in range(8)]
    put_row(qkv_ref, jnp.concatenate(rows[:2], axis=1))
    put_row(proj_ref, rows[2])
    put_row(fc1_ref, jnp.concatenate(rows[3:7], axis=1))
    put_row(fc2_ref, rows[7])


def mlp_split_kernel(rows, place, in_ref, out_ref):
    cols = 2 * rows
    out_ref[:, :, 3 * rows :] = jnp.zeros((8, rows, out_ref.shape[2] - 3 * rows), BF)
    for f in range(4):
        for y in range(2):
            out_ref[f * 2 + y, :, :rows] = in_ref[y * rows : (y + 1) * rows, f * rows : (f + 1) * rows]
            out_ref[f * 2 + y, :, rows : 3 * rows] = in_ref[
                (2 + f // 2) * rows : (3 + f // 2) * rows, f % 2 * cols : (f % 2 + 1) * cols
            ]


def mlp_join_kernel(rows, place, got_ref, fc1_ref, fc2_ref):
    for f in range(4):
        for y in range(2):
            at = (y * 4 + f) * rows
            fc1_ref[:, at : at + rows] = got_ref[f * 2 + y, :, :rows].astype(F32)
        fc2_ref[:, f * rows : (f + 1) * rows] = got_ref[f * 2 + place[AT_Y], :, rows : 3 * rows].astype(F32).T


def attn_split_kernel(rows, place, in_ref, out_ref):
    out_ref[...] = jnp.zeros_like(out_ref)
    for part in range(8):

        @pl.when(place[AT_G] == part)
        def _():
            for y in range(2):
                block = in_ref[y * rows : (y + 1) * rows]
                for t in range(3):
                    out_ref[(8 * t + part) // 6 * 2 + y, :, :rows] = block[:, t * rows : (t + 1) * rows]
                out_ref[part // 2 * 2 + y, :, rows : 2 * rows] = block[:, 3 * rows : 4 * rows]


def attn_join_kernel(rows, place, got_ref, qkv_ref, proj_ref):
    for y in range(2):
        proj_ref[:, y * rows : (y + 1) * rows] = got_ref[place[AT_F] * 2 + y, :, rows : 2 * rows].astype(F32)
    for to in range(4):

        @pl.when(place[AT_F] == to)
        def _():
            for k in range(6):
                qkv_ref[:, k * rows : (k + 1) * rows] = got_ref[(6 * to + k) % 8, :, :rows].astype(F32)


def output_kernel(place, b2_0, b2_1, b2_2, b2_3, tok_ref, after_ref, mask_ref, sel_ref, mod_ref, out_ref):
    branch = b2_0[...].astype(F32)
    for ref in (b2_1, b2_2, b2_3):
        branch = branch + ref[...].astype(F32)
    gate = mm(sel_ref[:, : mod_ref.shape[1]], mod_ref[5])
    tokens = tok_ref[...].astype(F32)
    out_ref[...] = jnp.where(mask_ref[...] == 1, tokens, after_ref[...] + gate * branch).astype(BF)


def input_grad_kernel(place, gin_0, gin_1, gin_2, gin_3, tok_ref, one_ref, cot_ref, mask_ref, sel_ref, mod_ref, grad_ref):
    grad_in = gin_0[...].astype(F32)
    for ref in (gin_1, gin_2, gin_3):
        grad_in = grad_in + ref[...].astype(F32)
    normed, inverse = normalize(tok_ref[...].astype(F32))
    scale = mm(sel_ref[:, : mod_ref.shape[1]], mod_ref[1])
    back = normalize_back(grad_in * (1.0 + scale), normed, inverse)
    grad_ref[...] = jnp.where(mask_ref[...] == 1, cot_ref[...].astype(F32), 0.0) + one_ref[...] + back


def slab_solution(mesh):
    names = ("x", "core", "z", "y")
    grid = Mesh(mesh.devices.reshape(2, 2, 4, 2), names)
    offsets = [(dc, dx, dy) for dc in range(2) for dx in range(2) for dy in range(2)]
    order = [dy == 1 for _, _, dy in offsets]
    group = ("x", "core", "y")
    table = [[0] * TABLE for _ in range(32)]
    for device, row in enumerate(table):
        x, c, z, y = device >> 4, (device >> 3) & 1, (device >> 1) & 3, device & 1
        f = x * 2 + c
        row[AT_F], row[AT_Y], row[AT_Z], row[AT_P], row[AT_G] = f, y, z, device & 7, f * 2 + y
        for slot, (dc, dx, dy) in enumerate(offsets):
            part = ((x ^ dx) * 2 + (c ^ dc)) * 2 + (y ^ dy)
            row[AT_PART + slot] = part
            row[AT_SLOT + part] = slot
        for piece in range(8):
            row[AT_SHARD + piece] = (z ^ (piece >> 1)) * 2 + (y ^ (piece & 1))
        for patch in range(8):
            row[AT_PIECE + patch] = ((patch & 1) ^ y) * 4 + (patch >> 1)

    def swap(a, axes):
        n = 2 ** len(axes)
        return lax.ppermute(a, axes, [(k, n - 1 - k) for k in range(n)])

    def from_z(a, apart):
        return lax.ppermute(a, ("z",), [(z, z ^ apart) for z in range(4)])

    def over(a, dx, dy):
        axes = (("x",) if dx else ()) + (("y",) if dy else ())
        return swap(a, axes) if axes else a

    def gather_near(a):
        return [over(a, dx, dy) for dx in range(2) for dy in range(2)]

    def gather_slots(a):
        mine = gather_near(a)
        return mine + [swap(piece, ("core",)) for piece in mine]

    def over_z(a):
        return [a] + [from_z(a, apart) for apart in (1, 2, 3)]

    def to_slab(a):
        return lax.all_to_all(jnp.broadcast_to(a, (8, *a.shape)), group, 0, 0, tiled=True)

    def core_sum(own, far):
        received = swap(far, ("core",))
        return [(own[slot].astype(F32) + received[slot].astype(F32)).astype(BF) for slot in range(4)]

    def scatter_sum(own, far):
        return [over(total, slot // 2, slot % 2) for slot, total in enumerate(core_sum(own, far))]

    def exchange(slots):
        moved = []
        for slot, offset in zip(slots, offsets):
            axes = tuple(axis for axis, apart in zip(("x", "core", "y"), (offset[1], offset[0], offset[2])) if apart)
            moved.append(swap(slot, axes) if axes else slot)
        return moved

    def local(tokens, image_mask, sample_index, condition, ada_weight, ada_bias, qkv_weight, qkv_bias,
              proj_weight, proj_bias, fc1_weight, fc1_bias, fc2_weight, fc2_bias, cotangent):
        frames, columns, d = tokens.shape
        T = frames * columns
        S = 8 * T
        TB = 2 * T
        samples = condition.shape[0]
        rows = ada_weight.shape[0]
        ff = fc1_weight.shape[1]
        width = d // 8
        part_ff = ff // 8
        cols = 2 * width
        me = lax.axis_index(names).astype(jnp.uint32)
        place = lax.dynamic_slice(jnp.array(table, jnp.int32), (me, jnp.uint32(0)), (1, TABLE)).reshape(TABLE)

        def shaped(shape, dtype=F32):
            return jax.ShapeDtypeStruct(shape, dtype)

        def rows_at(w):
            return pl.BlockSpec((TB, w), lambda j, *_: (j, 0))

        def lanes_at(h):
            return pl.BlockSpec((h, TB), lambda j, *_: (0, j))

        token_specs = [
            pl.BlockSpec((2, 2 * T + 16, d), lambda j, *_: (jnp.minimum(j, 1), 0, 0)),
            pl.BlockSpec((2, 2 * T + 16, d), lambda j, *_: (jnp.maximum(j - 2, 0), 0, 0)),
        ]

        def call(name, us, kernel, arrays, outs, steps=1, ins=None, specs=None, scratch=()):
            return pl.pallas_call(
                kernel,
                grid_spec=pltpu.PrefetchScalarGridSpec(
                    num_scalar_prefetch=1,
                    grid=(steps,),
                    in_specs=ins or [whole(array.shape) for array in arrays],
                    out_specs=specs or [whole(out.shape) for out in outs],
                    scratch_shapes=list(scratch),
                ),
                out_shape=outs,
                compiler_params=params(),
                cost_estimate=takes(us),
                name=name,
            )(place, *arrays)

        def lines(bias):
            return bias.reshape(-1, 128)

        flat_tokens = tokens.reshape(T, d)
        flat_cot = cotangent.reshape(T, d)
        mask = image_mask.reshape(T, 1)

        (partial_mod, act_rows, silu_slope, qkv_mine, fc1_mine, send, fc2_rows, slab_rows) = call(
            "prepare",
            6,
            functools.partial(prepare_kernel, d),
            [condition, ada_weight, qkv_weight, fc1_weight, proj_weight, fc2_weight, flat_tokens, flat_cot, sample_index.T, image_mask.T],
            [
                shaped((8, 8, d), BF),
                shaped((samples, wide(rows)), BF),
                shaped((samples, wide(rows))),
                shaped((rows, wide(3 * width)), BF),
                shaped((rows, wide(part_ff)), BF),
                shaped((rows, wide(part_ff) + wide(3 * width)), BF),
                shaped((rows, wide(d + cols)), BF),
                shaped((2 * T + 16, d), BF),
            ],
            scratch=[pltpu.VMEM((samples, rows), F32)],
        )

        fc2_in = lax.all_gather(fc2_rows, "z", axis=0)
        mod_terms = lax.all_to_all(partial_mod, ("z", "y"), 0, 0, tiled=True)
        got = swap(send, ("y",))
        qkv_pair = jnp.stack([qkv_mine, got[:, wide(part_ff) :]])
        fc1_pair = jnp.stack([fc1_mine, got[:, : wide(part_ff)]])
        mod_terms, qkv_pair, fc1_pair, slab_rows = lax.optimization_barrier((mod_terms, qkv_pair, fc1_pair, slab_rows))
        qkv_pair, fc2_in = lax.optimization_barrier((qkv_pair, fc2_in))
        qkv_in = lax.all_gather(qkv_pair, "z", axis=0)
        (mod_chunk,) = call(
            "mod_sum",
            2,
            mod_sum_kernel,
            [mod_terms, lines(ada_bias)],
            [shaped((8, d), BF)],
        )
        chunks = over_z(mod_chunk)
        tok_mine = gather_near(slab_rows)
        chunks, tok_mine = lax.optimization_barrier((chunks, tok_mine))
        mod_in = to_slab(jnp.stack(chunks))
        tok_near = jnp.stack(tok_mine)
        tok_far = swap(tok_near, ("core",))
        proj_slots = gather_slots(fc2_in[:, :, d : d + cols])
        (proj_all,) = call(
            "proj",
            3,
            functools.partial(proj_kernel, d),
            proj_slots,
            [shaped((d, d), BF)],
            scratch=[pltpu.VMEM((8, 4, rows, cols), BF)],
        )
        mod_in, tok_near, tok_far, qkv_in, fc1_pair, proj_all = lax.optimization_barrier(
            (mod_in, tok_near, tok_far, qkv_in, fc1_pair, proj_all)
        )
        fc1_in = lax.all_gather(fc1_pair, "z", axis=0)
        attn_t, qkv, sel, selt, w_qkv, mod = call(
            "attend",
            13,
            functools.partial(attend_kernel, d, width, columns),
            [tok_near, tok_far, qkv_in, mod_in, lines(qkv_bias)],
            [
                shaped((width, S), BF),
                shaped((S, wide(3 * width)), BF),
                shaped((S, 128), BF),
                shaped((samples, S), BF),
                shaped((d, wide(3 * width)), BF),
                shaped((6, samples, d), BF),
            ],
            steps=4,
            ins=token_specs
            + [whole(array.shape) for array in (qkv_in, mod_in, lines(qkv_bias))],
            specs=[
                lanes_at(width),
                rows_at(wide(3 * width)),
                rows_at(128),
                lanes_at(samples),
                whole((d, wide(3 * width))),
                whole((6, samples, d)),
            ],
            scratch=[pltpu.VMEM((1, 3 * width), F32)],
        )
        attn_slots = gather_slots(attn_t)

        def slot_spec(dc, dx):
            return pl.BlockSpec((width, TB), lambda j, *_: (0, lax.bitwise_xor(j, dc * 2 + dx)))

        slot_specs = [slot_spec(dc, dx) for dc, dx, _ in offsets]
        own_out = pl.BlockSpec((2, T, d), lambda j, *_: (jnp.minimum(j, 1), 0, 0))
        far_out = pl.BlockSpec((2, T, d), lambda j, *_: (jnp.maximum(j - 2, 0), 0, 0))
        half_shape = shaped((4, T, d), BF)

        mlp_rest = [mod, proj_all, lines(proj_bias), fc1_in, lines(fc1_bias), fc2_in, lines(fc2_bias)]
        (b2_own, b2_far, gm_own, gm_far, fcg, fc1_bias_g, fc2_bias_g, modg_two, after_own, branch_own) = call(
            "mlp",
            32,
            functools.partial(mlp_kernel, d, order),
            [*attn_slots, tok_near, tok_far, sel, selt, *mlp_rest],
            [
                half_shape,
                half_shape,
                half_shape,
                half_shape,
                shaped((16 * rows, wide(part_ff)), BF),
                shaped((1, part_ff)),
                shaped((1, d)),
                shaped((3, samples, d)),
                shaped((T, d)),
                shaped((T, d)),
            ],
            steps=4,
            ins=slot_specs
            + token_specs
            + [rows_at(128), lanes_at(samples)]
            + [whole(array.shape) for array in mlp_rest],
            specs=[
                own_out,
                far_out,
                own_out,
                far_out,
                whole((16 * rows, wide(part_ff))),
                whole((1, part_ff)),
                whole((1, d)),
                whole((3, samples, d)),
                whole((T, d)),
                whole((T, d)),
            ],
            scratch=[
                pltpu.VMEM((d, part_ff), F32),
                pltpu.VMEM((part_ff, d), F32),
                pltpu.VMEM((d, part_ff), BF),
                pltpu.VMEM((part_ff, d), BF),
                pltpu.VMEM((1, d), F32),
                pltpu.VMEM((1, part_ff), F32),
                pltpu.VMEM((1, d), F32),
            ],
        )

        fc_z = lax.psum_scatter(fcg, "z", scatter_dimension=0, tiled=True)
        gm_terms = scatter_sum(gm_own, gm_far)

        *ex_slots, grad_one, modg_gate, proj_bias_g = call(
            "middle",
            6,
            functools.partial(middle_kernel, d, len(gm_terms)),
            [*gm_terms, after_own, branch_own, slab_rows, sel, selt, mod, proj_all],
            [shaped((2, width, T), BF)] * 8 + [shaped((T, d)), shaped((samples, d)), shaped((1, d))],
            ins=[whole((T, d))] * (len(gm_terms) + 3)
            + [whole((T, 128)), whole((samples, T)), whole(mod.shape), whole((d, d))],
            scratch=[pltpu.VMEM((d, T), F32)],
        )
        grad_attn = exchange(ex_slots)
        b2_sums = core_sum(b2_own, b2_far)
        grad_attn, b2_sums = lax.optimization_barrier((grad_attn, b2_sums))
        b2_terms = [over(total, slot // 2, slot % 2) for slot, total in enumerate(b2_sums)]

        back_rest = [w_qkv, modg_two, modg_gate, proj_bias_g, fc1_bias_g, fc2_bias_g]
        gin_own, gin_far, grad_qkv, attn_in, to_sum = call(
            "back",
            22,
            functools.partial(back_kernel, d, width, columns),
            [*grad_attn, tok_near, tok_far, sel, selt, mod, qkv, *back_rest],
            [half_shape, half_shape, shaped((S, wide(3 * width)), BF), shaped((S, d), BF), shaped((32, 8, d), BF)],
            steps=4,
            ins=[whole((2, width, T))] * 8
            + token_specs
            + [rows_at(128), lanes_at(samples), whole(mod.shape), rows_at(wide(3 * width))]
            + [whole(array.shape) for array in back_rest],
            specs=[own_out, far_out, rows_at(wide(3 * width)), rows_at(d), whole((32, 8, d))],
            scratch=[
                pltpu.VMEM((8, 2, width, T), BF),
                pltpu.VMEM((2, samples, d), F32),
                pltpu.VMEM((1, 3 * width), F32),
            ],
        )
        gin_own, gin_far, grad_qkv, attn_in, to_sum, b2_terms = lax.optimization_barrier(
            (gin_own, gin_far, grad_qkv, attn_in, to_sum, b2_terms)
        )
        gin_terms = scatter_sum(gin_own, gin_far)
        (attn_g,) = call(
            "weights",
            8,
            functools.partial(weights_kernel, d, width, order),
            [*attn_slots, *grad_attn, grad_qkv, attn_in],
            [shaped((d, wide(4 * width)), BF)],
            steps=4,
            ins=slot_specs + [whole((2, width, T))] * 8 + [rows_at(wide(3 * width)), rows_at(d)],
            specs=[whole((d, wide(4 * width)))],
            scratch=[
                pltpu.VMEM((d, 3 * width), F32),
                pltpu.VMEM((d, width), F32),
                pltpu.VMEM((8, width, T), BF),
            ],
        )
        terms = lax.all_to_all(to_sum, names, 0, 0, tiled=True)
        attn_g, terms, fc_z, gin_terms = lax.optimization_barrier((attn_g, terms, fc_z, gin_terms))
        (mlp_send,) = call(
            "mlp_split", 3, functools.partial(mlp_split_kernel, rows), [fc_z], [shaped((8, rows, wide(3 * rows)), BF)]
        )
        mlp_got = lax.all_to_all(mlp_send, group, 0, 0, tiled=True)
        attn_z = lax.psum_scatter(attn_g, "z", scatter_dimension=0, tiled=True)

        (sums,) = call("grad_sum", 2, grad_sum_kernel, [terms], [shaped((8, d), BF)])
        sums, mlp_got = lax.optimization_barrier((over_z(sums), mlp_got))
        total = to_slab(jnp.stack(sums))

        (ada_weight_grad, condition_grad, ada_bias_grad, qkv_bias_grad, proj_bias_grad, fc1_bias_grad, fc2_bias_grad) = call(
            "ada",
            5,
            functools.partial(ada_kernel, d),
            [total, act_rows, silu_slope, ada_weight],
            [shaped((rows, 6 * d)), shaped((samples, rows))]
            + [shaped((n // 128, 128)) for n in (6 * d, 2 * d, d, ff, d)],
        )

        own_specs = [whole((T, 1)), whole((T, 128)), whole(mod.shape)]
        (result,) = call(
            "output",
            3,
            output_kernel,
            [*b2_terms, flat_tokens, after_own, mask, sel, mod],
            [shaped((T, d), BF)],
            ins=[whole((T, d))] * 6 + own_specs,
        )
        attn_z, result = lax.optimization_barrier((attn_z, result))
        (attn_send,) = call(
            "attn_split", 3, functools.partial(attn_split_kernel, rows), [attn_z], [shaped((8, rows, wide(2 * rows)), BF)]
        )
        attn_got = lax.all_to_all(attn_send, group, 0, 0, tiled=True)
        mlp_got = lax.optimization_barrier((mlp_got, attn_send))[0]
        fc1_weight_grad, fc2_weight_grad = call(
            "mlp_join",
            3,
            functools.partial(mlp_join_kernel, rows),
            [mlp_got],
            [shaped((rows, ff // 4)), shaped((d // 4, 4 * rows))],
        )
        gin_terms = lax.optimization_barrier((gin_terms, attn_send))[0]
        (input_grad,) = call(
            "input_grad",
            3,
            input_grad_kernel,
            [*gin_terms, flat_tokens, grad_one, flat_cot, mask, sel, mod],
            [shaped((T, d))],
            ins=[whole((T, d))] * 7 + own_specs,
        )
        qkv_weight_grad, proj_weight_grad = call(
            "attn_join",
            3,
            functools.partial(attn_join_kernel, rows),
            [attn_got],
            [shaped((rows, 3 * d // 4)), shaped((rows, d // 4))],
        )

        shape = (frames, columns, d)
        return (
            result.reshape(shape),
            input_grad.reshape(shape),
            condition_grad,
            ada_weight_grad,
            ada_bias_grad.reshape(-1),
            qkv_weight_grad,
            qkv_bias_grad.reshape(-1),
            proj_weight_grad,
            proj_bias_grad.reshape(-1),
            fc1_weight_grad,
            fc1_bias_grad.reshape(-1),
            fc2_weight_grad.T,
            fc2_bias_grad.reshape(-1),
        )

    frame, patch = ("x", "core"), ("z", "y")
    token_spec, number_spec = P(None, names, None), P(None, names)
    row_spec, both_spec = P(patch, None), P(patch, frame)
    return jax.shard_map(
        local,
        mesh=grid,
        in_specs=(
            token_spec, number_spec, number_spec, P(), row_spec, P(), row_spec, P(), row_spec, P(), row_spec, P(),
            row_spec, P(), token_spec,
        ),
        out_specs=(
            token_spec, token_spec, P(None, patch), row_spec, P(), both_spec, P(), both_spec, P(), both_spec, P(),
            both_spec, P(),
        ),
        check_vma=False,
    )


def solution(mesh):
    if (mesh.shape["frame"], mesh.shape["patch"]) == (4, 8):
        return slab_solution(mesh)
    return general_solution(mesh)
```

```python
import functools

import jax
import jax.numpy as jnp
from jax import lax
from jax.experimental import pallas as pl
from jax.experimental.pallas import tpu as pltpu
from jax.sharding import Mesh, PartitionSpec as P

HEAD_DIM = 72
EPSILON = 1e-06
SCORE_SCALE = HEAD_DIM**-0.5
GELU_C = 0.7978845608028654
GELU_A = 0.044715
VMEM_BYTES = 56 * 1024 * 1024
(AT_F, AT_Y, AT_Z, AT_P, AT_G) = range(5)
AT_PART, AT_SLOT, AT_SHARD, AT_PIECE, TABLE = 8, 16, 24, 32, 40
BF = jnp.bfloat16
F32 = jnp.float32


def mm(a, b, ca=1, cb=0):
    return lax.dot_general(a, b, (((ca,), (cb,)), ((), ())), preferred_element_type=F32)


def normalize(values):
    centred = values - jnp.mean(values, axis=-1, keepdims=True)
    inverse = lax.rsqrt(jnp.mean(centred * centred, axis=-1, keepdims=True) + EPSILON)
    return centred * inverse, inverse


def normalize_back(grad_normed, normed, inverse):
    return inverse * (
        grad_normed
        - jnp.mean(grad_normed, axis=-1, keepdims=True)
        - normed * jnp.mean(grad_normed * normed, axis=-1, keepdims=True)
    )


def stack_rows(pieces):
    if pieces[0].shape[0] % 16 == 0:
        return jnp.concatenate(pieces, axis=0)
    return jnp.concatenate([piece.astype(F32) for piece in pieces], axis=0).astype(pieces[0].dtype)


def softmax_prob(queries, key_rows, same_column):
    grid = mm(queries, key_rows, 1, 1) * SCORE_SCALE
    grid = jnp.where(same_column, grid, -1e30)
    expanded = jnp.exp(grid - jnp.max(grid, axis=-1, keepdims=True))
    return expanded / jnp.sum(expanded, axis=-1, keepdims=True)


def column_mask(tokens_per_part, columns):
    rows = lax.broadcasted_iota(jnp.int32, (tokens_per_part, tokens_per_part), 0)
    cols = lax.broadcasted_iota(jnp.int32, (tokens_per_part, tokens_per_part), 1)
    return lax.rem(rows, columns) == lax.rem(cols, columns)


def slab_attention(refs, order, size):
    pieces = []
    for ref, swapped in zip(refs, order):
        piece = ref[...]
        if swapped:
            piece = jnp.concatenate([piece[:, size:], piece[:, :size]], axis=1)
        pieces.append(piece)
    return stack_rows(pieces)


def general_attend_kernel(d, width, columns, tok_ref, sel_ref, mod_ref, w_ref, bias_ref, out_ref, qkv_ref):
    normed, _ = normalize(tok_ref[...].astype(F32))
    sel = sel_ref[...]
    shift = mm(sel, mod_ref[:, 0:d])
    scale = mm(sel, mod_ref[:, d : 2 * d])
    attn_in = (normed * (1.0 + scale) + shift).astype(BF)
    qkv = (mm(attn_in, w_ref[...]) + bias_ref[...]).astype(BF)
    qkv_ref[...] = qkv
    size = tok_ref.shape[0] // 2
    same = column_mask(size, columns)
    for half in range(2):
        rows = slice(half * size, (half + 1) * size)
        parts = []
        for head in range(width // HEAD_DIM):
            q, k, v = (
                qkv[rows, t * width + head * HEAD_DIM : t * width + (head + 1) * HEAD_DIM]
                for t in range(3)
            )
            prob = softmax_prob(q, k, same)
            parts.append(mm(prob.astype(BF), v).T)
        out_ref[:, rows] = jnp.concatenate(parts, axis=0).astype(BF)


def general_mlp_kernel(d, order, *refs):
    n = len(order)
    slots = refs[:n]
    (tok_ref, cot_ref, sel_ref, selt_ref, mod_ref, proj_ref, projb_ref, fc1_ref, fc1b_ref, fc2_ref, fc2b_ref) = refs[n : n + 11]
    (b2_ref, gm_ref, fc1g_ref, fc2g_ref, fc1bg_ref, fc2bg_ref, modg_ref, after_ref, branch_ref, fc1a, fc2a) = refs[n + 11 :]
    step = pl.program_id(0)
    size = tok_ref.shape[0] // 2
    sel = sel_ref[...]
    selt = selt_ref[...]

    def mod(block):
        return mm(sel, mod_ref[:, block * d : (block + 1) * d])

    attn_t = slab_attention(slots, order, size)
    branch_one = mm(attn_t, proj_ref[...], 0, 0) + projb_ref[...]
    after_one = tok_ref[...].astype(F32) + mod(2) * branch_one

    @pl.when(step == 0)
    def _():
        after_ref[...] = after_one[:size]
        branch_ref[...] = branch_one[:size]
        fc1a[...] = jnp.zeros_like(fc1a)
        fc2a[...] = jnp.zeros_like(fc2a)
        fc1bg_ref[...] = jnp.zeros_like(fc1bg_ref)
        fc2bg_ref[...] = jnp.zeros_like(fc2bg_ref)
        modg_ref[...] = jnp.zeros_like(modg_ref)

    normed, _ = normalize(after_one)
    mlp_in = (normed * (1.0 + mod(4)) + mod(3)).astype(BF)
    pre = mm(mlp_in, fc1_ref[...]) + fc1b_ref[...]
    square = pre * pre
    tanh = jnp.tanh(GELU_C * pre * (1.0 + GELU_A * square))
    hidden = (0.5 * pre * (1.0 + tanh)).astype(BF)
    slope = 0.5 * (1.0 + tanh) + 0.5 * pre * (1.0 - tanh * tanh) * GELU_C * (1.0 + 3.0 * GELU_A * square)
    branch_two = mm(hidden, fc2_ref[...]) + fc2b_ref[...]
    b2_ref[...] = branch_two.astype(BF).reshape(b2_ref.shape)
    grad_two = cot_ref[...].astype(F32)
    grad_branch = mod(5) * grad_two
    gb2 = grad_branch.astype(BF)
    fc2bg_ref[...] += jnp.sum(gb2.astype(F32), axis=0, keepdims=True)
    fc2a[...] += mm(hidden, gb2, 0, 0)
    grad_pre = (mm(gb2, fc2_ref[...], 1, 1) * slope).astype(BF)
    fc1bg_ref[...] += jnp.sum(grad_pre.astype(F32), axis=0, keepdims=True)
    fc1a[...] += mm(mlp_in, grad_pre, 0, 0)
    grad_in = mm(grad_pre, fc1_ref[...], 1, 1)
    gm_ref[...] = grad_in.astype(BF).reshape(gm_ref.shape)
    modg_ref[0] += mm(selt, grad_in.astype(BF))
    modg_ref[1] += mm(selt, (grad_in * normed).astype(BF))
    modg_ref[2] += mm(selt, (grad_two * branch_two).astype(BF))

    @pl.when(step == pl.num_programs(0) - 1)
    def _():
        fc1g_ref[...] = fc1a[...].astype(BF)
        fc2g_ref[...] = fc2a[...].astype(BF)


def general_middle_kernel(d, n_parts, count, place_ref, *refs):
    grads = refs[:count]
    (after_ref, branch_ref, cot_ref, sel_ref, selt_ref, mod_ref, proj_ref) = refs[count : count + 7]
    (ex_ref, one_ref, modg_ref, pbias_ref) = refs[count + 7 :]
    sel = sel_ref[...]
    grad_in = grads[0][...].astype(F32)
    for ref in grads[1:]:
        grad_in = grad_in + ref[...].astype(F32)
    normed, inverse = normalize(after_ref[...])
    scale = mm(sel, mod_ref[:, 4 * d : 5 * d])
    gate = mm(sel, mod_ref[:, 2 * d : 3 * d])
    grad_one = cot_ref[...].astype(F32) + normalize_back(grad_in * (1.0 + scale), normed, inverse)
    one_ref[...] = grad_one
    modg_ref[...] = mm(selt_ref[...], (grad_one * branch_ref[...]).astype(BF))
    gb1 = (gate * grad_one).astype(BF)
    gb1_wide = gb1.astype(F32)
    pbias_ref[...] = jnp.sum(gb1_wide, axis=0, keepdims=True)
    width = d // n_parts
    grad_attn = mm(proj_ref[...], gb1, 1, 1)
    gb1_t = gb1_wide.T
    for part in range(n_parts):
        rows = slice(part * width, (part + 1) * width)
        ex_ref[part, 0] = grad_attn[rows].astype(BF)
        ex_ref[place_ref[part], 1] = gb1_t[rows].astype(BF)


def general_attend_back_kernel(d, width, columns, order, place_ref, *refs):
    n = len(order)
    slots = refs[:n]
    (ga_ref, tok_ref, sel_ref, selt_ref, mod_ref, w_ref, qkv_ref) = refs[n : n + 7]
    (gin_ref, qkvg_ref, projg_ref, bias_ref, modg_ref, qkva, proja) = refs[n + 7 :]
    step = pl.program_id(0)
    size = tok_ref.shape[0] // 2

    @pl.when(step == 0)
    def _():
        qkva[...] = jnp.zeros_like(qkva)
        proja[...] = jnp.zeros_like(proja)
        bias_ref[...] = jnp.zeros_like(bias_ref)
        modg_ref[...] = jnp.zeros_like(modg_ref)

    qkv = qkv_ref[...]
    same = column_mask(size, columns)
    heads = width // HEAD_DIM
    halves = []
    for half in range(2):
        rows = slice(half * size, (half + 1) * size)
        grad_mixed = ga_ref[half, 0].astype(F32).T
        pieces = [None] * (3 * heads)
        for head in range(heads):
            q, k, v = (
                qkv[rows, t * width + head * HEAD_DIM : t * width + (head + 1) * HEAD_DIM]
                for t in range(3)
            )
            grad = grad_mixed[:, head * HEAD_DIM : (head + 1) * HEAD_DIM].astype(BF)
            prob = softmax_prob(q, k, same)
            grad_prob = mm(grad, v, 1, 1)
            delta = jnp.sum(prob * grad_prob, axis=-1, keepdims=True)
            grad_score = (prob * (grad_prob - delta) * SCORE_SCALE).astype(BF)
            pieces[head] = mm(grad_score, k)
            pieces[heads + head] = mm(grad_score, q, 0, 0)
            pieces[2 * heads + head] = mm(prob.astype(BF), grad, 0, 0)
        halves.append(jnp.concatenate(pieces, axis=1))
    grad_qkv = jnp.concatenate(halves, axis=0).astype(BF)
    bias_ref[...] += jnp.sum(grad_qkv.astype(F32), axis=0, keepdims=True)

    sel = sel_ref[...]
    selt = selt_ref[...]
    normed, _ = normalize(tok_ref[...].astype(F32))
    shift = mm(sel, mod_ref[:, 0:d])
    scale = mm(sel, mod_ref[:, d : 2 * d])
    attn_in = (normed * (1.0 + scale) + shift).astype(BF)
    qkva[...] += mm(attn_in, grad_qkv, 0, 0)
    grad_in = mm(grad_qkv, w_ref[...], 1, 1)
    gin_ref[...] = grad_in.astype(BF).reshape(gin_ref.shape)
    modg_ref[0] += mm(selt, grad_in.astype(BF))
    modg_ref[1] += mm(selt, (grad_in * normed).astype(BF))

    attn_t = slab_attention(slots, order, size)
    gb1_t = jnp.concatenate([ga_ref[0, 1], ga_ref[1, 1]], axis=1)
    proja[...] += mm(attn_t, gb1_t, 1, 1)

    @pl.when(step == pl.num_programs(0) - 1)
    def _():
        qkvg_ref[...] = qkva[...].astype(BF)
        rows = d // n
        for part in range(n):
            projg_ref[place_ref[part]] = proja[part * rows : (part + 1) * rows].astype(BF)


def general_last_kernel(d, count, count_b, *refs):
    grads = refs[:count]
    branches = refs[count : count + count_b]
    (tok_ref, one_ref, after_ref, cot_ref, mask_ref, sel_ref, mod_ref) = refs[count + count_b : count + count_b + 7]
    (out_ref, grad_ref) = refs[count + count_b + 7 :]
    sel = sel_ref[...]
    masked = mask_ref[...] == 1
    tokens = tok_ref[...].astype(F32)
    grad_in = grads[0][...].astype(F32)
    for ref in grads[1:]:
        grad_in = grad_in + ref[...].astype(F32)
    normed, inverse = normalize(tokens)
    scale = mm(sel, mod_ref[:, d : 2 * d])
    back = normalize_back(grad_in * (1.0 + scale), normed, inverse)
    grad_ref[...] = jnp.where(masked, cot_ref[...].astype(F32), 0.0) + one_ref[...] + back
    branch = branches[0][...].astype(F32)
    for ref in branches[1:]:
        branch = branch + ref[...].astype(F32)
    gate = mm(sel, mod_ref[:, 5 * d : 6 * d])
    out_ref[...] = jnp.where(masked, tokens, after_ref[...] + gate * branch).astype(BF)


def params(steps=1):
    return pltpu.CompilerParams(vmem_limit_bytes=VMEM_BYTES, dimension_semantics=("arbitrary",) * steps)


def cost(flops, bytes_accessed):
    return pl.CostEstimate(flops=int(flops), bytes_accessed=int(bytes_accessed), transcendentals=0)


def whole(shape):
    return pl.BlockSpec(shape, lambda *_: (0,) * len(shape))


def matchings(frames):
    left = {f: {t: (frames * t + f) // 3 for t in range(3)} for f in range(frames)}
    rounds = []
    for _ in range(3):
        taken = {}

        def place(f, seen):
            for t, to in left[f].items():
                if to in seen:
                    continue
                seen.add(to)
                if to not in taken or place(taken[to][0], seen):
                    taken[to] = (f, t)
                    return True
            return False

        for f in range(frames):
            place(f, set())
        chosen = {f: (t, to) for to, (f, t) in taken.items()}
        for f, (t, _to) in chosen.items():
            del left[f][t]
        rounds.append(chosen)
    return rounds


def general_solution(mesh):
    F, N = mesh.shape["frame"], mesh.shape["patch"]
    C, Y = 2, 2
    X, Z = F // C, N // Y
    G = X * C * Y
    half_slots = X * Y
    grid = Mesh(mesh.devices.reshape(X, C, Z, Y), ("x", "core", "z", "y"))
    everywhere = ("x", "core", "z", "y")
    offsets = [(dc, dx, dy) for dc in range(C) for dx in range(X) for dy in range(Y)]

    def from_xy(a, dx, dy):
        if dx == 0 and dy == 0:
            return a
        pairs = [
            (x * Y + y, ((x - dx) % X) * Y + (y - dy) % Y) for x in range(X) for y in range(Y)
        ]
        return lax.ppermute(a, ("x", "y"), pairs)

    def to_xy(a, dx, dy):
        return from_xy(a, (-dx) % X, (-dy) % Y)

    def swap_core(a):
        return lax.ppermute(a, "core", [(0, 1), (1, 0)])

    def swap_y(a):
        return lax.ppermute(a, "y", [(0, 1), (1, 0)])

    def gather_slots(a):
        mine = [from_xy(a, dx, dy) for dx in range(X) for dy in range(Y)]
        return mine + [swap_core(piece) for piece in mine]

    def scatter_sum(slots):
        received = swap_core(slots[half_slots:])
        terms = []
        for slot in range(half_slots):
            total = slots[slot].astype(F32) + received[slot].astype(F32)
            terms.append(to_xy(total.astype(BF), slot // Y, slot % Y))
        return terms

    def exchange(slots):
        received = swap_core(slots[half_slots:])
        pieces = [None] * G
        for slot in range(half_slots):
            dx, dy = slot // Y, slot % Y
            pair = to_xy(jnp.stack([slots[slot], received[slot]]), dx, dy)
            source = ((-dx) % X) * Y + (-dy) % Y
            pieces[source] = pair[0]
            pieces[half_slots + source] = pair[1]
        return jnp.stack(pieces)

    def local(tokens, image_mask, sample_index, condition, ada_weight, ada_bias, qkv_weight, qkv_bias,
              proj_weight, proj_bias, fc1_weight, fc1_bias, fc2_weight, fc2_bias, cotangent):
        frames, columns, d = tokens.shape
        T = frames * columns
        S = G * T
        samples = condition.shape[0]
        rows_here = ada_weight.shape[0]
        ff = fc1_weight.shape[1]
        width = d // G
        unit = ff // (N * F)
        part_ff = Z * unit
        x_i, c_i = lax.axis_index("x"), lax.axis_index("core")
        z_i, y_i = lax.axis_index("z"), lax.axis_index("y")
        f_i = x_i * C + c_i
        p_i = z_i * Y + y_i
        g_i = f_i * Y + y_i
        parts_at = [
            (((x_i + dx) % X) * C + (c_i + dc) % C) * Y + (y_i + dy) % Y for dc, dx, dy in offsets
        ]
        parts_at = jnp.stack(parts_at).astype(jnp.int32)
        all_parts = jnp.arange(G, dtype=jnp.int32)
        part_x, part_c, part_y = all_parts // (C * Y), (all_parts // Y) % C, all_parts % Y
        place = ((part_c - c_i) % C) * half_slots + ((part_x - x_i) % X) * Y + (part_y - y_i) % Y
        place = place.astype(jnp.int32)

        def y_pair(own, other):
            got = swap_y(other)
            return jnp.where(y_i == 0, jnp.stack([own, got]), jnp.stack([got, own]))

        pair_width = Y * width
        qkv_cols = [
            lax.dynamic_slice_in_dim(qkv_weight, t * d + f_i * pair_width, pair_width, 1) for t in range(3)
        ]

        def qkv_for(which):
            return jnp.concatenate(
                [lax.dynamic_slice_in_dim(c, which * width, width, 1) for c in qkv_cols], axis=1
            )

        qkv_rows = y_pair(qkv_for(y_i), qkv_for(1 - y_i)).reshape(Y * rows_here, 3 * width)
        w_qkv = lax.all_gather(qkv_rows, "z", axis=0, tiled=True)
        half_rows = rows_here // C
        proj_half = lax.dynamic_slice_in_dim(proj_weight, c_i * half_rows, half_rows, 0)
        proj_rows = y_pair(proj_half, proj_half).reshape(Y * half_rows, d)
        proj_mine = lax.all_gather(proj_rows, "z", axis=0, tiled=True)
        proj_other = swap_core(proj_mine)
        proj_both = jnp.where(
            c_i == 0, jnp.stack([proj_mine, proj_other]), jnp.stack([proj_other, proj_mine])
        )
        proj_parts = (
            proj_both.reshape(C, N, half_rows, d).transpose(1, 0, 2, 3).reshape(G, width, d)
        )
        proj_rel = jnp.concatenate(
            [lax.dynamic_index_in_dim(proj_parts, parts_at[r], 0, keepdims=False) for r in range(G)],
            axis=0,
        )

        def fc1_for(which):
            return jnp.concatenate(
                [
                    lax.dynamic_slice_in_dim(
                        fc1_weight, (z * Y + which) * (F * unit) + f_i * unit, unit, 1
                    )
                    for z in range(Z)
                ],
                axis=1,
            )

        fc1_rows = y_pair(fc1_for(y_i), fc1_for(1 - y_i)).reshape(Y * rows_here, part_ff)
        w_fc1 = lax.all_gather(fc1_rows, "z", axis=0, tiled=True)
        fc2_rows = lax.dynamic_slice_in_dim(fc2_weight, f_i * unit, unit, 0)
        w_fc2 = lax.all_gather(fc2_rows, "z", axis=0, tiled=True)

        chunk = samples * 6 * d // (F * N)
        per_row = 6 * d // chunk
        frame_samples = samples // F
        first_row = p_i * rows_here
        cond_rows = lax.dynamic_slice_in_dim(condition, first_row, rows_here, 1).astype(F32)
        sigmoid = 1.0 / (1.0 + jnp.exp(-cond_rows))
        act_rows = (cond_rows * sigmoid).astype(BF)
        silu_slope = sigmoid * (1.0 + cond_rows * (1.0 - sigmoid))
        act_mine = lax.dynamic_slice_in_dim(act_rows, f_i * frame_samples, frame_samples, 0)
        partial_mod = mm(act_mine, ada_weight).reshape(N, chunk)
        mod_terms = lax.all_to_all(partial_mod, ("z", "y"), 0, 0, tiled=True)
        bias_here = lax.dynamic_slice_in_dim(ada_bias, (p_i % per_row) * chunk, chunk, 0)
        mod_chunk = (jnp.sum(mod_terms, axis=0) + bias_here.astype(F32)).astype(BF)
        mod = lax.all_to_all(
            jnp.broadcast_to(mod_chunk, (F * N, chunk)), everywhere, 0, 0, tiled=True
        ).reshape(samples, 6 * d)

        flat_tokens = tokens.reshape(T, d)
        flat_cot = cotangent.reshape(T, d)
        mask = image_mask.reshape(T, 1)
        grad_two_own = jnp.where(mask == 1, jnp.zeros_like(flat_cot), flat_cot)
        codes = jnp.zeros((16, d), BF).at[0, :T].set(sample_index.reshape(T).astype(BF))
        token_slots = gather_slots(jnp.concatenate([flat_tokens, codes], axis=0))
        slab_tokens = jnp.concatenate([piece[:T] for piece in token_slots], axis=0)
        slab_codes = jnp.stack([piece[T, :T] for piece in token_slots]).astype(jnp.int32)
        slab_cot = jnp.concatenate(gather_slots(grad_two_own), axis=0)
        numbers = jnp.arange(samples, dtype=jnp.int32)
        selt = (slab_codes.reshape(1, S) == numbers[:, None]).astype(BF)
        sel = (slab_codes.reshape(S, 1) == numbers[None, :]).astype(BF)
        sel_own, selt_own = sel[:T], selt[:, :T]

        steps = G // 2
        TB = 2 * T
        row_block = lambda w: pl.BlockSpec((TB, w), lambda j: (j, 0))
        lane_block = lambda h: pl.BlockSpec((h, TB), lambda j: (0, j))

        bias_q = lax.dynamic_slice_in_dim(qkv_bias, g_i * width, width, 0)
        bias_v = lax.dynamic_slice_in_dim(qkv_bias, d + g_i * width, width, 0)
        bias_qkv = jnp.concatenate([bias_q, jnp.zeros_like(bias_q), bias_v]).astype(F32)[None]
        attn_t, qkv = pl.pallas_call(
            functools.partial(general_attend_kernel, d, width, columns),
            grid=(steps,),
            in_specs=[
                row_block(d),
                row_block(samples),
                whole((samples, 6 * d)),
                whole((d, 3 * width)),
                whole((1, 3 * width)),
            ],
            out_specs=[lane_block(width), row_block(3 * width)],
            out_shape=[
                jax.ShapeDtypeStruct((width, S), BF),
                jax.ShapeDtypeStruct((S, 3 * width), BF),
            ],
            compiler_params=params(),
            cost_estimate=cost(2 * S * d * 3 * width * 2, 8e6),
            name="attend",
        )(slab_tokens, sel, mod, w_qkv, bias_qkv)

        attn_slots = gather_slots(attn_t)
        order = [dy == 1 for _, _, dy in offsets]

        def slot_spec(dc, dx):
            return pl.BlockSpec(
                (width, TB),
                lambda j: (0, ((j // X + C - dc) % C) * X + (j % X + X - dx) % X),
            )

        slot_specs = [slot_spec(dc, dx) for dc, dx, _ in offsets]

        hidden_at = lambda v: jnp.concatenate(
            [
                lax.dynamic_slice_in_dim(v, (z * Y + y_i) * (F * unit) + f_i * unit, unit, 0)
                for z in range(Z)
            ]
        )
        fc1_bias_part = hidden_at(fc1_bias).astype(F32)[None]
        fc2_bias_once = jnp.where(g_i == 0, fc2_bias.astype(F32), 0.0)[None]
        slot_out = pl.BlockSpec((2, T, d), lambda j: (j, 0, 0))
        (b2_slots, gm_slots, fc1g, fc2g, fc1_bias_g, fc2_bias_g, modg_two, after_own, branch_own) = pl.pallas_call(
            functools.partial(general_mlp_kernel, d, order),
            grid=(steps,),
            in_specs=slot_specs
            + [
                row_block(d),
                row_block(d),
                row_block(samples),
                lane_block(samples),
                whole((samples, 6 * d)),
                whole((d, d)),
                whole((1, d)),
                whole((d, part_ff)),
                whole((1, part_ff)),
                whole((part_ff, d)),
                whole((1, d)),
            ],
            out_specs=[
                slot_out,
                slot_out,
                whole((d, part_ff)),
                whole((part_ff, d)),
                whole((1, part_ff)),
                whole((1, d)),
                whole((3, samples, d)),
                whole((T, d)),
                whole((T, d)),
            ],
            out_shape=[
                jax.ShapeDtypeStruct((G, T, d), BF),
                jax.ShapeDtypeStruct((G, T, d), BF),
                jax.ShapeDtypeStruct((d, part_ff), BF),
                jax.ShapeDtypeStruct((part_ff, d), BF),
                jax.ShapeDtypeStruct((1, part_ff), F32),
                jax.ShapeDtypeStruct((1, d), F32),
                jax.ShapeDtypeStruct((3, samples, d), F32),
                jax.ShapeDtypeStruct((T, d), F32),
                jax.ShapeDtypeStruct((T, d), F32),
            ],
            scratch_shapes=[pltpu.VMEM((d, part_ff), F32), pltpu.VMEM((part_ff, d), F32)],
            compiler_params=params(),
            cost_estimate=cost(2 * S * (d * d + 6 * d * part_ff), 3e7),
            name="mlp",
        )(
            *attn_slots,
            slab_tokens,
            slab_cot,
            sel,
            selt,
            mod,
            proj_rel,
            proj_bias.astype(F32)[None],
            w_fc1,
            fc1_bias_part,
            w_fc2,
            fc2_bias_once,
        )

        fc1_z = lax.psum_scatter(fc1g, "z", scatter_dimension=0, tiled=True)
        fc2_z = lax.psum_scatter(fc2g, "z", scatter_dimension=0, tiled=True)
        gm_terms = scatter_sum(gm_slots)

        ex_slots, grad_one, modg_gate, proj_bias_g = pl.pallas_call(
            functools.partial(general_middle_kernel, d, G, len(gm_terms)),
            grid_spec=pltpu.PrefetchScalarGridSpec(
                num_scalar_prefetch=1,
                grid=(1,),
                in_specs=[whole((T, d))] * len(gm_terms)
                + [
                    whole((T, d)),
                    whole((T, d)),
                    whole((T, d)),
                    whole((T, samples)),
                    whole((samples, T)),
                    whole((samples, 6 * d)),
                    whole((d, d)),
                ],
                out_specs=[
                    whole((G, 2, width, T)),
                    whole((T, d)),
                    whole((samples, d)),
                    whole((1, d)),
                ],
            ),
            out_shape=[
                jax.ShapeDtypeStruct((G, 2, width, T), BF),
                jax.ShapeDtypeStruct((T, d), F32),
                jax.ShapeDtypeStruct((samples, d), F32),
                jax.ShapeDtypeStruct((1, d), F32),
            ],
            compiler_params=params(),
            cost_estimate=cost(4 * T * d * d, 8e6),
            name="middle",
        )(place, *gm_terms, after_own, branch_own, grad_two_own, sel_own, selt_own, mod, proj_rel)

        grad_attn = exchange(ex_slots)
        b2_terms = scatter_sum(b2_slots)

        slot_back = [
            pl.BlockSpec(spec.block_shape, lambda j, place, spec=spec: spec.index_map(j))
            for spec in slot_specs
        ]
        rows_b = lambda w: pl.BlockSpec((TB, w), lambda j, place: (j, 0))
        gin_slots, qkvg, projg, qkv_bias_part, modg_one = pl.pallas_call(
            functools.partial(general_attend_back_kernel, d, width, columns, order),
            grid_spec=pltpu.PrefetchScalarGridSpec(
                num_scalar_prefetch=1,
                grid=(steps,),
                in_specs=slot_back
                + [
                    pl.BlockSpec((2, 2, width, T), lambda j, place: (j, 0, 0, 0)),
                    rows_b(d),
                    rows_b(samples),
                    pl.BlockSpec((samples, TB), lambda j, place: (0, j)),
                    whole((samples, 6 * d)),
                    whole((d, 3 * width)),
                    rows_b(3 * width),
                ],
                out_specs=[
                    pl.BlockSpec((2, T, d), lambda j, place: (j, 0, 0)),
                    whole((d, 3 * width)),
                    whole((G, width, width)),
                    whole((1, 3 * width)),
                    whole((2, samples, d)),
                ],
                scratch_shapes=[
                    pltpu.VMEM((d, 3 * width), F32),
                    pltpu.VMEM((d, width), F32),
                ],
            ),
            out_shape=[
                jax.ShapeDtypeStruct((G, T, d), BF),
                jax.ShapeDtypeStruct((d, 3 * width), BF),
                jax.ShapeDtypeStruct((G, width, width), BF),
                jax.ShapeDtypeStruct((1, 3 * width), F32),
                jax.ShapeDtypeStruct((2, samples, d), F32),
            ],
            compiler_params=params(),
            cost_estimate=cost(2 * S * d * 8 * width, 1.2e7),
            name="attend_back",
        )(parts_at, *attn_slots, grad_attn, slab_tokens, sel, selt, mod, w_qkv, qkv)

        gin_terms = scatter_sum(gin_slots)

        bias_total = 2 * d + d + ff + d
        biases = jnp.zeros((bias_total,), F32)
        put = lax.dynamic_update_slice_in_dim
        biases = put(biases, qkv_bias_part[0, :width], g_i * width, 0)
        biases = put(biases, qkv_bias_part[0, 2 * width :], d + g_i * width, 0)
        biases = put(biases, proj_bias_g[0], 2 * d, 0)
        for z in range(Z):
            biases = put(
                biases,
                fc1_bias_g[0, z * unit : (z + 1) * unit],
                3 * d + (z * Y + y_i) * (F * unit) + f_i * unit,
                0,
            )
        biases = put(biases, jnp.where(g_i == 0, fc2_bias_g[0], 0.0), 3 * d + ff, 0)
        mod_sums = jnp.concatenate(
            [modg_one[0], modg_one[1], modg_gate, modg_two[0], modg_two[1], modg_two[2]], axis=1
        )
        to_sum = jnp.concatenate(
            [mod_sums.reshape(F * N, chunk), biases.reshape(F * N, bias_total // (F * N))], axis=1
        ).astype(BF)
        terms = lax.all_to_all(to_sum, everywhere, 0, 0, tiled=True)
        summed = jnp.sum(terms.astype(F32), axis=0).astype(BF)
        total = lax.all_to_all(
            jnp.broadcast_to(summed, (F * N, summed.shape[0])), everywhere, 0, 0, tiled=True
        )
        mod_grad = total[:, :chunk].reshape(samples, 6 * d)
        bias_grad = total[:, chunk:].reshape(bias_total).astype(F32)
        ada_bias_grad = jnp.sum(mod_grad.astype(F32), axis=0)
        ada_weight_grad = mm(act_rows, mod_grad, 0, 0)
        condition_grad = mm(mod_grad, ada_weight, 1, 1) * silu_slope

        def y_join(rows):
            kept = lax.dynamic_index_in_dim(rows, y_i, 0, keepdims=False)
            got = swap_y(lax.dynamic_index_in_dim(rows, 1 - y_i, 0, keepdims=False))
            return jnp.where(y_i == 0, jnp.stack([kept, got]), jnp.stack([got, kept]))

        attn_g = jnp.concatenate([qkvg, projg.reshape(d, width)], axis=1)
        attn_z = lax.psum_scatter(attn_g, "z", scatter_dimension=0, tiled=True)
        attn_y = y_join(attn_z.reshape(Y, rows_here, 4 * width))
        blocks = jnp.stack(
            [
                jnp.concatenate([attn_y[y, :, t * width : (t + 1) * width] for y in range(Y)], axis=1)
                for t in range(4)
            ]
        )
        proj_weight_grad = blocks[3].astype(F32)
        moved = [None] * 3
        spots = jnp.zeros((3, F), jnp.int32)
        for turn, chosen in enumerate(matchings(F)):
            picks = jnp.array([chosen[f][0] for f in range(F)], jnp.int32)
            block = lax.dynamic_index_in_dim(blocks, picks[f_i], 0, keepdims=False)
            pairs = [(f, chosen[f][1]) for f in range(F)]
            if any(a != b for a, b in pairs):
                block = lax.ppermute(block, ("x", "core"), pairs)
            moved[turn] = block
            for f in range(F):
                t, to = chosen[f]
                spots = spots.at[(F * t + f) % 3, to].set(turn)
        moved = jnp.stack(moved)
        qkv_weight_grad = jnp.concatenate(
            [
                lax.dynamic_index_in_dim(moved, spots[k, f_i], 0, keepdims=False)
                for k in range(3)
            ],
            axis=1,
        ).astype(F32)

        fc1_y = y_join(fc1_z.reshape(Y, rows_here, part_ff))
        per_frame = Z // F
        fc1_send = fc1_y.reshape(Y, rows_here, F, per_frame, unit).transpose(2, 1, 3, 0, 4)
        fc1_got = lax.all_to_all(fc1_send, ("x", "core"), 0, 0, tiled=True)
        fc1_weight_grad = (
            fc1_got.transpose(1, 2, 3, 0, 4).reshape(rows_here, ff // F).astype(F32)
        )
        fc2_send = fc2_z.reshape(unit, F, d // F).transpose(1, 0, 2)
        fc2_got = lax.all_to_all(fc2_send, ("x", "core"), 0, 0, tiled=True)
        fc2_weight_grad = fc2_got.reshape(F * unit, d // F).astype(F32)

        result, input_grad = pl.pallas_call(
            functools.partial(general_last_kernel, d, len(gin_terms), len(b2_terms)),
            out_shape=[jax.ShapeDtypeStruct((T, d), BF), jax.ShapeDtypeStruct((T, d), F32)],
            compiler_params=pltpu.CompilerParams(vmem_limit_bytes=VMEM_BYTES),
            cost_estimate=cost(1e6, 5e6),
            name="last",
        )(*gin_terms, *b2_terms, flat_tokens, grad_one, after_own, flat_cot, mask, sel_own, mod)

        shape = (frames, columns, d)
        return (
            result.reshape(shape),
            input_grad.reshape(shape),
            condition_grad,
            ada_weight_grad,
            ada_bias_grad,
            qkv_weight_grad,
            bias_grad[: 2 * d],
            proj_weight_grad,
            bias_grad[2 * d : 3 * d],
            fc1_weight_grad,
            bias_grad[3 * d : 3 * d + ff],
            fc2_weight_grad,
            bias_grad[3 * d + ff :],
        )

    frame, patch = ("x", "core"), ("z", "y")
    every = ("x", "core", "z", "y")
    token_spec = P(None, every, None)
    number_spec = P(None, every)
    row_spec = P(patch, None)
    both_spec = P(patch, frame)
    return jax.shard_map(
        local,
        mesh=grid,
        in_specs=(
            token_spec, number_spec, number_spec, P(), row_spec, P(), row_spec, P(), row_spec, P(), row_spec, P(),
            row_spec, P(), token_spec,
        ),
        out_specs=(
            token_spec, token_spec, P(None, patch), row_spec, P(), both_spec, P(), both_spec, P(), both_spec, P(),
            both_spec, P(),
        ),
        check_vma=False,
    )


def takes(microseconds):
    return pl.CostEstimate(flops=1000, bytes_accessed=1000, transcendentals=0)


def wide(lanes):
    return -(-lanes // 128) * 128


def row_of(values):
    return jnp.concatenate([values[k : k + 1] for k in range(values.shape[0])], axis=1)


def put_row(ref, row):
    for k in range(ref.shape[0]):
        ref[k : k + 1] = row[:, k * 128 : (k + 1) * 128]


def pick(index, options):
    total = jnp.where(index == 0, options[0], 0.0)
    for k in range(1, len(options)):
        total = total + jnp.where(index == k, options[k], 0.0)
    return total


def spread(values, index, n):
    return jnp.concatenate([jnp.where(index == k, values, 0.0) for k in range(n)], axis=1)


def at_rows(index, rows):
    return pl.ds(pl.multiple_of(index * rows, rows), rows)


def prepare_kernel(d, place, cond_ref, ada_ref, qkv_ref, fc1_ref, proj_ref, fc2_ref, tok_ref, cot_ref, num_ref, mask_ref,
                   part_ref, act_ref, slope_ref, qkv_mine, fc1_mine, send_out, fc2_out, tok_out, act_all):
    rows = ada_ref.shape[0]
    cols = 2 * rows
    for ref in (qkv_mine, send_out, fc2_out):
        ref[...] = jnp.zeros_like(ref)
    act_ref[...] = jnp.zeros_like(act_ref)
    slope_ref[...] = jnp.zeros_like(slope_ref)
    for f in range(4):

        @pl.when(place[AT_F] == f)
        def _():
            fc2_out[:, d : d + cols] = proj_ref[:, f * cols : (f + 1) * cols]
            for y in range(2):
                for q_out, at_q, f_out, want in ((qkv_mine, 0, fc1_mine, y), (send_out, 512, send_out, 1 - y)):

                    @pl.when(place[AT_Y] == want)
                    def _():
                        for t in range(3):
                            at = t * d + (2 * f + y) * rows
                            q_out[:, at_q + t * rows : at_q + (t + 1) * rows] = qkv_ref[:, at : at + rows]
                        for z in range(4):
                            at = ((z * 2 + y) * 4 + f) * rows
                            kept = min(rows, 512 - z * rows)
                            f_out[:, z * rows : z * rows + kept] = fc1_ref[:, at : at + kept]
                            if kept < rows:
                                to = at_q + 3 * rows
                                q_out[:, to : to + rows - kept] = fc1_ref[:, at + kept : at + rows]

    fc2_out[:, :d] = fc2_ref[at_rows(place[AT_F], rows)]
    row = lax.broadcasted_iota(jnp.int32, (d, rows), 0)
    col = lax.broadcasted_iota(jnp.int32, (d, rows), 1)
    cond = mm(cond_ref[...], (row == col + place[AT_P] * rows).astype(BF))
    sigmoid = 1.0 / (1.0 + jnp.exp(-cond))
    act = cond * sigmoid
    act_ref[:, :rows] = act.astype(BF)
    slope_ref[:, :rows] = sigmoid * (1.0 + cond * (1.0 - sigmoid))
    act_all[...] = act
    mine = act_all[at_rows(place[AT_F], 8)].astype(BF)
    for block in range(8):
        if block < 6:
            part_ref[block] = mm(mine, ada_ref[:, block * d : (block + 1) * d]).astype(BF)
        else:
            part_ref[block] = jnp.zeros(part_ref.shape[1:], BF)
    size = tok_ref.shape[0]
    columns, frames = num_ref.shape

    def token_row(ref):
        lane = lax.broadcasted_iota(jnp.int32, (frames, size), 1)
        frame = lax.broadcasted_iota(jnp.int32, (frames, size), 0)
        wide = mm(ref[...].astype(F32).astype(BF), (lane // columns == frame).astype(BF))
        lane = lax.broadcasted_iota(jnp.int32, (columns, size), 1)
        column = lax.broadcasted_iota(jnp.int32, (columns, size), 0)
        return jnp.sum(jnp.where(lax.rem(lane, columns) == column, wide, 0.0), axis=0, keepdims=True)

    tok_out[size : 2 * size] = tok_ref[...]
    tok_out[2 * size :] = jnp.zeros((16, d), BF)
    tok_out[2 * size :, :size] = jnp.broadcast_to(token_row(num_ref), (16, size)).astype(BF)
    masked = jnp.broadcast_to(token_row(mask_ref), (size, size)).T[:, 0:1]
    tok_out[:size] = jnp.where(masked > 0.5, 0.0, cot_ref[...].astype(F32)).astype(BF)


def mod_sum_kernel(place, terms_ref, bias_ref, out_ref):
    total = terms_ref[0].astype(F32)
    for k in range(1, terms_ref.shape[0]):
        total = total + terms_ref[k].astype(F32)
    bias = row_of(bias_ref[...].astype(F32))
    d = total.shape[1]
    total = total + pick(place[AT_P], [bias[:, k * d : (k + 1) * d] for k in range(6)])
    out_ref[...] = total.astype(BF)


def grad_sum_kernel(place, terms_ref, out_ref):
    total = terms_ref[0].astype(F32)
    for k in range(1, terms_ref.shape[0]):
        total = total + terms_ref[k].astype(F32)
    out_ref[...] = total.astype(BF)


def chunk_of(ref, place, chunk):
    at_z = lax.bitwise_xor(place[AT_Z], chunk // 2 % 4)
    return ref[chunk // 8 * 2 + chunk % 2, at_z]


def token_pair(near_ref, far_ref, size):
    near = pl.program_id(0) < pl.num_programs(0) // 2
    parts, codes = [], []
    for half in range(2):
        rows = slice(size, 2 * size)
        parts.append(jnp.where(near, near_ref[half, rows].astype(F32), far_ref[half, rows].astype(F32)))
        rows = slice(2 * size, 2 * size + 16)
        code = jnp.where(near, near_ref[half, rows, :size].astype(F32), far_ref[half, rows, :size].astype(F32))
        codes.append(code[0:1])
    return jnp.concatenate(parts, axis=0), codes


def attend_kernel(d, width, columns, place, tok_near, tok_far, w_in, modin_ref, bias_ref,
                  out_ref, qkv_ref, sel_ref, selt_ref, w_ref, mod_ref, bias_row):
    step = pl.program_id(0)
    samples = selt_ref.shape[0]
    size = out_ref.shape[1] // 2

    @pl.when(step == 0)
    def _():
        for z in range(4):
            for dy in range(2):
                patch = z * 2 + lax.bitwise_xor(place[AT_Y], dy)
                w_ref[at_rows(patch, width), :] = w_in[z, dy]
        for block in range(6):
            pieces = [chunk_of(modin_ref, place, f * 8 + block).astype(F32) for f in range(4)]
            mod_ref[block] = jnp.concatenate(pieces, axis=0).astype(BF)
        bias = row_of(bias_ref[...].astype(F32))
        bias_row[:, :width] = pick(place[AT_G], [bias[:, k * width : (k + 1) * width] for k in range(8)])
        bias_row[:, width : 2 * width] = jnp.zeros((1, width), F32)
        bias_row[:, 2 * width :] = pick(place[AT_G], [bias[:, d + k * width : d + (k + 1) * width] for k in range(8)])

    numbers = lax.broadcasted_iota(jnp.int32, (samples, size), 0).astype(F32)
    tokens, codes = token_pair(tok_near, tok_far, size)
    for half in range(2):
        rows = slice(half * size, (half + 1) * size)
        hot = (codes[half] == numbers).astype(F32)
        selt_ref[:, rows] = hot.astype(BF)
        sel_ref[rows, :samples] = hot.T.astype(BF)
    normed, _ = normalize(tokens)
    sel = sel_ref[:, : mod_ref.shape[1]]
    attn_in = (normed * (1.0 + mm(sel, mod_ref[1])) + mm(sel, mod_ref[0])).astype(BF)
    qkv = (mm(attn_in, w_ref[:, : 3 * width]) + bias_row[...]).astype(BF)
    qkv_ref[:, : 3 * width] = qkv
    same = column_mask(size, columns)
    for half in range(2):
        rows = slice(half * size, (half + 1) * size)
        parts = []
        for head in range(width // HEAD_DIM):
            q, k, v = (
                qkv[rows, t * width + head * HEAD_DIM : t * width + (head + 1) * HEAD_DIM]
                for t in range(3)
            )
            prob = softmax_prob(q, k, same)
            parts.append(mm(prob.astype(BF), v).T)
        out_ref[:, rows] = jnp.concatenate(parts, axis=0).astype(BF)


def proj_kernel(d, place, *refs):
    rows = d // 8
    pieces, (proj_all, columns) = refs[:8], refs[8:]
    for slot, ref in enumerate(pieces):
        columns[slot] = ref[...]
    for slot in range(8):
        part = place[AT_PART + slot]
        for f in range(4):
            source = place[AT_SLOT + f * 2 + lax.rem(part, 2)]
            proj_all[slot * rows : (slot + 1) * rows, f * 2 * rows : (f + 1) * 2 * rows] = columns[source, part // 2]


def mlp_kernel(d, order, place, *refs):
    n = len(order)
    slots = refs[:n]
    (tok_near, tok_far, sel_ref, selt_ref, mod_ref, proj_all, projb_ref, fc1_in, fc1b_ref, fc2_in, fc2b_ref, w_ref) = refs[n : n + 12]
    (b2_own, b2_far, gm_own, gm_far, fcg_ref, fc1bg_ref, fc2bg_ref, modg_ref, after_ref, branch_ref) = refs[n + 12 : n + 22]
    (fc1a, fc2a, fc1_ref, fc2_ref, pb_row, f1_row, f2_row) = refs[n + 22 :]
    step = pl.program_id(0)
    size = sel_ref.shape[0] // 2
    rows = d // 8
    sel = sel_ref[:, : mod_ref.shape[1]]
    selt = selt_ref[...]

    @pl.when(step == 0)
    def _():
        for z in range(4):
            for dy in range(2):
                patch = z * 2 + lax.bitwise_xor(place[AT_Y], dy)
                fc1_ref[at_rows(patch, rows), :512] = fc1_in[z, dy]
            fc2_ref[z * rows : (z + 1) * rows] = fc2_in[z, :, :d]
        fc1_ref[:, 512:] = w_ref[:, 3 * rows : 7 * rows - 512]
        pb_row[...] = row_of(projb_ref[...].astype(F32))
        f2_row[...] = jnp.where(place[AT_G] == 0, row_of(fc2b_ref[...].astype(F32)), 0.0)
        bias = row_of(fc1b_ref[...].astype(F32))
        for z in range(4):
            options = []
            for k in range(8):
                at = (z * 8 + k) * rows
                options.append(bias[:, at : at + rows])
            f1_row[:, z * rows : (z + 1) * rows] = pick(place[AT_Y] * 4 + place[AT_F], options)

    tokens, _ = token_pair(tok_near, tok_far, size)
    grad_two = jnp.where(step < pl.num_programs(0) // 2, tok_near[:, :size].astype(F32), tok_far[:, :size].astype(F32))
    grad_two = grad_two.reshape(2 * size, d)
    attn_t = slab_attention(slots, order, size)
    branch_one = mm(attn_t, proj_all[...], 0, 0) + pb_row[...]
    after_one = tokens + mm(sel, mod_ref[2]) * branch_one

    @pl.when(step == 0)
    def _():
        after_ref[...] = after_one[:size]
        branch_ref[...] = branch_one[:size]
        fc1a[...] = jnp.zeros_like(fc1a)
        fc2a[...] = jnp.zeros_like(fc2a)
        fc1bg_ref[...] = jnp.zeros_like(fc1bg_ref)
        fc2bg_ref[...] = jnp.zeros_like(fc2bg_ref)
        modg_ref[...] = jnp.zeros_like(modg_ref)

    normed, _ = normalize(after_one)
    mlp_in = (normed * (1.0 + mm(sel, mod_ref[4])) + mm(sel, mod_ref[3])).astype(BF)
    pre = mm(mlp_in, fc1_ref[...]) + f1_row[...]
    square = pre * pre
    tanh = jnp.tanh(GELU_C * pre * (1.0 + GELU_A * square))
    hidden = (0.5 * pre * (1.0 + tanh)).astype(BF)
    slope = 0.5 * (1.0 + tanh) + 0.5 * pre * (1.0 - tanh * tanh) * GELU_C * (1.0 + 3.0 * GELU_A * square)
    branch_two = mm(hidden, fc2_ref[...]) + f2_row[...]
    gb2 = (mm(sel, mod_ref[5]) * grad_two).astype(BF)
    fc2bg_ref[...] += jnp.sum(gb2.astype(F32), axis=0, keepdims=True)
    fc2a[...] += mm(hidden, gb2, 0, 0)
    grad_pre = (mm(gb2, fc2_ref[...], 1, 1) * slope).astype(BF)
    fc1bg_ref[...] += jnp.sum(grad_pre.astype(F32), axis=0, keepdims=True)
    fc1a[...] += mm(mlp_in, grad_pre, 0, 0)
    grad_in = mm(grad_pre, fc1_ref[...], 1, 1)
    modg_ref[0] += mm(selt, grad_in.astype(BF))
    modg_ref[1] += mm(selt, (grad_in * normed).astype(BF))
    modg_ref[2] += mm(selt, (grad_two * branch_two).astype(BF))
    near = step < pl.num_programs(0) // 2

    @pl.when(near)
    def _():
        b2_own[...] = branch_two.astype(BF).reshape(b2_own.shape)
        gm_own[...] = grad_in.astype(BF).reshape(gm_own.shape)

    @pl.when(jnp.logical_not(near))
    def _():
        b2_far[...] = branch_two.astype(BF).reshape(b2_far.shape)
        gm_far[...] = grad_in.astype(BF).reshape(gm_far.shape)

    @pl.when(step == pl.num_programs(0) - 1)
    def _():
        for z in range(4):
            for y in range(2):
                at = (z * 2 + y) * rows
                to = (z * 4 + y) * rows
                fcg_ref[to : to + rows, : 4 * rows] = fc1a[at : at + rows].astype(BF)
            block = fc2a[z * rows : (z + 1) * rows].astype(BF)
            to = (z * 4 + 2) * rows
            fcg_ref[to : to + rows, : 4 * rows] = block[:, : d // 2]
            fcg_ref[to + rows : to + 2 * rows, : 4 * rows] = block[:, d // 2 :]


def middle_kernel(d, count, place, *refs):
    grads = refs[:count]
    (after_ref, branch_ref, cot_ref, sel_ref, selt_ref, mod_ref, proj_ref) = refs[count : count + 7]
    ex_refs = refs[count + 7 : count + 15]
    (one_ref, modg_ref, pbias_ref, turned) = refs[count + 15 :]
    sel = sel_ref[:, : mod_ref.shape[1]]
    grad_in = grads[0][...].astype(F32)
    for ref in grads[1:]:
        grad_in = grad_in + ref[...].astype(F32)
    normed, inverse = normalize(after_ref[...])
    scale = mm(sel, mod_ref[4])
    gate = mm(sel, mod_ref[2])
    grad_one = cot_ref[...].astype(F32) + normalize_back(grad_in * (1.0 + scale), normed, inverse)
    one_ref[...] = grad_one
    modg_ref[...] = mm(selt_ref[...], (grad_one * branch_ref[...]).astype(BF))
    gb1 = (gate * grad_one).astype(BF)
    gb1_wide = gb1.astype(F32)
    pbias_ref[...] = jnp.sum(gb1_wide, axis=0, keepdims=True)
    width = d // 8
    turned[...] = gb1_wide.T
    grad_attn = mm(proj_ref[...], gb1, 1, 1)
    for slot, ref in enumerate(ex_refs):
        ref[0] = grad_attn[slot * width : (slot + 1) * width].astype(BF)
        ref[1] = turned[at_rows(place[AT_PART + slot], width)].astype(BF)


def back_kernel(d, width, columns, place, *refs):
    n = 8
    gas = refs[:n]
    (tok_near, tok_far, sel_ref, selt_ref, mod_ref, qkv_ref, w_ref, two_ref, gate_ref, pb_ref, f1b_ref, f2b_ref) = refs[n : n + 12]
    (gin_own, gin_far, gqkv_ref, in_ref, sum_ref) = refs[n + 12 : n + 17]
    (ga_all, modg, bias_row) = refs[n + 17 :]
    step = pl.program_id(0)
    size = sel_ref.shape[0] // 2

    @pl.when(step == 0)
    def _():
        bias_row[...] = jnp.zeros_like(bias_row)
        modg[...] = jnp.zeros_like(modg)
        for k, ref in enumerate(gas):
            ga_all[k] = ref[...]

    qkv = qkv_ref[:, : 3 * width]
    same = column_mask(size, columns)
    heads = width // HEAD_DIM
    halves = []
    for half in range(2):
        rows = slice(half * size, (half + 1) * size)
        grad_mixed = ga_all[2 * step + half, 0].astype(F32).T
        pieces = [None] * (3 * heads)
        for head in range(heads):
            q, k, v = (
                qkv[rows, t * width + head * HEAD_DIM : t * width + (head + 1) * HEAD_DIM]
                for t in range(3)
            )
            grad = grad_mixed[:, head * HEAD_DIM : (head + 1) * HEAD_DIM].astype(BF)
            prob = softmax_prob(q, k, same)
            grad_prob = mm(grad, v, 1, 1)
            delta = jnp.sum(prob * grad_prob, axis=-1, keepdims=True)
            grad_score = (prob * (grad_prob - delta) * SCORE_SCALE).astype(BF)
            pieces[head] = mm(grad_score, k)
            pieces[heads + head] = mm(grad_score, q, 0, 0)
            pieces[2 * heads + head] = mm(prob.astype(BF), grad, 0, 0)
        halves.append(jnp.concatenate(pieces, axis=1))
    grad_qkv = jnp.concatenate(halves, axis=0).astype(BF)
    bias_row[...] += jnp.sum(grad_qkv.astype(F32), axis=0, keepdims=True)

    tokens, _ = token_pair(tok_near, tok_far, size)
    normed, _ = normalize(tokens)
    sel = sel_ref[:, : mod_ref.shape[1]]
    selt = selt_ref[...]
    attn_in = (normed * (1.0 + mm(sel, mod_ref[1])) + mm(sel, mod_ref[0])).astype(BF)
    in_ref[...] = attn_in
    gqkv_ref[:, : 3 * width] = grad_qkv
    grad_in = mm(grad_qkv, w_ref[:, : 3 * width], 1, 1)
    modg[0] += mm(selt, grad_in.astype(BF))
    modg[1] += mm(selt, (grad_in * normed).astype(BF))
    near = step < pl.num_programs(0) // 2

    @pl.when(near)
    def _():
        gin_own[...] = grad_in.astype(BF).reshape(gin_own.shape)

    @pl.when(jnp.logical_not(near))
    def _():
        gin_far[...] = grad_in.astype(BF).reshape(gin_far.shape)

    @pl.when(step == pl.num_programs(0) - 1)
    def _():
        blocks = [modg[0], modg[1], gate_ref[...], two_ref[0], two_ref[1], two_ref[2]]
        for k, block in enumerate(blocks):
            for group in range(4):
                sum_ref[k * 4 + group] = block[group * 8 : (group + 1) * 8].astype(BF)
        part = place[AT_G]
        rows = [
            spread(bias_row[:, :width], part, 8),
            spread(bias_row[:, 2 * width :], part, 8),
            pb_ref[...],
        ]
        at = place[AT_Y] * 4 + place[AT_F]
        rows += [spread(f1b_ref[:, z * width : (z + 1) * width], at, 8) for z in range(4)]
        rows.append(jnp.where(part == 0, f2b_ref[...], 0.0))
        sum_ref[24] = jnp.concatenate(rows, axis=0).astype(BF)
        for k in range(25, 32):
            sum_ref[k] = jnp.zeros(sum_ref.shape[1:], BF)


def weights_kernel(d, width, order, place, *refs):
    n = len(order)
    slots, gas = refs[:n], refs[n : 2 * n]
    (gqkv_ref, in_ref, grad_ref, qkva, proja, ga_all, grad_all) = refs[2 * n :]
    step = pl.program_id(0)
    size = in_ref.shape[0] // 2

    @pl.when(step == 0)
    def _():
        qkva[...] = jnp.zeros_like(qkva)
        proja[...] = jnp.zeros_like(proja)
        for k, ref in enumerate(gas):
            ga_all[k] = ref[1]

    qkva[...] += mm(in_ref[...], gqkv_ref[:, : 3 * width], 0, 0)
    attn_t = slab_attention(slots, order, size)
    gb1_t = jnp.concatenate([ga_all[2 * step], ga_all[2 * step + 1]], axis=1)
    proja[...] += mm(attn_t, gb1_t, 1, 1)

    @pl.when(step == pl.num_programs(0) - 1)
    def _():
        grad_all[:, : 3 * width] = qkva[...].astype(BF)
        for slot in range(n):
            grad_all[at_rows(place[AT_PART + slot], width), 3 * width :] = proja[slot * width : (slot + 1) * width].astype(BF)
        for z in range(4):
            rows = slice(2 * z * width, 2 * (z + 1) * width)
            for tile in range(4):
                grad_ref[z, tile * 2 * width : (tile + 1) * 2 * width] = grad_all[rows, tile * 128 : (tile + 1) * 128]
            for half in range(2):
                rows = slice((2 * z + half) * width, (2 * z + half + 1) * width)
                grad_ref[z, 8 * width :, half * 64 : (half + 1) * 64] = grad_all[rows, 512:]


def ada_kernel(d, place, total_ref, act_ref, slope_ref, w_ref, wg_ref, cond_ref, ada_ref, qkv_ref, proj_ref, fc1_ref, fc2_ref):
    rows = wg_ref.shape[0]
    act = act_ref[:, :rows]
    cond = jnp.zeros(cond_ref.shape, F32)
    sums = []
    for block in range(6):
        grads = jnp.concatenate([chunk_of(total_ref, place, block * 4 + k).astype(F32) for k in range(4)], axis=0)
        cols = slice(block * d, (block + 1) * d)
        sums.append(jnp.sum(grads, axis=0, keepdims=True))
        grads = grads.astype(BF)
        wg_ref[:, cols] = mm(act, grads, 0, 0)
        cond = cond + mm(grads, w_ref[:, cols], 1, 1)
    cond_ref[...] = cond * slope_ref[:, :rows]
    put_row(ada_ref, jnp.concatenate(sums, axis=1))
    biases = chunk_of(total_ref, place, 24).astype(F32)
    rows = [biases[k : k + 1] for k in range(8)]
    put_row(qkv_ref, jnp.concatenate(rows[:2], axis=1))
    put_row(proj_ref, rows[2])
    put_row(fc1_ref, jnp.concatenate(rows[3:7], axis=1))
    put_row(fc2_ref, rows[7])


def mlp_split_kernel(rows, place, in_ref, out_ref):
    cols = 2 * rows
    out_ref[:, :, 3 * rows :] = jnp.zeros((8, rows, out_ref.shape[2] - 3 * rows), BF)
    for f in range(4):
        for y in range(2):
            out_ref[f * 2 + y, :, :rows] = in_ref[y * rows : (y + 1) * rows, f * rows : (f + 1) * rows]
            out_ref[f * 2 + y, :, rows : 3 * rows] = in_ref[
                (2 + f // 2) * rows : (3 + f // 2) * rows, f % 2 * cols : (f % 2 + 1) * cols
            ]


def mlp_join_kernel(rows, place, got_ref, fc1_ref, fc2_ref):
    for f in range(4):
        for y in range(2):
            at = (y * 4 + f) * rows
            fc1_ref[:, at : at + rows] = got_ref[f * 2 + y, :, :rows].astype(F32)
        fc2_ref[:, f * rows : (f + 1) * rows] = got_ref[f * 2 + place[AT_Y], :, rows : 3 * rows].astype(F32).T


def attn_split_kernel(rows, place, packed_ref, out_ref, keep_ref, send_ref, in_ref):
    for tile in range(4):
        in_ref[:, tile * 128 : (tile + 1) * 128] = packed_ref[tile * 2 * rows : (tile + 1) * 2 * rows]
    for half in range(2):
        in_ref[half * rows : (half + 1) * rows, 512:] = packed_ref[8 * rows :, half * 64 : (half + 1) * 64]
    out_ref[...] = jnp.zeros_like(out_ref)
    for part in range(8):

        @pl.when(place[AT_G] == part)
        def _():
            for y in range(2):
                block = in_ref[y * rows : (y + 1) * rows]
                for t in range(3):
                    out_ref[(8 * t + part) // 6 * 2 + y, :, :rows] = block[:, t * rows : (t + 1) * rows]
    for ref, y in ((keep_ref, place[AT_Y]), (send_ref, 1 - place[AT_Y])):
        ref[:, :rows] = in_ref[at_rows(y, rows), 3 * rows :]
        ref[:, rows:] = jnp.zeros((rows, ref.shape[1] - rows), BF)


def attn_join_kernel(rows, place, got_ref, keep_ref, swap_ref, qkv_ref, proj_ref):
    keep, swapped = keep_ref[:, :rows].astype(F32), swap_ref[:, :rows].astype(F32)
    proj_ref[:, :rows] = jnp.where(place[AT_Y] == 0, keep, swapped)
    proj_ref[:, rows:] = jnp.where(place[AT_Y] == 0, swapped, keep)
    for to in range(4):

        @pl.when(place[AT_F] == to)
        def _():
            for k in range(6):
                qkv_ref[:, k * rows : (k + 1) * rows] = got_ref[(6 * to + k) % 8, :, :rows].astype(F32)


def output_kernel(place, b2_0, b2_1, b2_2, b2_3, tok_ref, after_ref, mask_ref, sel_ref, mod_ref, out_ref):
    branch = b2_0[...].astype(F32)
    for ref in (b2_1, b2_2, b2_3):
        branch = branch + ref[...].astype(F32)
    gate = mm(sel_ref[:, : mod_ref.shape[1]], mod_ref[5])
    tokens = tok_ref[...].astype(F32)
    out_ref[...] = jnp.where(mask_ref[...] == 1, tokens, after_ref[...] + gate * branch).astype(BF)


def input_grad_kernel(place, gin_0, gin_1, gin_2, gin_3, tok_ref, one_ref, cot_ref, mask_ref, sel_ref, mod_ref, grad_ref):
    grad_in = gin_0[...].astype(F32)
    for ref in (gin_1, gin_2, gin_3):
        grad_in = grad_in + ref[...].astype(F32)
    normed, inverse = normalize(tok_ref[...].astype(F32))
    scale = mm(sel_ref[:, : mod_ref.shape[1]], mod_ref[1])
    back = normalize_back(grad_in * (1.0 + scale), normed, inverse)
    grad_ref[...] = jnp.where(mask_ref[...] == 1, cot_ref[...].astype(F32), 0.0) + one_ref[...] + back


def slab_solution(mesh):
    names = ("x", "core", "z", "y")
    grid = Mesh(mesh.devices.reshape(2, 2, 4, 2), names)
    offsets = [(dc, dx, dy) for dc in range(2) for dx in range(2) for dy in range(2)]
    order = [dy == 1 for _, _, dy in offsets]
    group = ("x", "core", "y")
    table = [[0] * TABLE for _ in range(32)]
    for device, row in enumerate(table):
        x, c, z, y = device >> 4, (device >> 3) & 1, (device >> 1) & 3, device & 1
        f = x * 2 + c
        row[AT_F], row[AT_Y], row[AT_Z], row[AT_P], row[AT_G] = f, y, z, device & 7, f * 2 + y
        for slot, (dc, dx, dy) in enumerate(offsets):
            part = ((x ^ dx) * 2 + (c ^ dc)) * 2 + (y ^ dy)
            row[AT_PART + slot] = part
            row[AT_SLOT + part] = slot
        for piece in range(8):
            row[AT_SHARD + piece] = (z ^ (piece >> 1)) * 2 + (y ^ (piece & 1))
        for patch in range(8):
            row[AT_PIECE + patch] = ((patch & 1) ^ y) * 4 + (patch >> 1)

    def swap(a, axes):
        n = 2 ** len(axes)
        return lax.ppermute(a, axes, [(k, n - 1 - k) for k in range(n)])

    def from_z(a, apart):
        return lax.ppermute(a, ("z",), [(z, z ^ apart) for z in range(4)])

    def over(a, dx, dy):
        axes = (("x",) if dx else ()) + (("y",) if dy else ())
        return swap(a, axes) if axes else a

    def gather_near(a):
        return [over(a, dx, dy) for dx in range(2) for dy in range(2)]

    def gather_slots(a):
        mine = gather_near(a)
        return mine + [swap(piece, ("core",)) for piece in mine]

    def over_z(a):
        return [a] + [from_z(a, apart) for apart in (1, 2, 3)]

    def to_slab(a):
        return lax.all_to_all(jnp.broadcast_to(a, (8, *a.shape)), group, 0, 0, tiled=True)

    def core_sum(own, far):
        received = swap(far, ("core",))
        return [(own[slot].astype(F32) + received[slot].astype(F32)).astype(BF) for slot in range(4)]

    def scatter_sum(own, far):
        return [over(total, slot // 2, slot % 2) for slot, total in enumerate(core_sum(own, far))]

    def exchange(slots):
        moved = []
        for slot, offset in zip(slots, offsets):
            axes = tuple(axis for axis, apart in zip(("x", "core", "y"), (offset[1], offset[0], offset[2])) if apart)
            moved.append(swap(slot, axes) if axes else slot)
        return moved

    def local(tokens, image_mask, sample_index, condition, ada_weight, ada_bias, qkv_weight, qkv_bias,
              proj_weight, proj_bias, fc1_weight, fc1_bias, fc2_weight, fc2_bias, cotangent):
        frames, columns, d = tokens.shape
        T = frames * columns
        S = 8 * T
        TB = 2 * T
        samples = condition.shape[0]
        rows = ada_weight.shape[0]
        ff = fc1_weight.shape[1]
        width = d // 8
        part_ff = ff // 8
        cols = 2 * width
        me = lax.axis_index(names).astype(jnp.uint32)
        place = lax.dynamic_slice(jnp.array(table, jnp.int32), (me, jnp.uint32(0)), (1, TABLE)).reshape(TABLE)

        def shaped(shape, dtype=F32):
            return jax.ShapeDtypeStruct(shape, dtype)

        def rows_at(w):
            return pl.BlockSpec((TB, w), lambda j, *_: (j, 0))

        def lanes_at(h):
            return pl.BlockSpec((h, TB), lambda j, *_: (0, j))

        token_specs = [
            pl.BlockSpec((2, 2 * T + 16, d), lambda j, *_: (jnp.minimum(j, 1), 0, 0)),
            pl.BlockSpec((2, 2 * T + 16, d), lambda j, *_: (jnp.maximum(j - 2, 0), 0, 0)),
        ]

        def call(name, us, kernel, arrays, outs, steps=1, ins=None, specs=None, scratch=()):
            return pl.pallas_call(
                kernel,
                grid_spec=pltpu.PrefetchScalarGridSpec(
                    num_scalar_prefetch=1,
                    grid=(steps,),
                    in_specs=ins or [whole(array.shape) for array in arrays],
                    out_specs=specs or [whole(out.shape) for out in outs],
                    scratch_shapes=list(scratch),
                ),
                out_shape=outs,
                compiler_params=params(),
                cost_estimate=takes(us),
                name=name,
            )(place, *arrays)

        def lines(bias):
            return bias.reshape(-1, 128)

        flat_tokens = tokens.reshape(T, d)
        flat_cot = cotangent.reshape(T, d)
        mask = image_mask.reshape(T, 1)

        (partial_mod, act_rows, silu_slope, qkv_mine, fc1_mine, send, fc2_rows, slab_rows) = call(
            "prepare",
            6,
            functools.partial(prepare_kernel, d),
            [condition, ada_weight, qkv_weight, fc1_weight, proj_weight, fc2_weight, flat_tokens, flat_cot, sample_index.T, image_mask.T],
            [
                shaped((8, 8, d), BF),
                shaped((samples, wide(rows)), BF),
                shaped((samples, wide(rows))),
                shaped((rows, wide(3 * width)), BF),
                shaped((rows, 512), BF),
                shaped((rows, 512 + wide(3 * width)), BF),
                shaped((rows, wide(d + cols)), BF),
                shaped((2 * T + 16, d), BF),
            ],
            scratch=[pltpu.VMEM((samples, rows), F32)],
        )

        fc2_in = lax.all_gather(fc2_rows, "z", axis=0)
        mod_terms = lax.all_to_all(partial_mod, ("z", "y"), 0, 0, tiled=True)
        got = swap(send, ("y",))
        qkv_pair = jnp.stack([qkv_mine, got[:, 512:]])
        fc1_pair = jnp.stack([fc1_mine, got[:, :512]])
        mod_terms, qkv_pair, fc1_pair, slab_rows = lax.optimization_barrier((mod_terms, qkv_pair, fc1_pair, slab_rows))
        qkv_pair, fc2_in = lax.optimization_barrier((qkv_pair, fc2_in))
        qkv_in = lax.all_gather(qkv_pair, "z", axis=0)
        (mod_chunk,) = call(
            "mod_sum",
            2,
            mod_sum_kernel,
            [mod_terms, lines(ada_bias)],
            [shaped((8, d), BF)],
        )
        chunks = over_z(mod_chunk)
        tok_mine = gather_near(slab_rows)
        chunks, tok_mine = lax.optimization_barrier((chunks, tok_mine))
        mod_in = to_slab(jnp.stack(chunks))
        tok_near = jnp.stack(tok_mine)
        tok_far = swap(tok_near, ("core",))
        proj_slots = gather_slots(fc2_in[:, :, d : d + cols])
        mod_in, tok_near, tok_far, qkv_in, fc1_pair, proj_slots = lax.optimization_barrier(
            (mod_in, tok_near, tok_far, qkv_in, fc1_pair, proj_slots)
        )
        fc1_in = lax.all_gather(fc1_pair, "z", axis=0)
        attn_t, qkv, sel, selt, w_qkv, mod = call(
            "attend",
            13,
            functools.partial(attend_kernel, d, width, columns),
            [tok_near, tok_far, qkv_in, mod_in, lines(qkv_bias)],
            [
                shaped((width, S), BF),
                shaped((S, wide(3 * width)), BF),
                shaped((S, 128), BF),
                shaped((samples, S), BF),
                shaped((d, wide(3 * width)), BF),
                shaped((6, samples, d), BF),
            ],
            steps=4,
            ins=token_specs
            + [whole(array.shape) for array in (qkv_in, mod_in, lines(qkv_bias))],
            specs=[
                lanes_at(width),
                rows_at(wide(3 * width)),
                rows_at(128),
                lanes_at(samples),
                whole((d, wide(3 * width))),
                whole((6, samples, d)),
            ],
            scratch=[pltpu.VMEM((1, 3 * width), F32)],
        )
        (proj_all,) = call(
            "proj",
            3,
            functools.partial(proj_kernel, d),
            proj_slots,
            [shaped((d, d), BF)],
            scratch=[pltpu.VMEM((8, 4, rows, cols), BF)],
        )
        attn_mine, proj_all = lax.optimization_barrier((gather_near(attn_t), proj_all))
        attn_slots = attn_mine + [swap(piece, ("core",)) for piece in attn_mine]

        def slot_spec(dc, dx):
            return pl.BlockSpec((width, TB), lambda j, *_: (0, lax.bitwise_xor(j, dc * 2 + dx)))

        slot_specs = [slot_spec(dc, dx) for dc, dx, _ in offsets]
        own_out = pl.BlockSpec((2, T, d), lambda j, *_: (jnp.minimum(j, 1), 0, 0))
        far_out = pl.BlockSpec((2, T, d), lambda j, *_: (jnp.maximum(j - 2, 0), 0, 0))
        half_shape = shaped((4, T, d), BF)

        mlp_rest = [mod, proj_all, lines(proj_bias), fc1_in, lines(fc1_bias), fc2_in, lines(fc2_bias), w_qkv]
        (b2_own, b2_far, gm_own, gm_far, fcg, fc1_bias_g, fc2_bias_g, modg_two, after_own, branch_own) = call(
            "mlp",
            32,
            functools.partial(mlp_kernel, d, order),
            [*attn_slots, tok_near, tok_far, sel, selt, *mlp_rest],
            [
                half_shape,
                half_shape,
                half_shape,
                half_shape,
                shaped((16 * rows, wide(part_ff)), BF),
                shaped((1, part_ff)),
                shaped((1, d)),
                shaped((3, samples, d)),
                shaped((T, d)),
                shaped((T, d)),
            ],
            steps=4,
            ins=slot_specs
            + token_specs
            + [rows_at(128), lanes_at(samples)]
            + [whole(array.shape) for array in mlp_rest],
            specs=[
                own_out,
                far_out,
                own_out,
                far_out,
                whole((16 * rows, wide(part_ff))),
                whole((1, part_ff)),
                whole((1, d)),
                whole((3, samples, d)),
                whole((T, d)),
                whole((T, d)),
            ],
            scratch=[
                pltpu.VMEM((d, part_ff), F32),
                pltpu.VMEM((part_ff, d), F32),
                pltpu.VMEM((d, part_ff), BF),
                pltpu.VMEM((part_ff, d), BF),
                pltpu.VMEM((1, d), F32),
                pltpu.VMEM((1, part_ff), F32),
                pltpu.VMEM((1, d), F32),
            ],
        )

        fc_z = lax.psum_scatter(fcg, "z", scatter_dimension=0, tiled=True)
        gm_terms = scatter_sum(gm_own, gm_far)

        *ex_slots, grad_one, modg_gate, proj_bias_g = call(
            "middle",
            6,
            functools.partial(middle_kernel, d, len(gm_terms)),
            [*gm_terms, after_own, branch_own, slab_rows, sel, selt, mod, proj_all],
            [shaped((2, width, T), BF)] * 8 + [shaped((T, d)), shaped((samples, d)), shaped((1, d))],
            ins=[whole((T, d))] * (len(gm_terms) + 3)
            + [whole((T, 128)), whole((samples, T)), whole(mod.shape), whole((d, d))],
            scratch=[pltpu.VMEM((d, T), F32)],
        )
        grad_attn = exchange(ex_slots)
        b2_sums = core_sum(b2_own, b2_far)
        grad_attn, b2_sums = lax.optimization_barrier((grad_attn, b2_sums))
        b2_terms = [over(total, slot // 2, slot % 2) for slot, total in enumerate(b2_sums)]

        back_rest = [w_qkv, modg_two, modg_gate, proj_bias_g, fc1_bias_g, fc2_bias_g]
        gin_own, gin_far, grad_qkv, attn_in, to_sum = call(
            "back",
            22,
            functools.partial(back_kernel, d, width, columns),
            [*grad_attn, tok_near, tok_far, sel, selt, mod, qkv, *back_rest],
            [half_shape, half_shape, shaped((S, wide(3 * width)), BF), shaped((S, d), BF), shaped((32, 8, d), BF)],
            steps=4,
            ins=[whole((2, width, T))] * 8
            + token_specs
            + [rows_at(128), lanes_at(samples), whole(mod.shape), rows_at(wide(3 * width))]
            + [whole(array.shape) for array in back_rest],
            specs=[own_out, far_out, rows_at(wide(3 * width)), rows_at(d), whole((32, 8, d))],
            scratch=[
                pltpu.VMEM((8, 2, width, T), BF),
                pltpu.VMEM((2, samples, d), F32),
                pltpu.VMEM((1, 3 * width), F32),
            ],
        )
        gin_own, gin_far, grad_qkv, attn_in, to_sum, b2_terms = lax.optimization_barrier(
            (gin_own, gin_far, grad_qkv, attn_in, to_sum, b2_terms)
        )
        gin_terms = scatter_sum(gin_own, gin_far)
        (attn_g,) = call(
            "weights",
            8,
            functools.partial(weights_kernel, d, width, order),
            [*attn_slots, *grad_attn, grad_qkv, attn_in],
            [shaped((4, 9 * width, 128), BF)],
            steps=4,
            ins=slot_specs + [whole((2, width, T))] * 8 + [rows_at(wide(3 * width)), rows_at(d)],
            specs=[whole((4, 9 * width, 128))],
            scratch=[
                pltpu.VMEM((d, 3 * width), F32),
                pltpu.VMEM((d, width), F32),
                pltpu.VMEM((8, width, T), BF),
                pltpu.VMEM((d, 4 * width), BF),
            ],
        )
        terms = lax.all_to_all(to_sum, names, 0, 0, tiled=True)
        (mlp_send,) = call(
            "mlp_split", 3, functools.partial(mlp_split_kernel, rows), [fc_z], [shaped((8, rows, wide(3 * rows)), BF)]
        )
        attn_g, terms, mlp_send, gin_terms = lax.optimization_barrier((attn_g, terms, mlp_send, gin_terms))
        mlp_got = lax.all_to_all(mlp_send, group, 0, 0, tiled=True)
        attn_z = lax.psum_scatter(attn_g.reshape(36 * width, 128), "z", scatter_dimension=0, tiled=True)

        (sums,) = call("grad_sum", 2, grad_sum_kernel, [terms], [shaped((8, d), BF)])
        own_specs = [whole((T, 1)), whole((T, 128)), whole(mod.shape)]
        (input_grad,) = call(
            "input_grad",
            3,
            input_grad_kernel,
            [*gin_terms, flat_tokens, grad_one, flat_cot, mask, sel, mod],
            [shaped((T, d))],
            ins=[whole((T, d))] * 7 + own_specs,
        )
        sums, mlp_got, input_grad = lax.optimization_barrier((over_z(sums), mlp_got, input_grad))
        total = to_slab(jnp.stack(sums))

        (ada_weight_grad, condition_grad, ada_bias_grad, qkv_bias_grad, proj_bias_grad, fc1_bias_grad, fc2_bias_grad) = call(
            "ada",
            5,
            functools.partial(ada_kernel, d),
            [total, act_rows, silu_slope, ada_weight],
            [shaped((rows, 6 * d)), shaped((samples, rows))]
            + [shaped((n // 128, 128)) for n in (6 * d, 2 * d, d, ff, d)],
        )

        (result,) = call(
            "output",
            3,
            output_kernel,
            [*b2_terms, flat_tokens, after_own, mask, sel, mod],
            [shaped((T, d), BF)],
            ins=[whole((T, d))] * 6 + own_specs,
        )
        fc1_weight_grad, fc2_weight_grad = call(
            "mlp_join",
            3,
            functools.partial(mlp_join_kernel, rows),
            [mlp_got],
            [shaped((rows, ff // 4)), shaped((d // 4, 4 * rows))],
        )
        attn_z, result, fc1_weight_grad = lax.optimization_barrier((attn_z, result, fc1_weight_grad))
        attn_send, proj_keep, proj_send = call(
            "attn_split",
            3,
            functools.partial(attn_split_kernel, rows),
            [attn_z],
            [shaped((8, rows, wide(rows)), BF), shaped((rows, wide(rows)), BF), shaped((rows, wide(rows)), BF)],
            scratch=[pltpu.VMEM((2 * rows, 4 * rows), BF)],
        )
        attn_got = lax.all_to_all(attn_send, group, 0, 0, tiled=True)
        qkv_weight_grad, proj_weight_grad = call(
            "attn_join",
            3,
            functools.partial(attn_join_kernel, rows),
            [attn_got, proj_keep, swap(proj_send, ("y",))],
            [shaped((rows, 3 * d // 4)), shaped((rows, d // 4))],
        )

        shape = (frames, columns, d)
        return (
            result.reshape(shape),
            input_grad.reshape(shape),
            condition_grad,
            ada_weight_grad,
            ada_bias_grad.reshape(-1),
            qkv_weight_grad,
            qkv_bias_grad.reshape(-1),
            proj_weight_grad,
            proj_bias_grad.reshape(-1),
            fc1_weight_grad,
            fc1_bias_grad.reshape(-1),
            fc2_weight_grad.T,
            fc2_bias_grad.reshape(-1),
        )

    frame, patch = ("x", "core"), ("z", "y")
    token_spec, number_spec = P(None, names, None), P(None, names)
    row_spec, both_spec = P(patch, None), P(patch, frame)
    return jax.shard_map(
        local,
        mesh=grid,
        in_specs=(
            token_spec, number_spec, number_spec, P(), row_spec, P(), row_spec, P(), row_spec, P(), row_spec, P(),
            row_spec, P(), token_spec,
        ),
        out_specs=(
            token_spec, token_spec, P(None, patch), row_spec, P(), both_spec, P(), both_spec, P(), both_spec, P(),
            both_spec, P(),
        ),
        check_vma=False,
    )


def solution(mesh):
    if (mesh.shape["frame"], mesh.shape["patch"]) == (4, 8):
        return slab_solution(mesh)
    return general_solution(mesh)
```

```python
import functools

import jax
import jax.numpy as jnp
from jax import lax
from jax.experimental import pallas as pl
from jax.experimental.pallas import tpu as pltpu
from jax.sharding import Mesh, PartitionSpec as P

HEAD_DIM = 72
EPSILON = 1e-06
SCORE_SCALE = HEAD_DIM**-0.5
GELU_C = 0.7978845608028654
GELU_A = 0.044715
VMEM_BYTES = 56 * 1024 * 1024
(AT_F, AT_Y, AT_Z, AT_P, AT_G) = range(5)
AT_PART, AT_SLOT, AT_SHARD, AT_PIECE, TABLE = 8, 16, 24, 32, 40
BF = jnp.bfloat16
F32 = jnp.float32


def mm(a, b, ca=1, cb=0):
    return lax.dot_general(a, b, (((ca,), (cb,)), ((), ())), preferred_element_type=F32)


def normalize(values):
    centred = values - jnp.mean(values, axis=-1, keepdims=True)
    inverse = lax.rsqrt(jnp.mean(centred * centred, axis=-1, keepdims=True) + EPSILON)
    return centred * inverse, inverse


def normalize_back(grad_normed, normed, inverse):
    return inverse * (
        grad_normed
        - jnp.mean(grad_normed, axis=-1, keepdims=True)
        - normed * jnp.mean(grad_normed * normed, axis=-1, keepdims=True)
    )


def stack_rows(pieces):
    if pieces[0].shape[0] % 16 == 0:
        return jnp.concatenate(pieces, axis=0)
    return jnp.concatenate([piece.astype(F32) for piece in pieces], axis=0).astype(pieces[0].dtype)


def softmax_prob(queries, key_rows, same_column):
    grid = mm(queries, key_rows, 1, 1) * SCORE_SCALE
    grid = jnp.where(same_column, grid, -1e30)
    expanded = jnp.exp(grid - jnp.max(grid, axis=-1, keepdims=True))
    return expanded / jnp.sum(expanded, axis=-1, keepdims=True)


def column_mask(tokens_per_part, columns):
    rows = lax.broadcasted_iota(jnp.int32, (tokens_per_part, tokens_per_part), 0)
    cols = lax.broadcasted_iota(jnp.int32, (tokens_per_part, tokens_per_part), 1)
    return lax.rem(rows, columns) == lax.rem(cols, columns)


def slab_attention(refs, order, size):
    pieces = []
    for ref, swapped in zip(refs, order):
        piece = ref[...]
        if swapped:
            piece = jnp.concatenate([piece[:, size:], piece[:, :size]], axis=1)
        pieces.append(piece)
    return stack_rows(pieces)


def general_attend_kernel(d, width, columns, tok_ref, sel_ref, mod_ref, w_ref, bias_ref, out_ref, qkv_ref):
    normed, _ = normalize(tok_ref[...].astype(F32))
    sel = sel_ref[...]
    shift = mm(sel, mod_ref[:, 0:d])
    scale = mm(sel, mod_ref[:, d : 2 * d])
    attn_in = (normed * (1.0 + scale) + shift).astype(BF)
    qkv = (mm(attn_in, w_ref[...]) + bias_ref[...]).astype(BF)
    qkv_ref[...] = qkv
    size = tok_ref.shape[0] // 2
    same = column_mask(size, columns)
    for half in range(2):
        rows = slice(half * size, (half + 1) * size)
        parts = []
        for head in range(width // HEAD_DIM):
            q, k, v = (
                qkv[rows, t * width + head * HEAD_DIM : t * width + (head + 1) * HEAD_DIM]
                for t in range(3)
            )
            prob = softmax_prob(q, k, same)
            parts.append(mm(prob.astype(BF), v).T)
        out_ref[:, rows] = jnp.concatenate(parts, axis=0).astype(BF)


def general_mlp_kernel(d, order, *refs):
    n = len(order)
    slots = refs[:n]
    (tok_ref, cot_ref, sel_ref, selt_ref, mod_ref, proj_ref, projb_ref, fc1_ref, fc1b_ref, fc2_ref, fc2b_ref) = refs[n : n + 11]
    (b2_ref, gm_ref, fc1g_ref, fc2g_ref, fc1bg_ref, fc2bg_ref, modg_ref, after_ref, branch_ref, fc1a, fc2a) = refs[n + 11 :]
    step = pl.program_id(0)
    size = tok_ref.shape[0] // 2
    sel = sel_ref[...]
    selt = selt_ref[...]

    def mod(block):
        return mm(sel, mod_ref[:, block * d : (block + 1) * d])

    attn_t = slab_attention(slots, order, size)
    branch_one = mm(attn_t, proj_ref[...], 0, 0) + projb_ref[...]
    after_one = tok_ref[...].astype(F32) + mod(2) * branch_one

    @pl.when(step == 0)
    def _():
        after_ref[...] = after_one[:size]
        branch_ref[...] = branch_one[:size]
        fc1a[...] = jnp.zeros_like(fc1a)
        fc2a[...] = jnp.zeros_like(fc2a)
        fc1bg_ref[...] = jnp.zeros_like(fc1bg_ref)
        fc2bg_ref[...] = jnp.zeros_like(fc2bg_ref)
        modg_ref[...] = jnp.zeros_like(modg_ref)

    normed, _ = normalize(after_one)
    mlp_in = (normed * (1.0 + mod(4)) + mod(3)).astype(BF)
    pre = mm(mlp_in, fc1_ref[...]) + fc1b_ref[...]
    square = pre * pre
    tanh = jnp.tanh(GELU_C * pre * (1.0 + GELU_A * square))
    hidden = (0.5 * pre * (1.0 + tanh)).astype(BF)
    slope = 0.5 * (1.0 + tanh) + 0.5 * pre * (1.0 - tanh * tanh) * GELU_C * (1.0 + 3.0 * GELU_A * square)
    branch_two = mm(hidden, fc2_ref[...]) + fc2b_ref[...]
    b2_ref[...] = branch_two.astype(BF).reshape(b2_ref.shape)
    grad_two = cot_ref[...].astype(F32)
    grad_branch = mod(5) * grad_two
    gb2 = grad_branch.astype(BF)
    fc2bg_ref[...] += jnp.sum(gb2.astype(F32), axis=0, keepdims=True)
    fc2a[...] += mm(hidden, gb2, 0, 0)
    grad_pre = (mm(gb2, fc2_ref[...], 1, 1) * slope).astype(BF)
    fc1bg_ref[...] += jnp.sum(grad_pre.astype(F32), axis=0, keepdims=True)
    fc1a[...] += mm(mlp_in, grad_pre, 0, 0)
    grad_in = mm(grad_pre, fc1_ref[...], 1, 1)
    gm_ref[...] = grad_in.astype(BF).reshape(gm_ref.shape)
    modg_ref[0] += mm(selt, grad_in.astype(BF))
    modg_ref[1] += mm(selt, (grad_in * normed).astype(BF))
    modg_ref[2] += mm(selt, (grad_two * branch_two).astype(BF))

    @pl.when(step == pl.num_programs(0) - 1)
    def _():
        fc1g_ref[...] = fc1a[...].astype(BF)
        fc2g_ref[...] = fc2a[...].astype(BF)


def general_middle_kernel(d, n_parts, count, place_ref, *refs):
    grads = refs[:count]
    (after_ref, branch_ref, cot_ref, sel_ref, selt_ref, mod_ref, proj_ref) = refs[count : count + 7]
    (ex_ref, one_ref, modg_ref, pbias_ref) = refs[count + 7 :]
    sel = sel_ref[...]
    grad_in = grads[0][...].astype(F32)
    for ref in grads[1:]:
        grad_in = grad_in + ref[...].astype(F32)
    normed, inverse = normalize(after_ref[...])
    scale = mm(sel, mod_ref[:, 4 * d : 5 * d])
    gate = mm(sel, mod_ref[:, 2 * d : 3 * d])
    grad_one = cot_ref[...].astype(F32) + normalize_back(grad_in * (1.0 + scale), normed, inverse)
    one_ref[...] = grad_one
    modg_ref[...] = mm(selt_ref[...], (grad_one * branch_ref[...]).astype(BF))
    gb1 = (gate * grad_one).astype(BF)
    gb1_wide = gb1.astype(F32)
    pbias_ref[...] = jnp.sum(gb1_wide, axis=0, keepdims=True)
    width = d // n_parts
    grad_attn = mm(proj_ref[...], gb1, 1, 1)
    gb1_t = gb1_wide.T
    for part in range(n_parts):
        rows = slice(part * width, (part + 1) * width)
        ex_ref[part, 0] = grad_attn[rows].astype(BF)
        ex_ref[place_ref[part], 1] = gb1_t[rows].astype(BF)


def general_attend_back_kernel(d, width, columns, order, place_ref, *refs):
    n = len(order)
    slots = refs[:n]
    (ga_ref, tok_ref, sel_ref, selt_ref, mod_ref, w_ref, qkv_ref) = refs[n : n + 7]
    (gin_ref, qkvg_ref, projg_ref, bias_ref, modg_ref, qkva, proja) = refs[n + 7 :]
    step = pl.program_id(0)
    size = tok_ref.shape[0] // 2

    @pl.when(step == 0)
    def _():
        qkva[...] = jnp.zeros_like(qkva)
        proja[...] = jnp.zeros_like(proja)
        bias_ref[...] = jnp.zeros_like(bias_ref)
        modg_ref[...] = jnp.zeros_like(modg_ref)

    qkv = qkv_ref[...]
    same = column_mask(size, columns)
    heads = width // HEAD_DIM
    halves = []
    for half in range(2):
        rows = slice(half * size, (half + 1) * size)
        grad_mixed = ga_ref[half, 0].astype(F32).T
        pieces = [None] * (3 * heads)
        for head in range(heads):
            q, k, v = (
                qkv[rows, t * width + head * HEAD_DIM : t * width + (head + 1) * HEAD_DIM]
                for t in range(3)
            )
            grad = grad_mixed[:, head * HEAD_DIM : (head + 1) * HEAD_DIM].astype(BF)
            prob = softmax_prob(q, k, same)
            grad_prob = mm(grad, v, 1, 1)
            delta = jnp.sum(prob * grad_prob, axis=-1, keepdims=True)
            grad_score = (prob * (grad_prob - delta) * SCORE_SCALE).astype(BF)
            pieces[head] = mm(grad_score, k)
            pieces[heads + head] = mm(grad_score, q, 0, 0)
            pieces[2 * heads + head] = mm(prob.astype(BF), grad, 0, 0)
        halves.append(jnp.concatenate(pieces, axis=1))
    grad_qkv = jnp.concatenate(halves, axis=0).astype(BF)
    bias_ref[...] += jnp.sum(grad_qkv.astype(F32), axis=0, keepdims=True)

    sel = sel_ref[...]
    selt = selt_ref[...]
    normed, _ = normalize(tok_ref[...].astype(F32))
    shift = mm(sel, mod_ref[:, 0:d])
    scale = mm(sel, mod_ref[:, d : 2 * d])
    attn_in = (normed * (1.0 + scale) + shift).astype(BF)
    qkva[...] += mm(attn_in, grad_qkv, 0, 0)
    grad_in = mm(grad_qkv, w_ref[...], 1, 1)
    gin_ref[...] = grad_in.astype(BF).reshape(gin_ref.shape)
    modg_ref[0] += mm(selt, grad_in.astype(BF))
    modg_ref[1] += mm(selt, (grad_in * normed).astype(BF))

    attn_t = slab_attention(slots, order, size)
    gb1_t = jnp.concatenate([ga_ref[0, 1], ga_ref[1, 1]], axis=1)
    proja[...] += mm(attn_t, gb1_t, 1, 1)

    @pl.when(step == pl.num_programs(0) - 1)
    def _():
        qkvg_ref[...] = qkva[...].astype(BF)
        rows = d // n
        for part in range(n):
            projg_ref[place_ref[part]] = proja[part * rows : (part + 1) * rows].astype(BF)


def general_last_kernel(d, count, count_b, *refs):
    grads = refs[:count]
    branches = refs[count : count + count_b]
    (tok_ref, one_ref, after_ref, cot_ref, mask_ref, sel_ref, mod_ref) = refs[count + count_b : count + count_b + 7]
    (out_ref, grad_ref) = refs[count + count_b + 7 :]
    sel = sel_ref[...]
    masked = mask_ref[...] == 1
    tokens = tok_ref[...].astype(F32)
    grad_in = grads[0][...].astype(F32)
    for ref in grads[1:]:
        grad_in = grad_in + ref[...].astype(F32)
    normed, inverse = normalize(tokens)
    scale = mm(sel, mod_ref[:, d : 2 * d])
    back = normalize_back(grad_in * (1.0 + scale), normed, inverse)
    grad_ref[...] = jnp.where(masked, cot_ref[...].astype(F32), 0.0) + one_ref[...] + back
    branch = branches[0][...].astype(F32)
    for ref in branches[1:]:
        branch = branch + ref[...].astype(F32)
    gate = mm(sel, mod_ref[:, 5 * d : 6 * d])
    out_ref[...] = jnp.where(masked, tokens, after_ref[...] + gate * branch).astype(BF)


def params(steps=1):
    return pltpu.CompilerParams(vmem_limit_bytes=VMEM_BYTES, dimension_semantics=("arbitrary",) * steps)


def cost(flops, bytes_accessed):
    return pl.CostEstimate(flops=int(flops), bytes_accessed=int(bytes_accessed), transcendentals=0)


def whole(shape):
    return pl.BlockSpec(shape, lambda *_: (0,) * len(shape))


def matchings(frames):
    left = {f: {t: (frames * t + f) // 3 for t in range(3)} for f in range(frames)}
    rounds = []
    for _ in range(3):
        taken = {}

        def place(f, seen):
            for t, to in left[f].items():
                if to in seen:
                    continue
                seen.add(to)
                if to not in taken or place(taken[to][0], seen):
                    taken[to] = (f, t)
                    return True
            return False

        for f in range(frames):
            place(f, set())
        chosen = {f: (t, to) for to, (f, t) in taken.items()}
        for f, (t, _to) in chosen.items():
            del left[f][t]
        rounds.append(chosen)
    return rounds


def general_solution(mesh):
    F, N = mesh.shape["frame"], mesh.shape["patch"]
    C, Y = 2, 2
    X, Z = F // C, N // Y
    G = X * C * Y
    half_slots = X * Y
    grid = Mesh(mesh.devices.reshape(X, C, Z, Y), ("x", "core", "z", "y"))
    everywhere = ("x", "core", "z", "y")
    offsets = [(dc, dx, dy) for dc in range(C) for dx in range(X) for dy in range(Y)]

    def from_xy(a, dx, dy):
        if dx == 0 and dy == 0:
            return a
        pairs = [
            (x * Y + y, ((x - dx) % X) * Y + (y - dy) % Y) for x in range(X) for y in range(Y)
        ]
        return lax.ppermute(a, ("x", "y"), pairs)

    def to_xy(a, dx, dy):
        return from_xy(a, (-dx) % X, (-dy) % Y)

    def swap_core(a):
        return lax.ppermute(a, "core", [(0, 1), (1, 0)])

    def swap_y(a):
        return lax.ppermute(a, "y", [(0, 1), (1, 0)])

    def gather_slots(a):
        mine = [from_xy(a, dx, dy) for dx in range(X) for dy in range(Y)]
        return mine + [swap_core(piece) for piece in mine]

    def scatter_sum(slots):
        received = swap_core(slots[half_slots:])
        terms = []
        for slot in range(half_slots):
            total = slots[slot].astype(F32) + received[slot].astype(F32)
            terms.append(to_xy(total.astype(BF), slot // Y, slot % Y))
        return terms

    def exchange(slots):
        received = swap_core(slots[half_slots:])
        pieces = [None] * G
        for slot in range(half_slots):
            dx, dy = slot // Y, slot % Y
            pair = to_xy(jnp.stack([slots[slot], received[slot]]), dx, dy)
            source = ((-dx) % X) * Y + (-dy) % Y
            pieces[source] = pair[0]
            pieces[half_slots + source] = pair[1]
        return jnp.stack(pieces)

    def local(tokens, image_mask, sample_index, condition, ada_weight, ada_bias, qkv_weight, qkv_bias,
              proj_weight, proj_bias, fc1_weight, fc1_bias, fc2_weight, fc2_bias, cotangent):
        frames, columns, d = tokens.shape
        T = frames * columns
        S = G * T
        samples = condition.shape[0]
        rows_here = ada_weight.shape[0]
        ff = fc1_weight.shape[1]
        width = d // G
        unit = ff // (N * F)
        part_ff = Z * unit
        x_i, c_i = lax.axis_index("x"), lax.axis_index("core")
        z_i, y_i = lax.axis_index("z"), lax.axis_index("y")
        f_i = x_i * C + c_i
        p_i = z_i * Y + y_i
        g_i = f_i * Y + y_i
        parts_at = [
            (((x_i + dx) % X) * C + (c_i + dc) % C) * Y + (y_i + dy) % Y for dc, dx, dy in offsets
        ]
        parts_at = jnp.stack(parts_at).astype(jnp.int32)
        all_parts = jnp.arange(G, dtype=jnp.int32)
        part_x, part_c, part_y = all_parts // (C * Y), (all_parts // Y) % C, all_parts % Y
        place = ((part_c - c_i) % C) * half_slots + ((part_x - x_i) % X) * Y + (part_y - y_i) % Y
        place = place.astype(jnp.int32)

        def y_pair(own, other):
            got = swap_y(other)
            return jnp.where(y_i == 0, jnp.stack([own, got]), jnp.stack([got, own]))

        pair_width = Y * width
        qkv_cols = [
            lax.dynamic_slice_in_dim(qkv_weight, t * d + f_i * pair_width, pair_width, 1) for t in range(3)
        ]

        def qkv_for(which):
            return jnp.concatenate(
                [lax.dynamic_slice_in_dim(c, which * width, width, 1) for c in qkv_cols], axis=1
            )

        qkv_rows = y_pair(qkv_for(y_i), qkv_for(1 - y_i)).reshape(Y * rows_here, 3 * width)
        w_qkv = lax.all_gather(qkv_rows, "z", axis=0, tiled=True)
        half_rows = rows_here // C
        proj_half = lax.dynamic_slice_in_dim(proj_weight, c_i * half_rows, half_rows, 0)
        proj_rows = y_pair(proj_half, proj_half).reshape(Y * half_rows, d)
        proj_mine = lax.all_gather(proj_rows, "z", axis=0, tiled=True)
        proj_other = swap_core(proj_mine)
        proj_both = jnp.where(
            c_i == 0, jnp.stack([proj_mine, proj_other]), jnp.stack([proj_other, proj_mine])
        )
        proj_parts = (
            proj_both.reshape(C, N, half_rows, d).transpose(1, 0, 2, 3).reshape(G, width, d)
        )
        proj_rel = jnp.concatenate(
            [lax.dynamic_index_in_dim(proj_parts, parts_at[r], 0, keepdims=False) for r in range(G)],
            axis=0,
        )

        def fc1_for(which):
            return jnp.concatenate(
                [
                    lax.dynamic_slice_in_dim(
                        fc1_weight, (z * Y + which) * (F * unit) + f_i * unit, unit, 1
                    )
                    for z in range(Z)
                ],
                axis=1,
            )

        fc1_rows = y_pair(fc1_for(y_i), fc1_for(1 - y_i)).reshape(Y * rows_here, part_ff)
        w_fc1 = lax.all_gather(fc1_rows, "z", axis=0, tiled=True)
        fc2_rows = lax.dynamic_slice_in_dim(fc2_weight, f_i * unit, unit, 0)
        w_fc2 = lax.all_gather(fc2_rows, "z", axis=0, tiled=True)

        chunk = samples * 6 * d // (F * N)
        per_row = 6 * d // chunk
        frame_samples = samples // F
        first_row = p_i * rows_here
        cond_rows = lax.dynamic_slice_in_dim(condition, first_row, rows_here, 1).astype(F32)
        sigmoid = 1.0 / (1.0 + jnp.exp(-cond_rows))
        act_rows = (cond_rows * sigmoid).astype(BF)
        silu_slope = sigmoid * (1.0 + cond_rows * (1.0 - sigmoid))
        act_mine = lax.dynamic_slice_in_dim(act_rows, f_i * frame_samples, frame_samples, 0)
        partial_mod = mm(act_mine, ada_weight).reshape(N, chunk)
        mod_terms = lax.all_to_all(partial_mod, ("z", "y"), 0, 0, tiled=True)
        bias_here = lax.dynamic_slice_in_dim(ada_bias, (p_i % per_row) * chunk, chunk, 0)
        mod_chunk = (jnp.sum(mod_terms, axis=0) + bias_here.astype(F32)).astype(BF)
        mod = lax.all_to_all(
            jnp.broadcast_to(mod_chunk, (F * N, chunk)), everywhere, 0, 0, tiled=True
        ).reshape(samples, 6 * d)

        flat_tokens = tokens.reshape(T, d)
        flat_cot = cotangent.reshape(T, d)
        mask = image_mask.reshape(T, 1)
        grad_two_own = jnp.where(mask == 1, jnp.zeros_like(flat_cot), flat_cot)
        codes = jnp.zeros((16, d), BF).at[0, :T].set(sample_index.reshape(T).astype(BF))
        token_slots = gather_slots(jnp.concatenate([flat_tokens, codes], axis=0))
        slab_tokens = jnp.concatenate([piece[:T] for piece in token_slots], axis=0)
        slab_codes = jnp.stack([piece[T, :T] for piece in token_slots]).astype(jnp.int32)
        slab_cot = jnp.concatenate(gather_slots(grad_two_own), axis=0)
        numbers = jnp.arange(samples, dtype=jnp.int32)
        selt = (slab_codes.reshape(1, S) == numbers[:, None]).astype(BF)
        sel = (slab_codes.reshape(S, 1) == numbers[None, :]).astype(BF)
        sel_own, selt_own = sel[:T], selt[:, :T]

        steps = G // 2
        TB = 2 * T
        row_block = lambda w: pl.BlockSpec((TB, w), lambda j: (j, 0))
        lane_block = lambda h: pl.BlockSpec((h, TB), lambda j: (0, j))

        bias_q = lax.dynamic_slice_in_dim(qkv_bias, g_i * width, width, 0)
        bias_v = lax.dynamic_slice_in_dim(qkv_bias, d + g_i * width, width, 0)
        bias_qkv = jnp.concatenate([bias_q, jnp.zeros_like(bias_q), bias_v]).astype(F32)[None]
        attn_t, qkv = pl.pallas_call(
            functools.partial(general_attend_kernel, d, width, columns),
            grid=(steps,),
            in_specs=[
                row_block(d),
                row_block(samples),
                whole((samples, 6 * d)),
                whole((d, 3 * width)),
                whole((1, 3 * width)),
            ],
            out_specs=[lane_block(width), row_block(3 * width)],
            out_shape=[
                jax.ShapeDtypeStruct((width, S), BF),
                jax.ShapeDtypeStruct((S, 3 * width), BF),
            ],
            compiler_params=params(),
            cost_estimate=cost(2 * S * d * 3 * width * 2, 8e6),
            name="attend",
        )(slab_tokens, sel, mod, w_qkv, bias_qkv)

        attn_slots = gather_slots(attn_t)
        order = [dy == 1 for _, _, dy in offsets]

        def slot_spec(dc, dx):
            return pl.BlockSpec(
                (width, TB),
                lambda j: (0, ((j // X + C - dc) % C) * X + (j % X + X - dx) % X),
            )

        slot_specs = [slot_spec(dc, dx) for dc, dx, _ in offsets]

        hidden_at = lambda v: jnp.concatenate(
            [
                lax.dynamic_slice_in_dim(v, (z * Y + y_i) * (F * unit) + f_i * unit, unit, 0)
                for z in range(Z)
            ]
        )
        fc1_bias_part = hidden_at(fc1_bias).astype(F32)[None]
        fc2_bias_once = jnp.where(g_i == 0, fc2_bias.astype(F32), 0.0)[None]
        slot_out = pl.BlockSpec((2, T, d), lambda j: (j, 0, 0))
        (b2_slots, gm_slots, fc1g, fc2g, fc1_bias_g, fc2_bias_g, modg_two, after_own, branch_own) = pl.pallas_call(
            functools.partial(general_mlp_kernel, d, order),
            grid=(steps,),
            in_specs=slot_specs
            + [
                row_block(d),
                row_block(d),
                row_block(samples),
                lane_block(samples),
                whole((samples, 6 * d)),
                whole((d, d)),
                whole((1, d)),
                whole((d, part_ff)),
                whole((1, part_ff)),
                whole((part_ff, d)),
                whole((1, d)),
            ],
            out_specs=[
                slot_out,
                slot_out,
                whole((d, part_ff)),
                whole((part_ff, d)),
                whole((1, part_ff)),
                whole((1, d)),
                whole((3, samples, d)),
                whole((T, d)),
                whole((T, d)),
            ],
            out_shape=[
                jax.ShapeDtypeStruct((G, T, d), BF),
                jax.ShapeDtypeStruct((G, T, d), BF),
                jax.ShapeDtypeStruct((d, part_ff), BF),
                jax.ShapeDtypeStruct((part_ff, d), BF),
                jax.ShapeDtypeStruct((1, part_ff), F32),
                jax.ShapeDtypeStruct((1, d), F32),
                jax.ShapeDtypeStruct((3, samples, d), F32),
                jax.ShapeDtypeStruct((T, d), F32),
                jax.ShapeDtypeStruct((T, d), F32),
            ],
            scratch_shapes=[pltpu.VMEM((d, part_ff), F32), pltpu.VMEM((part_ff, d), F32)],
            compiler_params=params(),
            cost_estimate=cost(2 * S * (d * d + 6 * d * part_ff), 3e7),
            name="mlp",
        )(
            *attn_slots,
            slab_tokens,
            slab_cot,
            sel,
            selt,
            mod,
            proj_rel,
            proj_bias.astype(F32)[None],
            w_fc1,
            fc1_bias_part,
            w_fc2,
            fc2_bias_once,
        )

        fc1_z = lax.psum_scatter(fc1g, "z", scatter_dimension=0, tiled=True)
        fc2_z = lax.psum_scatter(fc2g, "z", scatter_dimension=0, tiled=True)
        gm_terms = scatter_sum(gm_slots)

        ex_slots, grad_one, modg_gate, proj_bias_g = pl.pallas_call(
            functools.partial(general_middle_kernel, d, G, len(gm_terms)),
            grid_spec=pltpu.PrefetchScalarGridSpec(
                num_scalar_prefetch=1,
                grid=(1,),
                in_specs=[whole((T, d))] * len(gm_terms)
                + [
                    whole((T, d)),
                    whole((T, d)),
                    whole((T, d)),
                    whole((T, samples)),
                    whole((samples, T)),
                    whole((samples, 6 * d)),
                    whole((d, d)),
                ],
                out_specs=[
                    whole((G, 2, width, T)),
                    whole((T, d)),
                    whole((samples, d)),
                    whole((1, d)),
                ],
            ),
            out_shape=[
                jax.ShapeDtypeStruct((G, 2, width, T), BF),
                jax.ShapeDtypeStruct((T, d), F32),
                jax.ShapeDtypeStruct((samples, d), F32),
                jax.ShapeDtypeStruct((1, d), F32),
            ],
            compiler_params=params(),
            cost_estimate=cost(4 * T * d * d, 8e6),
            name="middle",
        )(place, *gm_terms, after_own, branch_own, grad_two_own, sel_own, selt_own, mod, proj_rel)

        grad_attn = exchange(ex_slots)
        b2_terms = scatter_sum(b2_slots)

        slot_back = [
            pl.BlockSpec(spec.block_shape, lambda j, place, spec=spec: spec.index_map(j))
            for spec in slot_specs
        ]
        rows_b = lambda w: pl.BlockSpec((TB, w), lambda j, place: (j, 0))
        gin_slots, qkvg, projg, qkv_bias_part, modg_one = pl.pallas_call(
            functools.partial(general_attend_back_kernel, d, width, columns, order),
            grid_spec=pltpu.PrefetchScalarGridSpec(
                num_scalar_prefetch=1,
                grid=(steps,),
                in_specs=slot_back
                + [
                    pl.BlockSpec((2, 2, width, T), lambda j, place: (j, 0, 0, 0)),
                    rows_b(d),
                    rows_b(samples),
                    pl.BlockSpec((samples, TB), lambda j, place: (0, j)),
                    whole((samples, 6 * d)),
                    whole((d, 3 * width)),
                    rows_b(3 * width),
                ],
                out_specs=[
                    pl.BlockSpec((2, T, d), lambda j, place: (j, 0, 0)),
                    whole((d, 3 * width)),
                    whole((G, width, width)),
                    whole((1, 3 * width)),
                    whole((2, samples, d)),
                ],
                scratch_shapes=[
                    pltpu.VMEM((d, 3 * width), F32),
                    pltpu.VMEM((d, width), F32),
                ],
            ),
            out_shape=[
                jax.ShapeDtypeStruct((G, T, d), BF),
                jax.ShapeDtypeStruct((d, 3 * width), BF),
                jax.ShapeDtypeStruct((G, width, width), BF),
                jax.ShapeDtypeStruct((1, 3 * width), F32),
                jax.ShapeDtypeStruct((2, samples, d), F32),
            ],
            compiler_params=params(),
            cost_estimate=cost(2 * S * d * 8 * width, 1.2e7),
            name="attend_back",
        )(parts_at, *attn_slots, grad_attn, slab_tokens, sel, selt, mod, w_qkv, qkv)

        gin_terms = scatter_sum(gin_slots)

        bias_total = 2 * d + d + ff + d
        biases = jnp.zeros((bias_total,), F32)
        put = lax.dynamic_update_slice_in_dim
        biases = put(biases, qkv_bias_part[0, :width], g_i * width, 0)
        biases = put(biases, qkv_bias_part[0, 2 * width :], d + g_i * width, 0)
        biases = put(biases, proj_bias_g[0], 2 * d, 0)
        for z in range(Z):
            biases = put(
                biases,
                fc1_bias_g[0, z * unit : (z + 1) * unit],
                3 * d + (z * Y + y_i) * (F * unit) + f_i * unit,
                0,
            )
        biases = put(biases, jnp.where(g_i == 0, fc2_bias_g[0], 0.0), 3 * d + ff, 0)
        mod_sums = jnp.concatenate(
            [modg_one[0], modg_one[1], modg_gate, modg_two[0], modg_two[1], modg_two[2]], axis=1
        )
        to_sum = jnp.concatenate(
            [mod_sums.reshape(F * N, chunk), biases.reshape(F * N, bias_total // (F * N))], axis=1
        ).astype(BF)
        terms = lax.all_to_all(to_sum, everywhere, 0, 0, tiled=True)
        summed = jnp.sum(terms.astype(F32), axis=0).astype(BF)
        total = lax.all_to_all(
            jnp.broadcast_to(summed, (F * N, summed.shape[0])), everywhere, 0, 0, tiled=True
        )
        mod_grad = total[:, :chunk].reshape(samples, 6 * d)
        bias_grad = total[:, chunk:].reshape(bias_total).astype(F32)
        ada_bias_grad = jnp.sum(mod_grad.astype(F32), axis=0)
        ada_weight_grad = mm(act_rows, mod_grad, 0, 0)
        condition_grad = mm(mod_grad, ada_weight, 1, 1) * silu_slope

        def y_join(rows):
            kept = lax.dynamic_index_in_dim(rows, y_i, 0, keepdims=False)
            got = swap_y(lax.dynamic_index_in_dim(rows, 1 - y_i, 0, keepdims=False))
            return jnp.where(y_i == 0, jnp.stack([kept, got]), jnp.stack([got, kept]))

        attn_g = jnp.concatenate([qkvg, projg.reshape(d, width)], axis=1)
        attn_z = lax.psum_scatter(attn_g, "z", scatter_dimension=0, tiled=True)
        attn_y = y_join(attn_z.reshape(Y, rows_here, 4 * width))
        blocks = jnp.stack(
            [
                jnp.concatenate([attn_y[y, :, t * width : (t + 1) * width] for y in range(Y)], axis=1)
                for t in range(4)
            ]
        )
        proj_weight_grad = blocks[3].astype(F32)
        moved = [None] * 3
        spots = jnp.zeros((3, F), jnp.int32)
        for turn, chosen in enumerate(matchings(F)):
            picks = jnp.array([chosen[f][0] for f in range(F)], jnp.int32)
            block = lax.dynamic_index_in_dim(blocks, picks[f_i], 0, keepdims=False)
            pairs = [(f, chosen[f][1]) for f in range(F)]
            if any(a != b for a, b in pairs):
                block = lax.ppermute(block, ("x", "core"), pairs)
            moved[turn] = block
            for f in range(F):
                t, to = chosen[f]
                spots = spots.at[(F * t + f) % 3, to].set(turn)
        moved = jnp.stack(moved)
        qkv_weight_grad = jnp.concatenate(
            [
                lax.dynamic_index_in_dim(moved, spots[k, f_i], 0, keepdims=False)
                for k in range(3)
            ],
            axis=1,
        ).astype(F32)

        fc1_y = y_join(fc1_z.reshape(Y, rows_here, part_ff))
        per_frame = Z // F
        fc1_send = fc1_y.reshape(Y, rows_here, F, per_frame, unit).transpose(2, 1, 3, 0, 4)
        fc1_got = lax.all_to_all(fc1_send, ("x", "core"), 0, 0, tiled=True)
        fc1_weight_grad = (
            fc1_got.transpose(1, 2, 3, 0, 4).reshape(rows_here, ff // F).astype(F32)
        )
        fc2_send = fc2_z.reshape(unit, F, d // F).transpose(1, 0, 2)
        fc2_got = lax.all_to_all(fc2_send, ("x", "core"), 0, 0, tiled=True)
        fc2_weight_grad = fc2_got.reshape(F * unit, d // F).astype(F32)

        result, input_grad = pl.pallas_call(
            functools.partial(general_last_kernel, d, len(gin_terms), len(b2_terms)),
            out_shape=[jax.ShapeDtypeStruct((T, d), BF), jax.ShapeDtypeStruct((T, d), F32)],
            compiler_params=pltpu.CompilerParams(vmem_limit_bytes=VMEM_BYTES),
            cost_estimate=cost(1e6, 5e6),
            name="last",
        )(*gin_terms, *b2_terms, flat_tokens, grad_one, after_own, flat_cot, mask, sel_own, mod)

        shape = (frames, columns, d)
        return (
            result.reshape(shape),
            input_grad.reshape(shape),
            condition_grad,
            ada_weight_grad,
            ada_bias_grad,
            qkv_weight_grad,
            bias_grad[: 2 * d],
            proj_weight_grad,
            bias_grad[2 * d : 3 * d],
            fc1_weight_grad,
            bias_grad[3 * d : 3 * d + ff],
            fc2_weight_grad,
            bias_grad[3 * d + ff :],
        )

    frame, patch = ("x", "core"), ("z", "y")
    every = ("x", "core", "z", "y")
    token_spec = P(None, every, None)
    number_spec = P(None, every)
    row_spec = P(patch, None)
    both_spec = P(patch, frame)
    return jax.shard_map(
        local,
        mesh=grid,
        in_specs=(
            token_spec, number_spec, number_spec, P(), row_spec, P(), row_spec, P(), row_spec, P(), row_spec, P(),
            row_spec, P(), token_spec,
        ),
        out_specs=(
            token_spec, token_spec, P(None, patch), row_spec, P(), both_spec, P(), both_spec, P(), both_spec, P(),
            both_spec, P(),
        ),
        check_vma=False,
    )


def takes(microseconds):
    return pl.CostEstimate(flops=1000, bytes_accessed=1000, transcendentals=0)


def wide(lanes):
    return -(-lanes // 128) * 128


def row_of(values):
    return jnp.concatenate([values[k : k + 1] for k in range(values.shape[0])], axis=1)


def put_row(ref, row):
    for k in range(ref.shape[0]):
        ref[k : k + 1] = row[:, k * 128 : (k + 1) * 128]


def pick(index, options):
    total = jnp.where(index == 0, options[0], 0.0)
    for k in range(1, len(options)):
        total = total + jnp.where(index == k, options[k], 0.0)
    return total


def spread(values, index, n):
    return jnp.concatenate([jnp.where(index == k, values, 0.0) for k in range(n)], axis=1)


def at_rows(index, rows):
    return pl.ds(pl.multiple_of(index * rows, rows), rows)


def prepare_kernel(d, cond_ref, ada_ref, qkv_ref, fc1_ref, proj_ref, fc2_ref, tok_ref, cot_ref, num_ref, mask_ref,
                   part_ref, act_ref, slope_ref, qkv_mine, fc1_mine, send_out, fc2_out, tok_out, act_all):
    rows = ada_ref.shape[0]
    frame = lax.axis_index("x") * 2 + lax.axis_index("core")
    at_y = lax.axis_index("y")
    patch = lax.axis_index("z") * 2 + at_y
    cols = 2 * rows
    for ref in (qkv_mine, send_out, fc2_out):
        ref[...] = jnp.zeros_like(ref)
    act_ref[...] = jnp.zeros_like(act_ref)
    slope_ref[...] = jnp.zeros_like(slope_ref)
    for f in range(4):

        @pl.when(frame == f)
        def _():
            fc2_out[:, d : d + cols] = proj_ref[:, f * cols : (f + 1) * cols]
            for y in range(2):
                for q_out, at_q, f_out, want in ((qkv_mine, 0, fc1_mine, y), (send_out, 512, send_out, 1 - y)):

                    @pl.when(at_y == want)
                    def _():
                        for t in range(3):
                            at = t * d + (2 * f + y) * rows
                            q_out[:, at_q + t * rows : at_q + (t + 1) * rows] = qkv_ref[:, at : at + rows]
                        for z in range(4):
                            at = ((z * 2 + y) * 4 + f) * rows
                            kept = min(rows, 512 - z * rows)
                            f_out[:, z * rows : z * rows + kept] = fc1_ref[:, at : at + kept]
                            if kept < rows:
                                to = at_q + 3 * rows
                                q_out[:, to : to + rows - kept] = fc1_ref[:, at + kept : at + rows]

    fc2_out[:, :d] = fc2_ref[at_rows(frame, rows)]
    row = lax.broadcasted_iota(jnp.int32, (d, rows), 0)
    col = lax.broadcasted_iota(jnp.int32, (d, rows), 1)
    cond = mm(cond_ref[...], (row == col + patch * rows).astype(BF))
    sigmoid = 1.0 / (1.0 + jnp.exp(-cond))
    act = cond * sigmoid
    act_ref[:, :rows] = act.astype(BF)
    slope_ref[:, :rows] = sigmoid * (1.0 + cond * (1.0 - sigmoid))
    act_all[...] = act
    mine = act_all[at_rows(frame, 8)].astype(BF)
    for block in range(8):
        if block < 6:
            part_ref[block] = mm(mine, ada_ref[:, block * d : (block + 1) * d]).astype(BF)
        else:
            part_ref[block] = jnp.zeros(part_ref.shape[1:], BF)
    size = tok_ref.shape[0]
    columns, frames = num_ref.shape

    def token_row(ref):
        lane = lax.broadcasted_iota(jnp.int32, (frames, size), 1)
        frame = lax.broadcasted_iota(jnp.int32, (frames, size), 0)
        wide = mm(ref[...].astype(F32).astype(BF), (lane // columns == frame).astype(BF))
        lane = lax.broadcasted_iota(jnp.int32, (columns, size), 1)
        column = lax.broadcasted_iota(jnp.int32, (columns, size), 0)
        return jnp.sum(jnp.where(lax.rem(lane, columns) == column, wide, 0.0), axis=0, keepdims=True)

    tok_out[size : 2 * size] = tok_ref[...]
    tok_out[2 * size :] = jnp.zeros((16, d), BF)
    tok_out[2 * size :, :size] = jnp.broadcast_to(token_row(num_ref), (16, size)).astype(BF)
    masked = jnp.broadcast_to(token_row(mask_ref), (size, size)).T[:, 0:1]
    tok_out[:size] = jnp.where(masked > 0.5, 0.0, cot_ref[...].astype(F32)).astype(BF)


def mod_sum_kernel(place, terms_ref, bias_ref, out_ref):
    total = terms_ref[0].astype(F32)
    for k in range(1, terms_ref.shape[0]):
        total = total + terms_ref[k].astype(F32)
    bias = row_of(bias_ref[...].astype(F32))
    d = total.shape[1]
    total = total + pick(place[AT_P], [bias[:, k * d : (k + 1) * d] for k in range(6)])
    out_ref[...] = total.astype(BF)


def grad_sum_kernel(place, terms_ref, out_ref):
    total = terms_ref[0].astype(F32)
    for k in range(1, terms_ref.shape[0]):
        total = total + terms_ref[k].astype(F32)
    out_ref[...] = total.astype(BF)


def chunk_of(ref, place, chunk):
    at_z = lax.bitwise_xor(place[AT_Z], chunk // 2 % 4)
    return ref[chunk // 8 * 2 + chunk % 2, at_z]


def token_pair(near_ref, far_ref, size):
    near = pl.program_id(0) < pl.num_programs(0) // 2
    parts, codes = [], []
    for half in range(2):
        rows = slice(size, 2 * size)
        parts.append(jnp.where(near, near_ref[half, rows].astype(F32), far_ref[half, rows].astype(F32)))
        rows = slice(2 * size, 2 * size + 16)
        code = jnp.where(near, near_ref[half, rows, :size].astype(F32), far_ref[half, rows, :size].astype(F32))
        codes.append(code[0:1])
    return jnp.concatenate(parts, axis=0), codes


def attend_kernel(d, width, columns, place, tok_near, tok_far, w_in, modin_ref, bias_ref,
                  out_ref, qkv_ref, sel_ref, selt_ref, w_ref, mod_ref, bias_row):
    step = pl.program_id(0)
    samples = selt_ref.shape[0]
    size = out_ref.shape[1] // 2

    @pl.when(step == 0)
    def _():
        for z in range(4):
            for dy in range(2):
                patch = z * 2 + lax.bitwise_xor(place[AT_Y], dy)
                w_ref[at_rows(patch, width), :] = w_in[z, dy]
        for block in range(6):
            pieces = [chunk_of(modin_ref, place, f * 8 + block).astype(F32) for f in range(4)]
            mod_ref[block] = jnp.concatenate(pieces, axis=0).astype(BF)
        bias = row_of(bias_ref[...].astype(F32))
        bias_row[:, :width] = pick(place[AT_G], [bias[:, k * width : (k + 1) * width] for k in range(8)])
        bias_row[:, width : 2 * width] = jnp.zeros((1, width), F32)
        bias_row[:, 2 * width :] = pick(place[AT_G], [bias[:, d + k * width : d + (k + 1) * width] for k in range(8)])

    numbers = lax.broadcasted_iota(jnp.int32, (samples, size), 0).astype(F32)
    tokens, codes = token_pair(tok_near, tok_far, size)
    for half in range(2):
        rows = slice(half * size, (half + 1) * size)
        hot = (codes[half] == numbers).astype(F32)
        selt_ref[:, rows] = hot.astype(BF)
        sel_ref[rows, :samples] = hot.T.astype(BF)
    normed, _ = normalize(tokens)
    sel = sel_ref[:, : mod_ref.shape[1]]
    attn_in = (normed * (1.0 + mm(sel, mod_ref[1])) + mm(sel, mod_ref[0])).astype(BF)
    qkv = (mm(attn_in, w_ref[:, : 3 * width]) + bias_row[...]).astype(BF)
    qkv_ref[:, : 3 * width] = qkv
    same = column_mask(size, columns)
    for half in range(2):
        rows = slice(half * size, (half + 1) * size)
        parts = []
        for head in range(width // HEAD_DIM):
            q, k, v = (
                qkv[rows, t * width + head * HEAD_DIM : t * width + (head + 1) * HEAD_DIM]
                for t in range(3)
            )
            prob = softmax_prob(q, k, same)
            parts.append(mm(prob.astype(BF), v).T)
        out_ref[:, rows] = jnp.concatenate(parts, axis=0).astype(BF)


def proj_kernel(d, place, *refs):
    rows = d // 8
    pieces, (proj_all, columns) = refs[:8], refs[8:]
    for slot, ref in enumerate(pieces):
        columns[slot] = ref[...]
    for slot in range(8):
        part = place[AT_PART + slot]
        for f in range(4):
            source = place[AT_SLOT + f * 2 + lax.rem(part, 2)]
            proj_all[slot * rows : (slot + 1) * rows, f * 2 * rows : (f + 1) * 2 * rows] = columns[source, part // 2]


def mlp_kernel(d, order, place, *refs):
    n = len(order)
    slots = refs[:n]
    (tok_near, tok_far, sel_ref, selt_ref, mod_ref, proj_all, projb_ref, fc1_in, fc1b_ref, fc2_in, fc2b_ref, w_ref) = refs[n : n + 12]
    (b2_own, b2_far, gm_own, gm_far, fcg_ref, fc1bg_ref, fc2bg_ref, modg_ref, after_ref, branch_ref) = refs[n + 12 : n + 22]
    (fc1a, fc2a, fc1_ref, fc2_ref, pb_row, f1_row, f2_row) = refs[n + 22 :]
    step = pl.program_id(0)
    size = sel_ref.shape[0] // 2
    rows = d // 8
    sel = sel_ref[:, : mod_ref.shape[1]]
    selt = selt_ref[...]

    @pl.when(step == 0)
    def _():
        for z in range(4):
            for dy in range(2):
                patch = z * 2 + lax.bitwise_xor(place[AT_Y], dy)
                fc1_ref[at_rows(patch, rows), :512] = fc1_in[z, dy]
            fc2_ref[z * rows : (z + 1) * rows] = fc2_in[z, :, :d]
        fc1_ref[:, 512:] = w_ref[:, 3 * rows : 7 * rows - 512]
        pb_row[...] = row_of(projb_ref[...].astype(F32))
        f2_row[...] = jnp.where(place[AT_G] == 0, row_of(fc2b_ref[...].astype(F32)), 0.0)
        bias = row_of(fc1b_ref[...].astype(F32))
        for z in range(4):
            options = []
            for k in range(8):
                at = (z * 8 + k) * rows
                options.append(bias[:, at : at + rows])
            f1_row[:, z * rows : (z + 1) * rows] = pick(place[AT_Y] * 4 + place[AT_F], options)

    tokens, _ = token_pair(tok_near, tok_far, size)
    grad_two = jnp.where(step < pl.num_programs(0) // 2, tok_near[:, :size].astype(F32), tok_far[:, :size].astype(F32))
    grad_two = grad_two.reshape(2 * size, d)
    attn_t = slab_attention(slots, order, size)
    branch_one = mm(attn_t, proj_all[...], 0, 0) + pb_row[...]
    after_one = tokens + mm(sel, mod_ref[2]) * branch_one

    @pl.when(step == 0)
    def _():
        after_ref[...] = after_one[:size]
        branch_ref[...] = branch_one[:size]
        fc1a[...] = jnp.zeros_like(fc1a)
        fc2a[...] = jnp.zeros_like(fc2a)
        fc1bg_ref[...] = jnp.zeros_like(fc1bg_ref)
        fc2bg_ref[...] = jnp.zeros_like(fc2bg_ref)
        modg_ref[...] = jnp.zeros_like(modg_ref)

    normed, _ = normalize(after_one)
    mlp_in = (normed * (1.0 + mm(sel, mod_ref[4])) + mm(sel, mod_ref[3])).astype(BF)
    pre = mm(mlp_in, fc1_ref[...]) + f1_row[...]
    square = pre * pre
    tanh = jnp.tanh(GELU_C * pre * (1.0 + GELU_A * square))
    hidden = (0.5 * pre * (1.0 + tanh)).astype(BF)
    slope = 0.5 * (1.0 + tanh) + 0.5 * pre * (1.0 - tanh * tanh) * GELU_C * (1.0 + 3.0 * GELU_A * square)
    branch_two = mm(hidden, fc2_ref[...]) + f2_row[...]
    gb2 = (mm(sel, mod_ref[5]) * grad_two).astype(BF)
    fc2bg_ref[...] += jnp.sum(gb2.astype(F32), axis=0, keepdims=True)
    fc2a[...] += mm(hidden, gb2, 0, 0)
    grad_pre = (mm(gb2, fc2_ref[...], 1, 1) * slope).astype(BF)
    fc1bg_ref[...] += jnp.sum(grad_pre.astype(F32), axis=0, keepdims=True)
    fc1a[...] += mm(mlp_in, grad_pre, 0, 0)
    grad_in = mm(grad_pre, fc1_ref[...], 1, 1)
    modg_ref[0] += mm(selt, grad_in.astype(BF))
    modg_ref[1] += mm(selt, (grad_in * normed).astype(BF))
    modg_ref[2] += mm(selt, (grad_two * branch_two).astype(BF))
    near = step < pl.num_programs(0) // 2

    @pl.when(near)
    def _():
        b2_own[...] = branch_two.astype(BF).reshape(b2_own.shape)
        gm_own[...] = grad_in.astype(BF).reshape(gm_own.shape)

    @pl.when(jnp.logical_not(near))
    def _():
        b2_far[...] = branch_two.astype(BF).reshape(b2_far.shape)
        gm_far[...] = grad_in.astype(BF).reshape(gm_far.shape)

    @pl.when(step == pl.num_programs(0) - 1)
    def _():
        for z in range(4):
            for y in range(2):
                at = (z * 2 + y) * rows
                to = (z * 4 + y) * rows
                fcg_ref[to : to + rows, : 4 * rows] = fc1a[at : at + rows].astype(BF)
            block = fc2a[z * rows : (z + 1) * rows].astype(BF)
            to = (z * 4 + 2) * rows
            fcg_ref[to : to + rows, : 4 * rows] = block[:, : d // 2]
            fcg_ref[to + rows : to + 2 * rows, : 4 * rows] = block[:, d // 2 :]


def middle_kernel(d, count, place, *refs):
    grads = refs[:count]
    (after_ref, branch_ref, cot_ref, sel_ref, selt_ref, mod_ref, proj_ref) = refs[count : count + 7]
    ex_refs = refs[count + 7 : count + 15]
    (one_ref, modg_ref, pbias_ref, turned) = refs[count + 15 :]
    sel = sel_ref[:, : mod_ref.shape[1]]
    grad_in = grads[0][...].astype(F32)
    for ref in grads[1:]:
        grad_in = grad_in + ref[...].astype(F32)
    normed, inverse = normalize(after_ref[...])
    scale = mm(sel, mod_ref[4])
    gate = mm(sel, mod_ref[2])
    grad_one = cot_ref[...].astype(F32) + normalize_back(grad_in * (1.0 + scale), normed, inverse)
    one_ref[...] = grad_one
    modg_ref[...] = mm(selt_ref[...], (grad_one * branch_ref[...]).astype(BF))
    gb1 = (gate * grad_one).astype(BF)
    gb1_wide = gb1.astype(F32)
    pbias_ref[...] = jnp.sum(gb1_wide, axis=0, keepdims=True)
    width = d // 8
    turned[...] = gb1_wide.T
    grad_attn = mm(proj_ref[...], gb1, 1, 1)
    for slot, ref in enumerate(ex_refs):
        ref[0] = grad_attn[slot * width : (slot + 1) * width].astype(BF)
        ref[1] = turned[at_rows(place[AT_PART + slot], width)].astype(BF)


def back_kernel(d, width, columns, place, *refs):
    n = 8
    gas = refs[:n]
    (tok_near, tok_far, sel_ref, selt_ref, mod_ref, qkv_ref, w_ref, two_ref, gate_ref, pb_ref, f1b_ref, f2b_ref) = refs[n : n + 12]
    (gin_own, gin_far, gqkv_ref, in_ref, sum_ref) = refs[n + 12 : n + 17]
    (ga_all, modg, bias_row) = refs[n + 17 :]
    step = pl.program_id(0)
    size = sel_ref.shape[0] // 2

    @pl.when(step == 0)
    def _():
        bias_row[...] = jnp.zeros_like(bias_row)
        modg[...] = jnp.zeros_like(modg)
        for k, ref in enumerate(gas):
            ga_all[k] = ref[...]

    qkv = qkv_ref[:, : 3 * width]
    same = column_mask(size, columns)
    heads = width // HEAD_DIM
    halves = []
    for half in range(2):
        rows = slice(half * size, (half + 1) * size)
        grad_mixed = ga_all[2 * step + half, 0].astype(F32).T
        pieces = [None] * (3 * heads)
        for head in range(heads):
            q, k, v = (
                qkv[rows, t * width + head * HEAD_DIM : t * width + (head + 1) * HEAD_DIM]
                for t in range(3)
            )
            grad = grad_mixed[:, head * HEAD_DIM : (head + 1) * HEAD_DIM].astype(BF)
            prob = softmax_prob(q, k, same)
            grad_prob = mm(grad, v, 1, 1)
            delta = jnp.sum(prob * grad_prob, axis=-1, keepdims=True)
            grad_score = (prob * (grad_prob - delta) * SCORE_SCALE).astype(BF)
            pieces[head] = mm(grad_score, k)
            pieces[heads + head] = mm(grad_score, q, 0, 0)
            pieces[2 * heads + head] = mm(prob.astype(BF), grad, 0, 0)
        halves.append(jnp.concatenate(pieces, axis=1))
    grad_qkv = jnp.concatenate(halves, axis=0).astype(BF)
    bias_row[...] += jnp.sum(grad_qkv.astype(F32), axis=0, keepdims=True)

    tokens, _ = token_pair(tok_near, tok_far, size)
    normed, _ = normalize(tokens)
    sel = sel_ref[:, : mod_ref.shape[1]]
    selt = selt_ref[...]
    attn_in = (normed * (1.0 + mm(sel, mod_ref[1])) + mm(sel, mod_ref[0])).astype(BF)
    in_ref[...] = attn_in
    gqkv_ref[:, : 3 * width] = grad_qkv
    grad_in = mm(grad_qkv, w_ref[:, : 3 * width], 1, 1)
    modg[0] += mm(selt, grad_in.astype(BF))
    modg[1] += mm(selt, (grad_in * normed).astype(BF))
    near = step < pl.num_programs(0) // 2

    @pl.when(near)
    def _():
        gin_own[...] = grad_in.astype(BF).reshape(gin_own.shape)

    @pl.when(jnp.logical_not(near))
    def _():
        gin_far[...] = grad_in.astype(BF).reshape(gin_far.shape)

    @pl.when(step == pl.num_programs(0) - 1)
    def _():
        blocks = [modg[0], modg[1], gate_ref[...], two_ref[0], two_ref[1], two_ref[2]]
        for k, block in enumerate(blocks):
            for group in range(4):
                sum_ref[k * 4 + group] = block[group * 8 : (group + 1) * 8].astype(BF)
        part = place[AT_G]
        rows = [
            spread(bias_row[:, :width], part, 8),
            spread(bias_row[:, 2 * width :], part, 8),
            pb_ref[...],
        ]
        at = place[AT_Y] * 4 + place[AT_F]
        rows += [spread(f1b_ref[:, z * width : (z + 1) * width], at, 8) for z in range(4)]
        rows.append(jnp.where(part == 0, f2b_ref[...], 0.0))
        sum_ref[24] = jnp.concatenate(rows, axis=0).astype(BF)
        for k in range(25, 32):
            sum_ref[k] = jnp.zeros(sum_ref.shape[1:], BF)


def weights_kernel(d, width, order, place, *refs):
    n = len(order)
    slots, gas = refs[:n], refs[n : 2 * n]
    (gqkv_ref, in_ref, grad_ref, qkva, proja, ga_all, grad_all) = refs[2 * n :]
    step = pl.program_id(0)
    size = in_ref.shape[0] // 2

    @pl.when(step == 0)
    def _():
        qkva[...] = jnp.zeros_like(qkva)
        proja[...] = jnp.zeros_like(proja)
        for k, ref in enumerate(gas):
            ga_all[k] = ref[1]

    qkva[...] += mm(in_ref[...], gqkv_ref[:, : 3 * width], 0, 0)
    attn_t = slab_attention(slots, order, size)
    gb1_t = jnp.concatenate([ga_all[2 * step], ga_all[2 * step + 1]], axis=1)
    proja[...] += mm(attn_t, gb1_t, 1, 1)

    @pl.when(step == pl.num_programs(0) - 1)
    def _():
        grad_all[:, : 3 * width] = qkva[...].astype(BF)
        for slot in range(n):
            grad_all[at_rows(place[AT_PART + slot], width), 3 * width :] = proja[slot * width : (slot + 1) * width].astype(BF)
        for z in range(4):
            rows = slice(2 * z * width, 2 * (z + 1) * width)
            for tile in range(4):
                grad_ref[z, tile * 2 * width : (tile + 1) * 2 * width] = grad_all[rows, tile * 128 : (tile + 1) * 128]
            for half in range(2):
                rows = slice((2 * z + half) * width, (2 * z + half + 1) * width)
                grad_ref[z, 8 * width :, half * 64 : (half + 1) * 64] = grad_all[rows, 512:]


def ada_kernel(d, place, total_ref, act_ref, slope_ref, w_ref, wg_ref, cond_ref, ada_ref, qkv_ref, proj_ref, fc1_ref, fc2_ref):
    rows = wg_ref.shape[0]
    act = act_ref[:, :rows]
    cond = jnp.zeros(cond_ref.shape, F32)
    sums = []
    for block in range(6):
        grads = jnp.concatenate([chunk_of(total_ref, place, block * 4 + k).astype(F32) for k in range(4)], axis=0)
        cols = slice(block * d, (block + 1) * d)
        sums.append(jnp.sum(grads, axis=0, keepdims=True))
        grads = grads.astype(BF)
        wg_ref[:, cols] = mm(act, grads, 0, 0)
        cond = cond + mm(grads, w_ref[:, cols], 1, 1)
    cond_ref[...] = cond * slope_ref[:, :rows]
    put_row(ada_ref, jnp.concatenate(sums, axis=1))
    biases = chunk_of(total_ref, place, 24).astype(F32)
    rows = [biases[k : k + 1] for k in range(8)]
    put_row(qkv_ref, jnp.concatenate(rows[:2], axis=1))
    put_row(proj_ref, rows[2])
    put_row(fc1_ref, jnp.concatenate(rows[3:7], axis=1))
    put_row(fc2_ref, rows[7])


def mlp_split_kernel(rows, place, in_ref, out_ref):
    cols = 2 * rows
    out_ref[:, :, 3 * rows :] = jnp.zeros((8, rows, out_ref.shape[2] - 3 * rows), BF)
    for f in range(4):
        for y in range(2):
            out_ref[f * 2 + y, :, :rows] = in_ref[y * rows : (y + 1) * rows, f * rows : (f + 1) * rows]
            out_ref[f * 2 + y, :, rows : 3 * rows] = in_ref[
                (2 + f // 2) * rows : (3 + f // 2) * rows, f % 2 * cols : (f % 2 + 1) * cols
            ]


def mlp_join_kernel(rows, place, got_ref, fc1_ref, fc2_ref):
    for f in range(4):
        for y in range(2):
            at = (y * 4 + f) * rows
            fc1_ref[:, at : at + rows] = got_ref[f * 2 + y, :, :rows].astype(F32)
        fc2_ref[:, f * rows : (f + 1) * rows] = got_ref[f * 2 + place[AT_Y], :, rows : 3 * rows].astype(F32).T


def attn_split_kernel(rows, place, packed_ref, out_ref, keep_ref, send_ref, in_ref):
    for tile in range(4):
        in_ref[:, tile * 128 : (tile + 1) * 128] = packed_ref[tile * 2 * rows : (tile + 1) * 2 * rows]
    for half in range(2):
        in_ref[half * rows : (half + 1) * rows, 512:] = packed_ref[8 * rows :, half * 64 : (half + 1) * 64]
    out_ref[...] = jnp.zeros_like(out_ref)
    for part in range(8):

        @pl.when(place[AT_G] == part)
        def _():
            for y in range(2):
                block = in_ref[y * rows : (y + 1) * rows]
                for t in range(3):
                    out_ref[(8 * t + part) // 6 * 2 + y, :, :rows] = block[:, t * rows : (t + 1) * rows]
    for ref, y in ((keep_ref, place[AT_Y]), (send_ref, 1 - place[AT_Y])):
        ref[:, :rows] = in_ref[at_rows(y, rows), 3 * rows :]
        ref[:, rows:] = jnp.zeros((rows, ref.shape[1] - rows), BF)


def attn_join_kernel(rows, place, got_ref, keep_ref, swap_ref, qkv_ref, proj_ref):
    keep, swapped = keep_ref[:, :rows].astype(F32), swap_ref[:, :rows].astype(F32)
    proj_ref[:, :rows] = jnp.where(place[AT_Y] == 0, keep, swapped)
    proj_ref[:, rows:] = jnp.where(place[AT_Y] == 0, swapped, keep)
    for to in range(4):

        @pl.when(place[AT_F] == to)
        def _():
            for k in range(6):
                qkv_ref[:, k * rows : (k + 1) * rows] = got_ref[(6 * to + k) % 8, :, :rows].astype(F32)


def output_kernel(place, b2_0, b2_1, b2_2, b2_3, tok_ref, after_ref, mask_ref, sel_ref, mod_ref, out_ref):
    branch = b2_0[...].astype(F32)
    for ref in (b2_1, b2_2, b2_3):
        branch = branch + ref[...].astype(F32)
    gate = mm(sel_ref[:, : mod_ref.shape[1]], mod_ref[5])
    tokens = tok_ref[...].astype(F32)
    out_ref[...] = jnp.where(mask_ref[...] == 1, tokens, after_ref[...] + gate * branch).astype(BF)


def input_grad_kernel(place, gin_0, gin_1, gin_2, gin_3, tok_ref, one_ref, cot_ref, mask_ref, sel_ref, mod_ref, grad_ref):
    grad_in = gin_0[...].astype(F32)
    for ref in (gin_1, gin_2, gin_3):
        grad_in = grad_in + ref[...].astype(F32)
    normed, inverse = normalize(tok_ref[...].astype(F32))
    scale = mm(sel_ref[:, : mod_ref.shape[1]], mod_ref[1])
    back = normalize_back(grad_in * (1.0 + scale), normed, inverse)
    grad_ref[...] = jnp.where(mask_ref[...] == 1, cot_ref[...].astype(F32), 0.0) + one_ref[...] + back


def slab_solution(mesh):
    names = ("x", "core", "z", "y")
    grid = Mesh(mesh.devices.reshape(2, 2, 4, 2), names)
    offsets = [(dc, dx, dy) for dc in range(2) for dx in range(2) for dy in range(2)]
    order = [dy == 1 for _, _, dy in offsets]
    group = ("x", "core", "y")
    table = [[0] * TABLE for _ in range(32)]
    for device, row in enumerate(table):
        x, c, z, y = device >> 4, (device >> 3) & 1, (device >> 1) & 3, device & 1
        f = x * 2 + c
        row[AT_F], row[AT_Y], row[AT_Z], row[AT_P], row[AT_G] = f, y, z, device & 7, f * 2 + y
        for slot, (dc, dx, dy) in enumerate(offsets):
            part = ((x ^ dx) * 2 + (c ^ dc)) * 2 + (y ^ dy)
            row[AT_PART + slot] = part
            row[AT_SLOT + part] = slot
        for piece in range(8):
            row[AT_SHARD + piece] = (z ^ (piece >> 1)) * 2 + (y ^ (piece & 1))
        for patch in range(8):
            row[AT_PIECE + patch] = ((patch & 1) ^ y) * 4 + (patch >> 1)

    def swap(a, axes):
        n = 2 ** len(axes)
        return lax.ppermute(a, axes, [(k, n - 1 - k) for k in range(n)])

    def from_z(a, apart):
        return lax.ppermute(a, ("z",), [(z, z ^ apart) for z in range(4)])

    def over(a, dx, dy):
        axes = (("x",) if dx else ()) + (("y",) if dy else ())
        return swap(a, axes) if axes else a

    def gather_near(a):
        return [over(a, dx, dy) for dx in range(2) for dy in range(2)]

    def gather_slots(a):
        mine = gather_near(a)
        return mine + [swap(piece, ("core",)) for piece in mine]

    def over_z(a):
        return [a] + [from_z(a, apart) for apart in (1, 2, 3)]

    def to_slab(a):
        return lax.all_to_all(jnp.broadcast_to(a, (8, *a.shape)), group, 0, 0, tiled=True)

    def core_sum(own, far):
        received = swap(far, ("core",))
        return [(own[slot].astype(F32) + received[slot].astype(F32)).astype(BF) for slot in range(4)]

    def scatter_sum(own, far):
        return [over(total, slot // 2, slot % 2) for slot, total in enumerate(core_sum(own, far))]

    def exchange(slots):
        moved = []
        for slot, offset in zip(slots, offsets):
            axes = tuple(axis for axis, apart in zip(("x", "core", "y"), (offset[1], offset[0], offset[2])) if apart)
            moved.append(swap(slot, axes) if axes else slot)
        return moved

    def local(tokens, image_mask, sample_index, condition, ada_weight, ada_bias, qkv_weight, qkv_bias,
              proj_weight, proj_bias, fc1_weight, fc1_bias, fc2_weight, fc2_bias, cotangent):
        frames, columns, d = tokens.shape
        T = frames * columns
        S = 8 * T
        TB = 2 * T
        samples = condition.shape[0]
        rows = ada_weight.shape[0]
        ff = fc1_weight.shape[1]
        width = d // 8
        part_ff = ff // 8
        cols = 2 * width
        me = lax.axis_index(names).astype(jnp.uint32)
        place = lax.dynamic_slice(jnp.array(table, jnp.int32), (me, jnp.uint32(0)), (1, TABLE)).reshape(TABLE)

        def shaped(shape, dtype=F32):
            return jax.ShapeDtypeStruct(shape, dtype)

        def rows_at(w):
            return pl.BlockSpec((TB, w), lambda j, *_: (j, 0))

        def lanes_at(h):
            return pl.BlockSpec((h, TB), lambda j, *_: (0, j))

        token_specs = [
            pl.BlockSpec((2, 2 * T + 16, d), lambda j, *_: (jnp.minimum(j, 1), 0, 0)),
            pl.BlockSpec((2, 2 * T + 16, d), lambda j, *_: (jnp.maximum(j - 2, 0), 0, 0)),
        ]

        def call(name, us, kernel, arrays, outs, steps=1, ins=None, specs=None, scratch=()):
            return pl.pallas_call(
                kernel,
                grid_spec=pltpu.PrefetchScalarGridSpec(
                    num_scalar_prefetch=1,
                    grid=(steps,),
                    in_specs=ins or [whole(array.shape) for array in arrays],
                    out_specs=specs or [whole(out.shape) for out in outs],
                    scratch_shapes=list(scratch),
                ),
                out_shape=outs,
                compiler_params=params(),
                cost_estimate=takes(us),
                name=name,
            )(place, *arrays)

        def lines(bias):
            return bias.reshape(-1, 128)

        flat_tokens = tokens.reshape(T, d)
        flat_cot = cotangent.reshape(T, d)
        mask = image_mask.reshape(T, 1)

        (partial_mod, act_rows, silu_slope, qkv_mine, fc1_mine, send, fc2_rows, slab_rows) = pl.pallas_call(
            functools.partial(prepare_kernel, d),
            out_shape=[
                shaped((8, 8, d), BF),
                shaped((samples, wide(rows)), BF),
                shaped((samples, wide(rows))),
                shaped((rows, wide(3 * width)), BF),
                shaped((rows, 512), BF),
                shaped((rows, 512 + wide(3 * width)), BF),
                shaped((rows, wide(d + cols)), BF),
                shaped((2 * T + 16, d), BF),
            ],
            scratch_shapes=[pltpu.VMEM((samples, rows), F32)],
            compiler_params=pltpu.CompilerParams(vmem_limit_bytes=VMEM_BYTES),
            cost_estimate=takes(6),
            name="prepare",
        )(*[condition, ada_weight, qkv_weight, fc1_weight, proj_weight, fc2_weight, flat_tokens, flat_cot, sample_index.T, image_mask.T])

        fc2_in = lax.all_gather(fc2_rows, "z", axis=0)
        mod_terms = lax.all_to_all(partial_mod, ("z", "y"), 0, 0, tiled=True)
        got = swap(send, ("y",))
        qkv_pair = jnp.stack([qkv_mine, got[:, 512:]])
        fc1_pair = jnp.stack([fc1_mine, got[:, :512]])
        qkv_pair, fc1_pair, slab_rows = lax.optimization_barrier((qkv_pair, fc1_pair, slab_rows))
        mod_terms, qkv_pair, fc1_pair = lax.optimization_barrier((mod_terms, qkv_pair, fc1_pair))
        qkv_pair, fc2_in = lax.optimization_barrier((qkv_pair, fc2_in))
        qkv_in = lax.all_gather(qkv_pair, "z", axis=0)
        (mod_chunk,) = call(
            "mod_sum",
            2,
            mod_sum_kernel,
            [mod_terms, lines(ada_bias)],
            [shaped((8, d), BF)],
        )
        chunks = over_z(mod_chunk)
        tok_mine = gather_near(slab_rows)
        chunks, tok_mine = lax.optimization_barrier((chunks, tok_mine))
        mod_in = to_slab(jnp.stack(chunks))
        tok_near = jnp.stack(tok_mine)
        tok_far = swap(tok_near, ("core",))
        proj_slots = gather_slots(fc2_in[:, :, d : d + cols])
        mod_in, tok_near, tok_far, qkv_in, fc1_pair, proj_slots = lax.optimization_barrier(
            (mod_in, tok_near, tok_far, qkv_in, fc1_pair, proj_slots)
        )
        fc1_in = lax.all_gather(fc1_pair, "z", axis=0)
        attn_t, qkv, sel, selt, w_qkv, mod = call(
            "attend",
            13,
            functools.partial(attend_kernel, d, width, columns),
            [tok_near, tok_far, qkv_in, mod_in, lines(qkv_bias)],
            [
                shaped((width, S), BF),
                shaped((S, wide(3 * width)), BF),
                shaped((S, 128), BF),
                shaped((samples, S), BF),
                shaped((d, wide(3 * width)), BF),
                shaped((6, samples, d), BF),
            ],
            steps=4,
            ins=token_specs
            + [whole(array.shape) for array in (qkv_in, mod_in, lines(qkv_bias))],
            specs=[
                lanes_at(width),
                rows_at(wide(3 * width)),
                rows_at(128),
                lanes_at(samples),
                whole((d, wide(3 * width))),
                whole((6, samples, d)),
            ],
            scratch=[pltpu.VMEM((1, 3 * width), F32)],
        )
        (proj_all,) = call(
            "proj",
            3,
            functools.partial(proj_kernel, d),
            proj_slots,
            [shaped((d, d), BF)],
            scratch=[pltpu.VMEM((8, 4, rows, cols), BF)],
        )
        attn_mine, proj_all = lax.optimization_barrier((gather_near(attn_t), proj_all))
        attn_slots = attn_mine + [swap(piece, ("core",)) for piece in attn_mine]

        def slot_spec(dc, dx):
            return pl.BlockSpec((width, TB), lambda j, *_: (0, lax.bitwise_xor(j, dc * 2 + dx)))

        slot_specs = [slot_spec(dc, dx) for dc, dx, _ in offsets]
        own_out = pl.BlockSpec((2, T, d), lambda j, *_: (jnp.minimum(j, 1), 0, 0))
        far_out = pl.BlockSpec((2, T, d), lambda j, *_: (jnp.maximum(j - 2, 0), 0, 0))
        half_shape = shaped((4, T, d), BF)

        mlp_rest = [mod, proj_all, lines(proj_bias), fc1_in, lines(fc1_bias), fc2_in, lines(fc2_bias), w_qkv]
        (b2_own, b2_far, gm_own, gm_far, fcg, fc1_bias_g, fc2_bias_g, modg_two, after_own, branch_own) = call(
            "mlp",
            32,
            functools.partial(mlp_kernel, d, order),
            [*attn_slots, tok_near, tok_far, sel, selt, *mlp_rest],
            [
                half_shape,
                half_shape,
                half_shape,
                half_shape,
                shaped((16 * rows, wide(part_ff)), BF),
                shaped((1, part_ff)),
                shaped((1, d)),
                shaped((3, samples, d)),
                shaped((T, d)),
                shaped((T, d)),
            ],
            steps=4,
            ins=slot_specs
            + token_specs
            + [rows_at(128), lanes_at(samples)]
            + [whole(array.shape) for array in mlp_rest],
            specs=[
                own_out,
                far_out,
                own_out,
                far_out,
                whole((16 * rows, wide(part_ff))),
                whole((1, part_ff)),
                whole((1, d)),
                whole((3, samples, d)),
                whole((T, d)),
                whole((T, d)),
            ],
            scratch=[
                pltpu.VMEM((d, part_ff), F32),
                pltpu.VMEM((part_ff, d), F32),
                pltpu.VMEM((d, part_ff), BF),
                pltpu.VMEM((part_ff, d), BF),
                pltpu.VMEM((1, d), F32),
                pltpu.VMEM((1, part_ff), F32),
                pltpu.VMEM((1, d), F32),
            ],
        )

        fc_z = lax.psum_scatter(fcg, "z", scatter_dimension=0, tiled=True)
        gm_terms = scatter_sum(gm_own, gm_far)

        *ex_slots, grad_one, modg_gate, proj_bias_g = call(
            "middle",
            6,
            functools.partial(middle_kernel, d, len(gm_terms)),
            [*gm_terms, after_own, branch_own, slab_rows, sel, selt, mod, proj_all],
            [shaped((2, width, T), BF)] * 8 + [shaped((T, d)), shaped((samples, d)), shaped((1, d))],
            ins=[whole((T, d))] * (len(gm_terms) + 3)
            + [whole((T, 128)), whole((samples, T)), whole(mod.shape), whole((d, d))],
            scratch=[pltpu.VMEM((d, T), F32)],
        )
        grad_attn = exchange(ex_slots)
        b2_sums = core_sum(b2_own, b2_far)
        grad_attn, b2_sums = lax.optimization_barrier((grad_attn, b2_sums))
        b2_terms = [over(total, slot // 2, slot % 2) for slot, total in enumerate(b2_sums)]

        back_rest = [w_qkv, modg_two, modg_gate, proj_bias_g, fc1_bias_g, fc2_bias_g]
        gin_own, gin_far, grad_qkv, attn_in, to_sum = call(
            "back",
            22,
            functools.partial(back_kernel, d, width, columns),
            [*grad_attn, tok_near, tok_far, sel, selt, mod, qkv, *back_rest],
            [half_shape, half_shape, shaped((S, wide(3 * width)), BF), shaped((S, d), BF), shaped((32, 8, d), BF)],
            steps=4,
            ins=[whole((2, width, T))] * 8
            + token_specs
            + [rows_at(128), lanes_at(samples), whole(mod.shape), rows_at(wide(3 * width))]
            + [whole(array.shape) for array in back_rest],
            specs=[own_out, far_out, rows_at(wide(3 * width)), rows_at(d), whole((32, 8, d))],
            scratch=[
                pltpu.VMEM((8, 2, width, T), BF),
                pltpu.VMEM((2, samples, d), F32),
                pltpu.VMEM((1, 3 * width), F32),
            ],
        )
        gin_own, gin_far, grad_qkv, attn_in, to_sum, b2_terms = lax.optimization_barrier(
            (gin_own, gin_far, grad_qkv, attn_in, to_sum, b2_terms)
        )
        gin_terms = scatter_sum(gin_own, gin_far)
        (attn_g,) = call(
            "weights",
            8,
            functools.partial(weights_kernel, d, width, order),
            [*attn_slots, *grad_attn, grad_qkv, attn_in],
            [shaped((4, 9 * width, 128), BF)],
            steps=4,
            ins=slot_specs + [whole((2, width, T))] * 8 + [rows_at(wide(3 * width)), rows_at(d)],
            specs=[whole((4, 9 * width, 128))],
            scratch=[
                pltpu.VMEM((d, 3 * width), F32),
                pltpu.VMEM((d, width), F32),
                pltpu.VMEM((8, width, T), BF),
                pltpu.VMEM((d, 4 * width), BF),
            ],
        )
        terms = lax.all_to_all(to_sum, names, 0, 0, tiled=True)
        (mlp_send,) = call(
            "mlp_split", 3, functools.partial(mlp_split_kernel, rows), [fc_z], [shaped((8, rows, wide(3 * rows)), BF)]
        )
        attn_g, terms, mlp_send, gin_terms = lax.optimization_barrier((attn_g, terms, mlp_send, gin_terms))
        mlp_got = lax.all_to_all(mlp_send, group, 0, 0, tiled=True)
        attn_z = lax.psum_scatter(attn_g.reshape(36 * width, 128), "z", scatter_dimension=0, tiled=True)

        (sums,) = call("grad_sum", 2, grad_sum_kernel, [terms], [shaped((8, d), BF)])
        own_specs = [whole((T, 1)), whole((T, 128)), whole(mod.shape)]
        (input_grad,) = call(
            "input_grad",
            3,
            input_grad_kernel,
            [*gin_terms, flat_tokens, grad_one, flat_cot, mask, sel, mod],
            [shaped((T, d))],
            ins=[whole((T, d))] * 7 + own_specs,
        )
        sums, mlp_got, input_grad = lax.optimization_barrier((over_z(sums), mlp_got, input_grad))
        total = to_slab(jnp.stack(sums))

        (ada_weight_grad, condition_grad, ada_bias_grad, qkv_bias_grad, proj_bias_grad, fc1_bias_grad, fc2_bias_grad) = call(
            "ada",
            5,
            functools.partial(ada_kernel, d),
            [total, act_rows, silu_slope, ada_weight],
            [shaped((rows, 6 * d)), shaped((samples, rows))]
            + [shaped((n // 128, 128)) for n in (6 * d, 2 * d, d, ff, d)],
        )

        (result,) = call(
            "output",
            3,
            output_kernel,
            [*b2_terms, flat_tokens, after_own, mask, sel, mod],
            [shaped((T, d), BF)],
            ins=[whole((T, d))] * 6 + own_specs,
        )
        fc1_weight_grad, fc2_weight_grad = call(
            "mlp_join",
            3,
            functools.partial(mlp_join_kernel, rows),
            [mlp_got],
            [shaped((rows, ff // 4)), shaped((d // 4, 4 * rows))],
        )
        attn_z, result, fc1_weight_grad = lax.optimization_barrier((attn_z, result, fc1_weight_grad))
        attn_send, proj_keep, proj_send = call(
            "attn_split",
            3,
            functools.partial(attn_split_kernel, rows),
            [attn_z],
            [shaped((8, rows, wide(rows)), BF), shaped((rows, wide(rows)), BF), shaped((rows, wide(rows)), BF)],
            scratch=[pltpu.VMEM((2 * rows, 4 * rows), BF)],
        )
        attn_got = lax.all_to_all(attn_send, group, 0, 0, tiled=True)
        qkv_weight_grad, proj_weight_grad = call(
            "attn_join",
            3,
            functools.partial(attn_join_kernel, rows),
            [attn_got, proj_keep, swap(proj_send, ("y",))],
            [shaped((rows, 3 * d // 4)), shaped((rows, d // 4))],
        )

        shape = (frames, columns, d)
        return (
            result.reshape(shape),
            input_grad.reshape(shape),
            condition_grad,
            ada_weight_grad,
            ada_bias_grad.reshape(-1),
            qkv_weight_grad,
            qkv_bias_grad.reshape(-1),
            proj_weight_grad,
            proj_bias_grad.reshape(-1),
            fc1_weight_grad,
            fc1_bias_grad.reshape(-1),
            fc2_weight_grad.T,
            fc2_bias_grad.reshape(-1),
        )

    frame, patch = ("x", "core"), ("z", "y")
    token_spec, number_spec = P(None, names, None), P(None, names)
    row_spec, both_spec = P(patch, None), P(patch, frame)
    return jax.shard_map(
        local,
        mesh=grid,
        in_specs=(
            token_spec, number_spec, number_spec, P(), row_spec, P(), row_spec, P(), row_spec, P(), row_spec, P(),
            row_spec, P(), token_spec,
        ),
        out_specs=(
            token_spec, token_spec, P(None, patch), row_spec, P(), both_spec, P(), both_spec, P(), both_spec, P(),
            both_spec, P(),
        ),
        check_vma=False,
    )


def solution(mesh):
    if (mesh.shape["frame"], mesh.shape["patch"]) == (4, 8):
        return slab_solution(mesh)
    return general_solution(mesh)
```
